512 devices in a mesh: ctx: 256 (over z, x, y), mp: 2 (over core).
Axes of the slice: x: 4, y: 8, z: 8, core: 2. Of those that a mesh axis runs over, the one named last changes fastest.
Arguments:
- queries: bfloat16 [32768, 2048], P('ctx', 'mp'), may hold values from -4.5 to 4.5
- keys: bfloat16 [32768, 512], P('ctx', 'mp'), may hold values from -6 to 6
- values: bfloat16 [32768, 512], P('ctx', 'mp'), may hold values from -6 to 6
- lengths: int32 [256], P('ctx'), may hold values from 16 to 128, as said below
- fire_w1: float32 [32], replicated, may hold values from -8 to 8
- fire_b1: float32 [32], replicated, may hold values from -1 to 1
- fire_w2: float32 [32, 16], replicated, may hold values from -1 to 1
- grad_out: bfloat16 [32768, 2048], P('ctx', 'mp'), may hold values from -6 to 6
Outputs:
- attended: bfloat16 [32768, 2048], P('ctx', 'mp')
- grad_q: bfloat16 [32768, 2048], P('ctx', 'mp')
- grad_k: bfloat16 [32768, 512], P('ctx', 'mp')
- grad_v: bfloat16 [32768, 512], P('ctx', 'mp')
- grad_w1: float32 [32], replicated
- grad_b1: float32 [32], replicated
- grad_w2: float32 [32, 16], replicated
The draws below stay inside these ranges and needn't reach their ends.
Inputs may be any that keep to these rules, and one draw needn't show every extreme that they name: Tokens at offsets lengths[b] and beyond in block b are padding; some block is full.
All inputs are finite; a program needn't handle non-finite values.
Results may differ from the reference program's by a relative error of at most 0.014.
Values sent between devices are 32-bit elements; how exact they have to be, the bound alone decides.
No kernel may reach another device: no remote copies, remote signals or barrier semaphores. Data moves between devices by JAX's collectives and lax.ppermute only.
A program may use at most 64 MiB of HBM per device.

```python
import jax
import jax.numpy as jnp
from jax import lax

HQ = 16
KEY_VALUE_HEADS = 4
HEAD_SIZE = 128
FH = 32
COARSE = 32
BLOCK_TOKENS = 128
BLOCKS = 256
SEQUENCE_TOKENS = 32768
LEVELS = 8


def draw_queries(key, part):
    key = jax.random.fold_in(key, 3)
    return jnp.clip(jax.random.normal(key, (SEQUENCE_TOKENS, HQ * HEAD_SIZE)), -4.5, 4.5).astype(jnp.bfloat16)


def draw_keys(key, part):
    key = jax.random.fold_in(key, 4)
    random_noise_key, offset_random_key = jax.random.split(key)
    block_offset = jnp.clip(jax.random.normal(offset_random_key, (SEQUENCE_TOKENS // BLOCK_TOKENS, 1, KEY_VALUE_HEADS * HEAD_SIZE)), -2.0, 2.0)
    block_offset = jnp.broadcast_to(block_offset, (SEQUENCE_TOKENS // BLOCK_TOKENS, BLOCK_TOKENS, KEY_VALUE_HEADS * HEAD_SIZE)).reshape(SEQUENCE_TOKENS, KEY_VALUE_HEADS * HEAD_SIZE)
    return jnp.clip(jnp.clip(jax.random.normal(random_noise_key, (SEQUENCE_TOKENS, KEY_VALUE_HEADS * HEAD_SIZE)), -4.5, 4.5) + 1.5 * block_offset, -6.0, 6.0).astype(jnp.bfloat16)


def draw_values(key, part):
    key = jax.random.fold_in(key, 6)
    random_noise_key, offset_random_key = jax.random.split(key)
    block_offset = jnp.clip(jax.random.normal(offset_random_key, (SEQUENCE_TOKENS // BLOCK_TOKENS, 1, KEY_VALUE_HEADS * HEAD_SIZE)), -2.0, 2.0)
    block_offset = jnp.broadcast_to(block_offset, (SEQUENCE_TOKENS // BLOCK_TOKENS, BLOCK_TOKENS, KEY_VALUE_HEADS * HEAD_SIZE)).reshape(SEQUENCE_TOKENS, KEY_VALUE_HEADS * HEAD_SIZE)
    return jnp.clip(jnp.clip(jax.random.normal(random_noise_key, (SEQUENCE_TOKENS, KEY_VALUE_HEADS * HEAD_SIZE)), -4.5, 4.5) + 1.5 * block_offset, -6.0, 6.0).astype(jnp.bfloat16)


def draw_lengths(key, part):
    key = jax.random.fold_in(key, 5)
    pick_key, spot_key = jax.random.split(key)
    drawn = jax.random.randint(pick_key, (BLOCKS,), BLOCK_TOKENS // 8, BLOCK_TOKENS + 1)
    spot = jax.random.randint(spot_key, (), 0, BLOCKS)
    places = jnp.arange(BLOCKS)
    drawn = jnp.where(places == spot, BLOCK_TOKENS, drawn)
    drawn = jnp.where(places == (spot + 1) % BLOCKS, BLOCK_TOKENS // 8, drawn)
    return drawn.astype(jnp.int32)


def steps_of(own_key, dims, pieces, smallest, high):
    loudness, own = 1.0, jax.random.fold_in(own_key, 6)
    for position, parts in pieces:
        draws = jnp.exp(jax.random.uniform(jax.random.fold_in(own, position), (parts,), jnp.float32, smallest / len(pieces), high / len(pieces)))
        loudness = loudness * jnp.repeat(draws, dims[position] // parts).reshape([-1 if axis == position else 1 for axis in range(len(dims))])
    return loudness


def scatter_about(rng, dims, scale, limit, cuts=(), held_as=jnp.bfloat16):
    level = steps_of(rng, dims, cuts, -0.22, 0.18) if cuts else 1.0
    result = jax.random.normal(rng, dims, jnp.float32) * scale * level
    return jnp.minimum(jnp.maximum(result, -limit), limit).astype(held_as)


def setup_inputs(seed: int = 0) -> dict:
    streams_of = jax.random.split(jax.random.key(seed), 9)
    return {
        "queries": draw_queries(jax.random.fold_in(streams_of[8], 71), 0),
        "keys": draw_keys(jax.random.fold_in(streams_of[8], 71), 0),
        "values": draw_values(jax.random.fold_in(streams_of[8], 71), 0),
        "lengths": draw_lengths(jax.random.fold_in(streams_of[8], 71), 0),
        "fire_w1": scatter_about(streams_of[4], (FH,), 2.0, 8.0, (), jnp.float32),
        "fire_b1": jnp.clip(jax.random.uniform(streams_of[5], (FH,), jnp.float32, -1.0, 1.0), -1.0, 1.0),
        "fire_w2": scatter_about(streams_of[6], (FH, HQ), FH ** -0.5, 1.0, (), jnp.float32),
        "grad_out": scatter_about(streams_of[7], (SEQUENCE_TOKENS, HQ * HEAD_SIZE), 1.0, 6.0, ((0, 256), (1, 2))),
    }


def block_pass(inputs):
    (query_blk, key_blk, value_blk, grad_blk, live_blk, coarse_k, coarse_v, coarse_c, coarse_pos, block_no, fire_w1, fire_b1, fire_w2, seq_total) = inputs
    tok_rows = query_blk.shape[0]
    kv_heads = key_blk.shape[1] // HEAD_SIZE
    q_heads = query_blk.shape[1] // HEAD_SIZE
    group_size = q_heads // kv_heads
    score_scale = HEAD_SIZE ** -0.5
    safe_count = jnp.maximum(coarse_c, 1.0)
    mean_k = (coarse_k / safe_count[:, None]).astype(jnp.bfloat16)
    mean_v = (coarse_v / safe_count[:, None]).astype(jnp.bfloat16)
    keys_all = jnp.concatenate([key_blk, mean_k], 0).astype(jnp.float32)
    values_all = jnp.concatenate([value_blk, mean_v], 0).astype(jnp.float32)
    key_live = jnp.concatenate([live_blk > 0, coarse_c > 0])
    query_pos = (block_no * tok_rows + jnp.arange(tok_rows)).astype(jnp.float32)
    key_pos = jnp.concatenate([query_pos, coarse_pos])
    phase = jnp.log1p(jnp.abs(query_pos[:, None] - key_pos[None, :])) / jnp.log1p(seq_total)
    hidden = jax.nn.relu(phase[:, :, None] * fire_w1 + fire_b1)
    fire_bias = jnp.einsum('tkm,mh->htk', hidden, fire_w2, precision=lax.Precision.HIGHEST)
    query_f = query_blk.astype(jnp.float32).reshape(tok_rows, kv_heads, group_size, HEAD_SIZE)
    key_f = keys_all.reshape(-1, kv_heads, HEAD_SIZE)
    value_f = values_all.reshape(-1, kv_heads, HEAD_SIZE)
    raw_scores = jnp.einsum('tjgd,kjd->jgtk', query_f, key_f, precision=lax.Precision.HIGHEST).reshape(q_heads, tok_rows, -1)
    scores = raw_scores * score_scale + fire_bias
    scores = jnp.where(key_live[None, None, :], scores, -jnp.inf)
    top_score = jnp.max(scores, axis=-1, keepdims=True)
    weights = jnp.exp(scores - top_score)
    probs = weights / jnp.sum(weights, axis=-1, keepdims=True)
    probs_b = probs.astype(jnp.bfloat16).astype(jnp.float32).reshape(kv_heads, group_size, tok_rows, -1)
    output = jnp.einsum('jgtk,kjd->tjgd', probs_b, value_f, precision=lax.Precision.HIGHEST).reshape(tok_rows, -1)
    attended = (output * live_blk[:, None]).astype(jnp.bfloat16)
    masked_grad = jnp.where(live_blk[:, None] > 0, grad_blk, jnp.zeros_like(grad_blk))
    grad_f = masked_grad.astype(jnp.float32).reshape(tok_rows, kv_heads, group_size, HEAD_SIZE)
    dprobs = jnp.einsum('tjgd,kjd->jgtk', grad_f, value_f, precision=lax.Precision.HIGHEST).reshape(q_heads, tok_rows, -1)
    dscores = probs * (dprobs - jnp.sum(probs * dprobs, axis=-1, keepdims=True))
    dscores_b = dscores.astype(jnp.bfloat16).astype(jnp.float32).reshape(kv_heads, group_size, tok_rows, -1)
    grad_query = score_scale * jnp.einsum('jgtk,kjd->tjgd', dscores_b, key_f, precision=lax.Precision.HIGHEST)
    grad_query = grad_query.reshape(tok_rows, -1).astype(jnp.bfloat16)
    key_grads = score_scale * jnp.einsum('jgtk,tjgd->kjd', dscores_b, query_f, precision=lax.Precision.HIGHEST)
    key_grads = key_grads.reshape(-1, kv_heads * HEAD_SIZE)
    value_grads = jnp.einsum('jgtk,tjgd->kjd', probs_b, grad_f, precision=lax.Precision.HIGHEST).reshape(-1, kv_heads * HEAD_SIZE)
    coarse_gk = key_grads[tok_rows:] / safe_count[:, None]
    coarse_gv = value_grads[tok_rows:] / safe_count[:, None]
    grad_w2 = jnp.einsum('htk,tkm->mh', dscores, hidden, precision=lax.Precision.HIGHEST)
    active = (hidden > 0).astype(jnp.float32)
    plain_sum = jnp.einsum('htk,tkm->hm', dscores, active, precision=lax.Precision.HIGHEST)
    phase_sum = jnp.einsum('htk,tkm->hm', dscores * phase[None], active, precision=lax.Precision.HIGHEST)
    grad_b1 = jnp.sum(fire_w2 * plain_sum.T, axis=1)
    grad_w1 = jnp.sum(fire_w2 * phase_sum.T, axis=1)
    return (attended, grad_query, key_grads[:tok_rows], value_grads[:tok_rows], coarse_gk, coarse_gv, grad_w1, grad_b1, grad_w2)


def reference(queries, keys, values, lengths, fire_w1, fire_b1, fire_w2, grad_out):
    tok_rows = BLOCK_TOKENS
    block_count = BLOCKS
    kv_width = keys.shape[1]
    offsets = jnp.arange(SEQUENCE_TOKENS) % tok_rows
    token_live = (offsets < jnp.repeat(lengths, tok_rows)).astype(jnp.float32)
    key_f = keys.astype(jnp.float32) * token_live[:, None]
    value_f = values.astype(jnp.float32) * token_live[:, None]
    block_ids = jnp.arange(block_count).astype(jnp.int32)
    sib_keys, sib_values, sib_counts, sib_pos = [], [], [], []
    for height in range(LEVELS):
        run_length = (2 ** height) * tok_rows // COARSE
        groups = block_count >> height
        sums_k = key_f.reshape(SEQUENCE_TOKENS // run_length, run_length, kv_width).sum(1).reshape(groups, COARSE, kv_width)
        sums_v = value_f.reshape(SEQUENCE_TOKENS // run_length, run_length, kv_width).sum(1).reshape(groups, COARSE, kv_width)
        counts = token_live.reshape(SEQUENCE_TOKENS // run_length, run_length).sum(1).reshape(groups, COARSE)
        sibling = (block_ids >> height) ^ 1
        sib_keys.append(sums_k[sibling])
        sib_values.append(sums_v[sibling])
        sib_counts.append(counts[sibling])
        start = (sibling * (2 ** height) * tok_rows).astype(jnp.float32)
        inside = (jnp.arange(COARSE) * run_length).astype(jnp.float32) + (run_length - 1) / 2.0
        sib_pos.append(start[:, None] + inside[None, :])
    coarse_k = jnp.concatenate(sib_keys, 1)
    coarse_v = jnp.concatenate(sib_values, 1)
    coarse_c = jnp.concatenate(sib_counts, 1)
    coarse_pos = jnp.concatenate(sib_pos, 1)
    seq_total = jnp.asarray(SEQUENCE_TOKENS, dtype=jnp.float32)

    def one_block(packed):
        return block_pass(packed + (fire_w1, fire_b1, fire_w2, seq_total))

    results = lax.map(one_block, (queries.reshape(block_count, tok_rows, -1), keys.reshape(block_count, tok_rows, -1), values.reshape(block_count, tok_rows, -1), grad_out.reshape(block_count, tok_rows, -1), token_live.reshape(block_count, tok_rows), coarse_k, coarse_v, coarse_c, coarse_pos, block_ids))
    attended, grad_query, local_gk, local_gv, coarse_gk, coarse_gv, part_w1, part_b1, part_w2 = results
    total_gk = local_gk.reshape(SEQUENCE_TOKENS, kv_width)
    total_gv = local_gv.reshape(SEQUENCE_TOKENS, kv_width)
    for height in range(LEVELS):
        run_length = (2 ** height) * tok_rows // COARSE
        groups = block_count >> height
        slab_k = coarse_gk[:, height * COARSE:(height + 1) * COARSE]
        slab_v = coarse_gv[:, height * COARSE:(height + 1) * COARSE]
        slab_k = slab_k.reshape(groups, 2 ** height, COARSE, kv_width).sum(1)
        slab_v = slab_v.reshape(groups, 2 ** height, COARSE, kv_width).sum(1)
        slab_k = slab_k.reshape(groups // 2, 2, COARSE, kv_width)[:, ::-1].reshape(groups * COARSE, kv_width)
        slab_v = slab_v.reshape(groups // 2, 2, COARSE, kv_width)[:, ::-1].reshape(groups * COARSE, kv_width)
        total_gk = total_gk + jnp.repeat(slab_k, run_length, axis=0)
        total_gv = total_gv + jnp.repeat(slab_v, run_length, axis=0)
    grad_k = (total_gk * token_live[:, None]).astype(jnp.bfloat16)
    grad_v = (total_gv * token_live[:, None]).astype(jnp.bfloat16)
    return (attended.reshape(SEQUENCE_TOKENS, -1), grad_query.reshape(SEQUENCE_TOKENS, -1), grad_k, grad_v, jnp.sum(part_w1, 0), jnp.sum(part_b1, 0), jnp.sum(part_w2, 0))
```

```python
import functools

import jax
import jax.numpy as jnp
from jax import lax
from jax.experimental import pallas as pl
from jax.experimental.pallas import tpu as pltpu
from jax.sharding import PartitionSpec as P

D = 128
COARSE = 32
T = 128
LEVELS = 8
KEYS = T + LEVELS * COARSE
HIDDEN = 32
HEADS = 8
KV = 2
GROUP = HEADS // KV
SUB = 8
SCALE = D ** (-0.5)
MASKS = (1, 2, 6, 8, 24, 32, 64, 192)
NT = (((1,), (1,)), ((), ()))
TN = (((0,), (0,)), ((), ()))
VMEM = pl.BlockSpec(memory_space=pltpu.VMEM)
SMEM = pl.BlockSpec(memory_space=pltpu.SMEM)


def dot(a, b, dims=(((1,), (0,)), ((), ()))):
    return lax.dot_general(a, b, dims, preferred_element_type=jnp.float32)


def exchange(value, level):
    pairs = [(i, i ^ MASKS[level]) for i in range(lax.axis_size("ctx"))]
    return lax.ppermute(value, "ctx", pairs)


def leaf_kernel(len_ref, k_ref, v_ref, out_ref):
    run = T // COARSE
    row = lax.broadcasted_iota(jnp.int32, (COARSE, T), 0)
    tok = lax.broadcasted_iota(jnp.int32, (COARSE, T), 1)
    member = jnp.where((tok // run == row) & (tok < len_ref[0]), 1.0, 0.0)
    member_b = member.astype(jnp.bfloat16)
    out_ref[:, : KV * D] = dot(member_b, k_ref[...])
    out_ref[:, KV * D : 2 * KV * D] = dot(member_b, v_ref[...])
    count = jnp.sum(member, axis=1, keepdims=True)
    out_ref[:, 2 * KV * D :] = jnp.broadcast_to(count, (COARSE, D))


def bias_kernel(ctx_ref, w1_ref, b1_ref, w2_ref, bias_ref, phase_ref):
    ctx = ctx_ref[0]
    col = lax.broadcasted_iota(jnp.int32, (1, KEYS), 1)
    level = (col - T) // COARSE
    pos = col.astype(jnp.float32)
    for k in range(LEVELS):
        run = 2**k * T // COARSE
        start = ((ctx >> k) ^ 1) * 2**k * T - ctx * T
        inside = (col - T - k * COARSE) * run
        here = (start + inside).astype(jnp.float32) + (run - 1) / 2.0
        pos = jnp.where((col >= T) & (level == k), here, pos)
    top = jnp.log1p(jnp.full((1, KEYS), 1.0, jnp.float32) * (LEVEL_TOKENS))

    def body(i, carry):
        row = i * SUB + lax.broadcasted_iota(jnp.int32, (SUB, KEYS), 0)
        phase = jnp.log1p(jnp.abs(row.astype(jnp.float32) - pos)) / top
        phase_ref[pl.ds(i * SUB, SUB), :] = phase
        sums = [jnp.zeros((SUB, KEYS), jnp.float32) for _ in range(HEADS)]
        for m in range(HIDDEN):
            hidden = jnp.maximum(phase * w1_ref[m] + b1_ref[m], 0.0)
            for h in range(HEADS):
                sums[h] = sums[h] + hidden * w2_ref[m, h]
        for h in range(HEADS):
            bias_ref[h, pl.ds(i * SUB, SUB), :] = sums[h]
        return carry

    lax.fori_loop(0, T // SUB, body, 0)


LEVEL_TOKENS = float(T * 2**LEVELS)


def main_kernel(
    len_ref, w1_ref, b1_ref, coef_ref, q_ref, k_ref, v_ref, g_ref, sib_ref, bias_ref, phase_ref,
    out_ref, gq_ref, gk_ref, gv_ref, ck_ref, cv_ref, w_ref, ds_ref, acc_ref,
):
    length = len_ref[0]
    count = sib_ref[:, 2 * KV * D :]
    safe = jnp.maximum(count, 1.0)
    count_t = jnp.concatenate([count[:T].T[:1], count[T:].T[:1]], axis=1)
    token_live = lax.broadcasted_iota(jnp.int32, (1, T), 1) < length
    live = jnp.concatenate([token_live.astype(jnp.float32), count_t], axis=1) > 0.0
    row_live = lax.broadcasted_iota(jnp.int32, (T, 1), 0) < length
    row_live_f = row_live.astype(jnp.float32)
    for j in range(KV):
        cols = slice(j * D, (j + 1) * D)
        vcols = slice((KV + j) * D, (KV + j + 1) * D)
        keys = jnp.concatenate([k_ref[:, cols], (sib_ref[:, cols] / safe).astype(jnp.bfloat16)], axis=0)
        values = jnp.concatenate([v_ref[:, cols], (sib_ref[:, vcols] / safe).astype(jnp.bfloat16)], axis=0)
        key_grads = jnp.zeros((KEYS, D), jnp.float32)
        value_grads = jnp.zeros((KEYS, D), jnp.float32)
        for g in range(GROUP):
            h = j * GROUP + g
            hcols = slice(h * D, (h + 1) * D)
            query = q_ref[:, hcols]
            scores = dot(query, keys, NT) * SCALE + bias_ref[h]
            scores = jnp.where(live, scores, -jnp.inf)
            top = jnp.max(scores, axis=1, keepdims=True)
            weights = jnp.exp(scores - top)
            probs = weights / jnp.sum(weights, axis=1, keepdims=True)
            probs_b = probs.astype(jnp.bfloat16)
            out_ref[:, hcols] = (dot(probs_b, values) * row_live_f).astype(jnp.bfloat16)
            grad = g_ref[:, hcols]
            grad = jnp.where(row_live, grad, jnp.zeros_like(grad))
            dprobs = dot(grad, values, NT)
            dscores = probs * (dprobs - jnp.sum(probs * dprobs, axis=1, keepdims=True))
            ds_ref[h] = dscores
            dscores_b = dscores.astype(jnp.bfloat16)
            gq_ref[:, hcols] = (SCALE * dot(dscores_b, keys)).astype(jnp.bfloat16)
            key_grads = key_grads + dot(dscores_b, query, TN)
            value_grads = value_grads + dot(probs_b, grad, TN)
        key_grads = key_grads * SCALE
        gk_ref[:, cols] = key_grads[:T]
        gv_ref[:, cols] = value_grads[:T]
        ck_ref[:, cols] = key_grads[T:] / safe
        cv_ref[:, cols] = value_grads[T:] / safe
    acc_ref[...] = jnp.zeros_like(acc_ref)

    def body(i, carry):
        rows = pl.ds(i * SUB, SUB)
        phase = phase_ref[rows, :]
        parts = [ds_ref[h, rows, :] for h in range(HEADS)]
        parts = jnp.concatenate(parts + [p * phase for p in parts], axis=0)
        high = parts.astype(jnp.bfloat16)
        low = (parts - high.astype(jnp.float32)).astype(jnp.bfloat16)
        both = jnp.concatenate([high, low], axis=0)
        active = [
            jnp.where(phase * w1_ref[m] + b1_ref[m] > 0.0, 1.0, 0.0) for m in range(HIDDEN)
        ]
        active = jnp.concatenate(active, axis=0).astype(jnp.bfloat16)
        acc_ref[...] += dot(both, active, NT)
        return carry

    lax.fori_loop(0, T // SUB, body, 0)
    acc = acc_ref[...]
    rows = 2 * HEADS * SUB
    acc = acc[:rows] + acc[rows:]
    sub_row = lax.broadcasted_iota(jnp.int32, acc.shape, 0) % SUB
    sub_col = lax.broadcasted_iota(jnp.int32, acc.shape, 1) % SUB
    acc = jnp.where(sub_row == sub_col, acc, 0.0)
    acc = acc.reshape(2 * HEADS, SUB, HIDDEN * SUB).sum(axis=1)
    unit = lax.broadcasted_iota(jnp.int32, (HIDDEN * SUB, D), 0) // SUB
    lane = lax.broadcasted_iota(jnp.int32, (HIDDEN * SUB, D), 1) % HIDDEN
    gather = jnp.where(unit == lane, 1.0, 0.0)
    sums = lax.dot_general(
        acc, gather, (((1,), (0,)), ((), ())),
        precision=lax.Precision.HIGHEST, preferred_element_type=jnp.float32,
    )
    w_ref[...] = coef_ref[0] * sums[:HEADS] + coef_ref[1] * sums[HEADS:]


def shards(queries, keys, values, lengths, fire_w1, fire_b1, fire_w2, grad_out):
    f32, bf16 = jnp.float32, jnp.bfloat16
    shape = jax.ShapeDtypeStruct
    ctx = lax.axis_index("ctx")
    mp = lax.axis_index("mp")
    w2 = lax.dynamic_slice_in_dim(fire_w2, mp * HEADS, HEADS, 1)
    w2_t = w2.T
    spread = lambda row: jnp.broadcast_to(row[None], (HEADS, HIDDEN))
    zero = jnp.zeros((HEADS, HIDDEN), f32)
    coef = jnp.stack([
        jnp.concatenate([spread(fire_b1), zero, w2_t, zero], axis=1),
        jnp.concatenate([spread(fire_w1), w2_t, zero, zero], axis=1),
    ])
    own = pl.pallas_call(
        leaf_kernel,
        out_shape=shape((COARSE, (2 * KV + 1) * D), f32),
        in_specs=[SMEM, VMEM, VMEM],
        out_specs=VMEM,
        name="leaf",
    )(lengths, keys, values)
    bias, phase = pl.pallas_call(
        bias_kernel,
        out_shape=(shape((HEADS, T, KEYS), f32), shape((T, KEYS), f32)),
        in_specs=[SMEM] * 4,
        out_specs=(VMEM, VMEM),
        cost_estimate=pl.CostEstimate(flops=60_000_000, bytes_accessed=2_000_000, transcendentals=50_000),
        name="bias",
    )(ctx.reshape(1), fire_w1, fire_b1, w2)
    siblings = []
    for level in range(LEVELS):
        got = exchange(own, level)
        siblings.append(got)
        if level + 1 < LEVELS:
            upper = (ctx >> level) & 1 == 1
            first = jnp.where(upper, got, own)
            second = jnp.where(upper, own, got)
            own = jnp.concatenate([first, second], 0).reshape(COARSE, 2, -1).sum(1)
    siblings = jnp.concatenate(siblings, 0)
    width = KV * D
    attended, grad_q, own_gk, own_gv, coarse_gk, coarse_gv, w_part = pl.pallas_call(
        main_kernel,
        out_shape=(
            shape((T, HEADS * D), bf16),
            shape((T, HEADS * D), bf16),
            shape((T, width), f32),
            shape((T, width), f32),
            shape((LEVELS * COARSE, width), f32),
            shape((LEVELS * COARSE, width), f32),
            shape((HEADS, D), f32),
        ),
        in_specs=[SMEM, SMEM, SMEM] + [VMEM] * 8,
        out_specs=(VMEM,) * 7,
        scratch_shapes=[
            pltpu.VMEM((HEADS, T, KEYS), f32),
            pltpu.VMEM((4 * HEADS * SUB, HIDDEN * SUB), f32),
        ],
        compiler_params=pltpu.CompilerParams(vmem_limit_bytes=32 * 2**20),
        name="attention",
    )(lengths, fire_w1, fire_b1, coef, queries, keys, values, grad_out, siblings, bias, phase)
    coarse = jnp.concatenate([coarse_gk, coarse_gv], 1)
    w_sum = w_part.reshape(2, -1)
    back = jnp.zeros((COARSE, 2 * width), f32)
    half = COARSE // 2
    for level in reversed(range(LEVELS)):
        send = coarse[level * COARSE : (level + 1) * COARSE]
        keep = 0.0
        if level + 1 < LEVELS:
            upper = (ctx >> level) & 1 == 1
            lower_part = jnp.repeat(back[:half], 2, axis=0)
            upper_part = jnp.repeat(back[half:], 2, axis=0)
            keep = jnp.where(upper, upper_part, lower_part)
            send = send + jnp.where(upper, lower_part, upper_part)
        came = exchange(jnp.concatenate([send, w_sum], 0), level)
        back = keep + came[:COARSE]
        w_sum = w_sum + came[COARSE:]
    token_live = (jnp.arange(T) < lengths[0]).astype(f32)[:, None]
    back = jnp.repeat(back, T // COARSE, axis=0)
    grad_k = ((own_gk + back[:, :width]) * token_live).astype(bf16)
    grad_v = ((own_gv + back[:, width:]) * token_live).astype(bf16)
    w_mine = w_sum.reshape(HEADS, D)
    placed = lax.dynamic_update_slice_in_dim(jnp.zeros((2 * HEADS, D), f32), w_mine, mp * HEADS, 0)
    w_all = lax.psum(placed, "mp")
    grad_w2 = w_all[:, :HIDDEN].T
    grad_w1 = w_all[:, HIDDEN : 2 * HIDDEN].sum(0)
    grad_b1 = w_all[:, 2 * HIDDEN : 3 * HIDDEN].sum(0)
    return (attended, grad_q, grad_k, grad_v, grad_w1, grad_b1, grad_w2)


def solution(mesh):
    split = P("ctx", "mp")
    return jax.shard_map(
        shards,
        mesh=mesh,
        in_specs=(split, split, split, P("ctx"), P(), P(), P(), split),
        out_specs=(split, split, split, split, P(), P(), P()),
        check_vma=False,
    )
```

```python
import jax
import jax.numpy as jnp
from jax import lax
from jax.experimental import pallas as pl
from jax.experimental.pallas import tpu as pltpu
from jax.sharding import PartitionSpec as P

D = 128
COARSE = 32
T = 128
LEVELS = 8
KEYS = T + LEVELS * COARSE
HIDDEN = 32
HEADS = 8
KV = 2
GROUP = HEADS // KV
SUB = 8
CHUNK = 8
SIDE = 16
WIDTH = KV * D
LEVEL_TOKENS = float(T * 2**LEVELS)
SCALE = D ** (-0.5)
MASKS = (1, 2, 6, 8, 24, 32, 64, 192)
NT = (((1,), (1,)), ((), ()))
TN = (((0,), (0,)), ((), ()))
VMEM = pl.BlockSpec(memory_space=pltpu.VMEM)
SMEM = pl.BlockSpec(memory_space=pltpu.SMEM)


def dot(a, b, dims=(((1,), (0,)), ((), ()))):
    return lax.dot_general(a, b, dims, preferred_element_type=jnp.float32)


def exchange(value, level):
    pairs = [(i, i ^ MASKS[level]) for i in range(lax.axis_size("ctx"))]
    return lax.ppermute(value, "ctx", pairs)


def leaf_kernel(len_ref, k_ref, v_ref, fine_ref, wide_ref):
    for ref, run in ((fine_ref, T // COARSE), (wide_ref, T // CHUNK)):
        row = lax.broadcasted_iota(jnp.int32, (T // run, T), 0)
        tok = lax.broadcasted_iota(jnp.int32, (T // run, T), 1)
        member = jnp.where((tok // run == row) & (tok < len_ref[0]), 1.0, 0.0)
        member_b = member.astype(jnp.bfloat16)
        ref[:, :WIDTH] = dot(member_b, k_ref[...])
        ref[:, WIDTH : 2 * WIDTH] = dot(member_b, v_ref[...])
        count = jnp.sum(member, axis=1, keepdims=True)
        ref[:, 2 * WIDTH :] = jnp.broadcast_to(count, (T // run, D))


def bias_kernel(ctx_ref, w1_ref, b1_ref, w2_ref, bias_ref, phase_ref):
    ctx = ctx_ref[0]
    col = lax.broadcasted_iota(jnp.int32, (1, KEYS), 1)
    level = (col - T) // COARSE
    pos = col.astype(jnp.float32)
    for k in range(LEVELS):
        run = 2**k * T // COARSE
        start = ((ctx >> k) ^ 1) * 2**k * T - ctx * T
        inside = (col - T - k * COARSE) * run
        here = (start + inside).astype(jnp.float32) + (run - 1) / 2.0
        pos = jnp.where((col >= T) & (level == k), here, pos)
    top = jnp.log1p(jnp.full((1, KEYS), LEVEL_TOKENS, jnp.float32))
    weight = w2_ref[...]
    weight_high = weight.astype(jnp.bfloat16)
    weight_low = (weight - weight_high.astype(jnp.float32)).astype(jnp.bfloat16)
    weight_both = jnp.concatenate([weight_high, weight_low], axis=0)

    def body(i, carry):
        rows = pl.ds(pl.multiple_of(i * SUB, SUB), SUB)
        row = i * SUB + lax.broadcasted_iota(jnp.int32, (SUB, KEYS), 0)
        phase = jnp.log1p(jnp.abs(row.astype(jnp.float32) - pos)) / top
        phase_ref[rows, :] = phase
        hidden = [jnp.maximum(phase * w1_ref[m] + b1_ref[m], 0.0) for m in range(HIDDEN)]
        hidden = jnp.concatenate(hidden, axis=0)
        high = hidden.astype(jnp.bfloat16)
        low = (hidden - high.astype(jnp.float32)).astype(jnp.bfloat16)
        with_high = dot(weight_both, high)
        bias = with_high[: HEADS * SUB] + with_high[HEADS * SUB :] + dot(weight_high, low)
        for h in range(HEADS):
            bias_ref[h, rows, :] = bias[h * SUB : (h + 1) * SUB]
        return carry

    lax.fori_loop(0, T // SUB, body, 0)


def main_kernel(
    len_ref, q_ref, k_ref, v_ref, g_ref, sib_ref, bias_ref,
    out_ref, gq_ref, own_ref, coarse_ref, ds_ref,
):
    length = len_ref[0]
    count = sib_ref[:, 2 * KV * D :]
    safe = jnp.maximum(count, 1.0)
    count_t = jnp.concatenate([count[:T].T[:1], count[T:].T[:1]], axis=1)
    token_live = lax.broadcasted_iota(jnp.int32, (1, T), 1) < length
    live = jnp.concatenate([token_live.astype(jnp.float32), count_t], axis=1) > 0.0
    row_live = lax.broadcasted_iota(jnp.int32, (T, 1), 0) < length
    row_live_f = row_live.astype(jnp.float32)
    for j in range(KV):
        cols = slice(j * D, (j + 1) * D)
        vcols = slice((KV + j) * D, (KV + j + 1) * D)
        keys = jnp.concatenate([k_ref[:, cols], (sib_ref[:, cols] / safe).astype(jnp.bfloat16)], axis=0)
        values = jnp.concatenate([v_ref[:, cols], (sib_ref[:, vcols] / safe).astype(jnp.bfloat16)], axis=0)
        key_grads = jnp.zeros((KEYS, D), jnp.float32)
        value_grads = jnp.zeros((KEYS, D), jnp.float32)
        for g in range(GROUP):
            h = j * GROUP + g
            hcols = slice(h * D, (h + 1) * D)
            query = q_ref[:, hcols]
            scores = dot(query, keys, NT) * SCALE + bias_ref[h]
            scores = jnp.where(live, scores, -jnp.inf)
            top = jnp.max(scores, axis=1, keepdims=True)
            weights = jnp.exp(scores - top)
            probs = weights / jnp.sum(weights, axis=1, keepdims=True)
            probs_b = probs.astype(jnp.bfloat16)
            out_ref[:, hcols] = (dot(probs_b, values) * row_live_f).astype(jnp.bfloat16)
            grad = g_ref[:, hcols]
            grad = jnp.where(row_live, grad, jnp.zeros_like(grad))
            dprobs = dot(grad, values, NT)
            dscores = probs * (dprobs - jnp.sum(probs * dprobs, axis=1, keepdims=True))
            ds_ref[h] = dscores
            dscores_b = dscores.astype(jnp.bfloat16)
            gq_ref[:, hcols] = (SCALE * dot(dscores_b, keys)).astype(jnp.bfloat16)
            key_grads = key_grads + dot(dscores_b, query, TN)
            value_grads = value_grads + dot(probs_b, grad, TN)
        key_grads = key_grads * SCALE
        own_ref[:, cols] = key_grads[:T]
        own_ref[:, vcols] = value_grads[:T]
        coarse_ref[:, cols] = key_grads[T:] / safe
        coarse_ref[:, vcols] = value_grads[T:] / safe


def weight_kernel(w1_ref, b1_ref, coef_ref, ds_ref, phase_ref, w_ref, acc_ref):
    acc_ref[...] = jnp.zeros_like(acc_ref)

    def body(i, carry):
        rows = pl.ds(i * SUB, SUB)
        phase = phase_ref[rows, :]
        parts = [ds_ref[h, rows, :] for h in range(HEADS)]
        parts = jnp.concatenate(parts + [p * phase for p in parts], axis=0)
        high = parts.astype(jnp.bfloat16)
        low = (parts - high.astype(jnp.float32)).astype(jnp.bfloat16)
        both = jnp.concatenate([high, low], axis=0)
        active = [
            jnp.where(phase * w1_ref[m] + b1_ref[m] > 0.0, 1.0, 0.0) for m in range(HIDDEN)
        ]
        active = jnp.concatenate(active, axis=0).astype(jnp.bfloat16)
        acc_ref[...] += dot(both, active, NT)
        return carry

    lax.fori_loop(0, T // SUB, body, 0)
    acc = acc_ref[...]
    rows = 2 * HEADS * SUB
    acc = acc[:rows] + acc[rows:]
    sub_row = lax.broadcasted_iota(jnp.int32, acc.shape, 0) % SUB
    sub_col = lax.broadcasted_iota(jnp.int32, acc.shape, 1) % SUB
    acc = jnp.where(sub_row == sub_col, acc, 0.0)
    acc = acc.reshape(2 * HEADS, SUB, HIDDEN * SUB).sum(axis=1)
    unit = lax.broadcasted_iota(jnp.int32, (HIDDEN * SUB, D), 0) // SUB
    lane = lax.broadcasted_iota(jnp.int32, (HIDDEN * SUB, D), 1) % HIDDEN
    gather = jnp.where(unit == lane, 1.0, 0.0)
    sums = lax.dot_general(
        acc, gather, (((1,), (0,)), ((), ())),
        precision=lax.Precision.HIGHEST, preferred_element_type=jnp.float32,
    )
    w_ref[...] = coef_ref[0] * sums[:HEADS] + coef_ref[1] * sums[HEADS:]


def merge(own, got, upper):
    first = jnp.where(upper, got, own)
    second = jnp.where(upper, own, got)
    return pairs_summed(jnp.concatenate([first, second], 0))


def pairs_summed(rows, by=2):
    return rows.reshape(rows.shape[0] // by, by, rows.shape[1]).sum(1)


def spread(rows, by):
    return jnp.repeat(rows, by, axis=0)


def sibling(rows, group):
    return lax.dynamic_slice_in_dim(rows, (group ^ 1) * COARSE, COARSE, 0)


def placed(mine, other, upper):
    return jnp.where(upper, jnp.concatenate([other, mine], 0), jnp.concatenate([mine, other], 0))


def halves(back, upper):
    low, high = spread(back[: COARSE // 2], 2), spread(back[COARSE // 2 :], 2)
    return jnp.where(upper, high, low), jnp.where(upper, low, high)


def swap_groups(value, groups):
    return lax.all_to_all(value, "ctx", 0, 0, axis_index_groups=groups)


def shards(queries, keys, values, lengths, fire_w1, fire_b1, fire_w2, grad_out):
    f32, bf16 = jnp.float32, jnp.bfloat16
    shape = jax.ShapeDtypeStruct
    ctx = lax.axis_index("ctx")
    mp = lax.axis_index("mp")
    bit = [(ctx >> k) & 1 == 1 for k in range(LEVELS)]
    blocks = range(SIDE)
    low_groups = [[high * SIDE + low for low in blocks] for high in blocks]
    high_groups = [[high * SIDE + (low ^ (8 * (high % 2))) for high in blocks] for low in blocks]

    w2 = lax.dynamic_slice_in_dim(fire_w2, mp * HEADS, HEADS, 1)
    w2_t = w2.T
    same = jnp.eye(SUB, dtype=f32)
    w2_wide = (w2_t[:, None, :, None] * same[None, :, None, :]).reshape(HEADS * SUB, HIDDEN * SUB)
    zero = jnp.zeros((HEADS, HIDDEN), f32)
    own_w2 = lambda row, core: jnp.broadcast_to(jnp.where(mp == core, row, 0.0)[None], (HEADS, HIDDEN))
    coef = jnp.stack([
        jnp.concatenate([own_w2(fire_b1, 0), own_w2(fire_b1, 1), zero, w2_t], axis=1),
        jnp.concatenate([own_w2(fire_w1, 0), own_w2(fire_w1, 1), w2_t, zero], axis=1),
    ])

    fine, wide = pl.pallas_call(
        leaf_kernel,
        out_shape=(shape((COARSE, 2 * WIDTH + D), f32), shape((CHUNK, 2 * WIDTH + D), f32)),
        in_specs=[SMEM, VMEM, VMEM],
        out_specs=(VMEM, VMEM),
        name="leaf",
    )(lengths, keys, values)
    bias, phase = pl.pallas_call(
        bias_kernel,
        out_shape=(shape((HEADS, T, KEYS), f32), shape((T, KEYS), f32)),
        in_specs=[SMEM] * 3 + [VMEM],
        out_specs=(VMEM, VMEM),
        cost_estimate=pl.CostEstimate(flops=600_000_000, bytes_accessed=2_000_000, transcendentals=50_000),
        name="bias",
    )(ctx.reshape(1), fire_w1, fire_b1, w2_wide)

    got0 = exchange(fine, 0)
    got1 = exchange(merge(fine, got0, bit[0]), 1)
    low = swap_groups(jnp.broadcast_to(wide[None], (SIDE,) + wide.shape), low_groups)
    low = low.reshape(SIDE * CHUNK, -1)
    sib2 = sibling(low, (ctx >> 2) & 3)
    low = pairs_summed(low)
    sib3 = sibling(low, (ctx >> 3) & 1)
    own4 = pairs_summed(low)
    got4 = exchange(own4, 4)
    got5 = exchange(merge(own4, got4, bit[4]), 5)
    wide4 = pairs_summed(own4, 4)
    high = swap_groups(jnp.broadcast_to(wide4[None], (SIDE,) + wide4.shape), high_groups)
    high = high.reshape(SIDE * CHUNK, -1)
    sib6 = sibling(high, (ctx >> 6) & 3)
    sib7 = sibling(pairs_summed(high), (ctx >> 7) & 1)
    siblings = jnp.concatenate([got0, got1, sib2, sib3, got4, got5, sib6, sib7], 0)

    attended, grad_q, own_grad, coarse, dscores = pl.pallas_call(
        main_kernel,
        out_shape=(
            shape((T, HEADS * D), bf16),
            shape((T, HEADS * D), bf16),
            shape((T, 2 * WIDTH), f32),
            shape((LEVELS * COARSE, 2 * WIDTH), f32),
            shape((HEADS, T, KEYS), f32),
        ),
        in_specs=[SMEM] + [VMEM] * 6,
        out_specs=(VMEM,) * 5,
        compiler_params=pltpu.CompilerParams(vmem_limit_bytes=32 * 2**20),
        name="attention",
    )(lengths, queries, keys, values, grad_out, siblings, bias)
    w_part = pl.pallas_call(
        weight_kernel,
        out_shape=shape((HEADS, D), f32),
        in_specs=[SMEM, SMEM] + [VMEM] * 3,
        out_specs=VMEM,
        scratch_shapes=[pltpu.VMEM((4 * HEADS * SUB, HIDDEN * SUB), f32)],
        cost_estimate=pl.CostEstimate(flops=900_000_000, bytes_accessed=2_000_000, transcendentals=0),
        name="weights",
    )(fire_w1, fire_b1, coef, dscores, phase)
    w_part = w_part + lax.ppermute(w_part, "mp", [(0, 1), (1, 0)])

    part = [coarse[k * COARSE : (k + 1) * COARSE] for k in range(LEVELS)]
    none = jnp.zeros_like(part[0])
    keep4, send4 = halves(exchange(part[5], 5), bit[4])
    keep0, send0 = halves(exchange(part[1], 1), bit[0])
    came4 = exchange(part[4] + send4, 4)
    came0 = exchange(part[0] + send0, 0)
    away = placed(placed(none, part[6], bit[6]), spread(part[7], 2), bit[7])
    away = sent_back(away, w_part, high_groups)
    group4 = keep4 + came4 + spread(away[:, : 2 * WIDTH], SIDE // 4)
    near = placed(placed(none, part[2], bit[2]), spread(part[3], 2), bit[3])
    near = sent_back(near + spread(group4, SIDE // 4), away[:, 2 * WIDTH :], low_groups)
    back = keep0 + came0 + spread(near[:, : 2 * WIDTH], SIDE // 4)

    token_live = (jnp.arange(T) < lengths[0]).astype(f32)[:, None]
    token_grad = ((own_grad + spread(back, T // COARSE)) * token_live).astype(bf16)
    w_all = near[:, 2 * WIDTH :]
    grad_w2 = jnp.concatenate([w_all[:, :HIDDEN], w_all[:, HIDDEN : 2 * HIDDEN]], 0).T
    grad_w1 = w_all[:, 2 * HIDDEN : 3 * HIDDEN].sum(0)
    grad_b1 = w_all[:, 3 * HIDDEN :].sum(0)
    return (attended, grad_q, token_grad[:, :WIDTH], token_grad[:, WIDTH:], grad_w1, grad_b1, grad_w2)


def sent_back(rows, weights, groups):
    rows = rows.reshape(SIDE, CHUNK, -1)
    weights = jnp.broadcast_to(weights[None], (SIDE,) + weights.shape)
    got = swap_groups(jnp.concatenate([rows, weights], 2), groups)
    return (got[: SIDE // 2] + got[SIDE // 2 :]).sum(0)


def solution(mesh):
    split = P("ctx", "mp")
    return jax.shard_map(
        shards,
        mesh=mesh,
        in_specs=(split, split, split, P("ctx"), P(), P(), P(), split),
        out_specs=(split, split, split, split, P(), P(), P()),
        check_vma=False,
    )
```

```python
import functools

import jax
import jax.numpy as jnp
from jax import lax
from jax.experimental import pallas as pl
from jax.experimental.pallas import tpu as pltpu
from jax.sharding import PartitionSpec as P

D = 128
COARSE = 32
T = 128
HALF = T // 2
LEVELS = 8
KEYS = T + LEVELS * COARSE
HIDDEN = 32
HEADS = 8
KV = 2
GROUP = HEADS // KV
SUB = 8
CHUNK = 8
SIDE = 16
WIDTH = KV * D
LEVEL_TOKENS = float(T * 2**LEVELS)
SCALE = D ** (-0.5)
MASKS = (1, 2, 6, 8, 24, 32, 64, 192)
NT = (((1,), (1,)), ((), ()))
TN = (((0,), (0,)), ((), ()))
VMEM = pl.BlockSpec(memory_space=pltpu.VMEM)
SMEM = pl.BlockSpec(memory_space=pltpu.SMEM)


def dot(a, b, dims=(((1,), (0,)), ((), ()))):
    return lax.dot_general(a, b, dims, preferred_element_type=jnp.float32)


def exchange(value, level):
    pairs = [(i, i ^ MASKS[level]) for i in range(lax.axis_size("ctx"))]
    return lax.ppermute(value, "ctx", pairs)


def leaf_kernel(len_ref, k_ref, v_ref, fine_ref, wide_ref):
    wide = []
    for run in (T // COARSE, T // CHUNK):
        row = lax.broadcasted_iota(jnp.int32, (T // run, T), 0)
        tok = lax.broadcasted_iota(jnp.int32, (T // run, T), 1)
        member = jnp.where((tok // run == row) & (tok < len_ref[0]), 1.0, 0.0)
        member_b = member.astype(jnp.bfloat16)
        count = jnp.sum(member, axis=1, keepdims=True)
        wide = [dot(member_b, k_ref[...]), dot(member_b, v_ref[...]), jnp.broadcast_to(count, (T // run, D))]
        if run == T // COARSE:
            fine_ref[...] = jnp.concatenate(wide, axis=1)
    wide = jnp.concatenate(wide, axis=1)
    for n in range(SIDE):
        wide_ref[n] = wide


def bias_kernel(first, ctx_ref, w1_ref, b1_ref, w2_ref, after_ref, bias_ref, phase_ref):
    ctx = ctx_ref[0]
    col = lax.broadcasted_iota(jnp.int32, (1, KEYS), 1)
    level = (col - T) // COARSE
    pos = col.astype(jnp.float32)
    for k in range(LEVELS):
        run = 2**k * T // COARSE
        start = ((ctx >> k) ^ 1) * 2**k * T - ctx * T
        inside = (col - T - k * COARSE) * run
        here = (start + inside).astype(jnp.float32) + (run - 1) / 2.0
        pos = jnp.where((col >= T) & (level == k), here, pos)
    top = jnp.log1p(jnp.full((1, KEYS), LEVEL_TOKENS, jnp.float32))
    weight = w2_ref[...]
    weight_high = weight.astype(jnp.bfloat16)
    weight_low = (weight - weight_high.astype(jnp.float32)).astype(jnp.bfloat16)
    weight_both = jnp.concatenate([weight_high, weight_low], axis=0)

    def body(i, carry):
        rows = pl.ds(pl.multiple_of(i * SUB, SUB), SUB)
        row = first + i * SUB + lax.broadcasted_iota(jnp.int32, (SUB, KEYS), 0)
        phase = jnp.log1p(jnp.abs(row.astype(jnp.float32) - pos)) / top
        phase_ref[rows, :] = phase
        hidden = [jnp.maximum(phase * w1_ref[m] + b1_ref[m], 0.0) for m in range(HIDDEN)]
        hidden = jnp.concatenate(hidden, axis=0)
        high = hidden.astype(jnp.bfloat16)
        low = (hidden - high.astype(jnp.float32)).astype(jnp.bfloat16)
        with_high = dot(weight_both, high)
        bias = with_high[: HEADS * SUB] + with_high[HEADS * SUB :] + dot(weight_high, low)
        for h in range(HEADS):
            bias_ref[h, rows, :] = bias[h * SUB : (h + 1) * SUB]
        return carry

    lax.fori_loop(0, HALF // SUB, body, 0)


def pooled(rows, by):
    shape = (rows.shape[0] // by, rows.shape[0])
    row = lax.broadcasted_iota(jnp.int32, shape, 0)
    col = lax.broadcasted_iota(jnp.int32, shape, 1)
    return lax.dot_general(
        jnp.where(col // by == row, 1.0, 0.0), rows, (((1,), (0,)), ((), ())),
        precision=lax.Precision.HIGHEST, preferred_element_type=jnp.float32,
    )


def middle_kernel(low_ref, after_ref, own_ref, wide_ref):
    own = pooled(low_ref[...], SIDE * CHUNK // COARSE)
    own_ref[...] = own
    wide = pooled(own, COARSE // CHUNK)
    for n in range(SIDE):
        wide_ref[n] = wide


def main_kernel(
    ctx_ref, len_ref, q_ref, k_ref, v_ref, g_ref, got0_ref, got1_ref, low_ref, got4_ref, got5_ref, high_ref,
    bias_a_ref, bias_b_ref, out_ref, gq_ref, own_ref, coarse_ref, ds_ref, sib_ref,
):
    length = len_ref[0]
    ctx = ctx_ref[0]
    for level, ref in ((0, got0_ref), (1, got1_ref), (4, got4_ref), (5, got5_ref)):
        sib_ref[level * COARSE : (level + 1) * COARSE, :] = ref[...]
    for level, ref in ((2, low_ref), (6, high_ref)):
        start = pl.multiple_of((((ctx >> level) & 3) ^ 1) * COARSE, COARSE)
        sib_ref[level * COARSE : (level + 1) * COARSE, :] = ref[pl.ds(start, COARSE), :]
        start = pl.multiple_of((((ctx >> level + 1) & 1) ^ 1) * 2 * COARSE, 2 * COARSE)
        sib_ref[(level + 1) * COARSE : (level + 2) * COARSE, :] = pooled(ref[pl.ds(start, 2 * COARSE), :], 2)
    count = sib_ref[:, 2 * KV * D :]
    safe = jnp.maximum(count, 1.0)
    count_t = jnp.concatenate([count[:T].T[:1], count[T:].T[:1]], axis=1)
    token_live = lax.broadcasted_iota(jnp.int32, (1, T), 1) < length
    live = jnp.concatenate([token_live.astype(jnp.float32), count_t], axis=1) > 0.0
    row_live = lax.broadcasted_iota(jnp.int32, (T, 1), 0) < length
    row_live_f = row_live.astype(jnp.float32)
    for j in range(KV):
        cols = slice(j * D, (j + 1) * D)
        vcols = slice((KV + j) * D, (KV + j + 1) * D)
        keys = jnp.concatenate([k_ref[:, cols], (sib_ref[:, cols] / safe).astype(jnp.bfloat16)], axis=0)
        values = jnp.concatenate([v_ref[:, cols], (sib_ref[:, vcols] / safe).astype(jnp.bfloat16)], axis=0)
        key_grads = jnp.zeros((KEYS, D), jnp.float32)
        value_grads = jnp.zeros((KEYS, D), jnp.float32)
        for g in range(GROUP):
            h = j * GROUP + g
            hcols = slice(h * D, (h + 1) * D)
            query = q_ref[:, hcols]
            scores = dot(query, keys, NT) * SCALE
            scores = scores + jnp.concatenate([bias_a_ref[h], bias_b_ref[h]], axis=0)
            scores = jnp.where(live, scores, -jnp.inf)
            top = jnp.max(scores, axis=1, keepdims=True)
            weights = jnp.exp(scores - top)
            probs = weights / jnp.sum(weights, axis=1, keepdims=True)
            probs_b = probs.astype(jnp.bfloat16)
            out_ref[:, hcols] = (dot(probs_b, values) * row_live_f).astype(jnp.bfloat16)
            grad = g_ref[:, hcols]
            grad = jnp.where(row_live, grad, jnp.zeros_like(grad))
            dprobs = dot(grad, values, NT)
            dscores = probs * (dprobs - jnp.sum(probs * dprobs, axis=1, keepdims=True))
            ds_ref[h] = dscores
            dscores_b = dscores.astype(jnp.bfloat16)
            gq_ref[:, hcols] = (SCALE * dot(dscores_b, keys)).astype(jnp.bfloat16)
            key_grads = key_grads + dot(dscores_b, query, TN)
            value_grads = value_grads + dot(probs_b, grad, TN)
        key_grads = key_grads * SCALE
        own_ref[:, cols] = key_grads[:T]
        own_ref[:, vcols] = value_grads[:T]
        coarse_ref[:, cols] = key_grads[T:] / safe
        coarse_ref[:, vcols] = value_grads[T:] / safe


def weight_kernel(ctx_ref, w1_ref, b1_ref, coef_ref, ds_ref, phase_a_ref, phase_b_ref, coarse_ref, away_ref, acc_ref):
    acc_ref[...] = jnp.zeros_like(acc_ref)

    def body(phase_of, first, i, carry):
        rows = pl.ds(pl.multiple_of(i * SUB, SUB), SUB)
        phase = phase_of[rows, :]
        rows = pl.ds(pl.multiple_of(first + i * SUB, SUB), SUB)
        parts = [ds_ref[h, rows, :] for h in range(HEADS)]
        parts = jnp.concatenate(parts + [p * phase for p in parts], axis=0)
        high = parts.astype(jnp.bfloat16)
        low = (parts - high.astype(jnp.float32)).astype(jnp.bfloat16)
        both = jnp.concatenate([high, low], axis=0)
        active = [
            jnp.where(phase * w1_ref[m] + b1_ref[m] > 0.0, 1.0, 0.0) for m in range(HIDDEN)
        ]
        active = jnp.concatenate(active, axis=0).astype(jnp.bfloat16)
        acc_ref[...] += dot(both, active, NT)
        return carry

    lax.fori_loop(0, HALF // SUB, functools.partial(body, phase_a_ref, 0), 0)
    lax.fori_loop(0, HALF // SUB, functools.partial(body, phase_b_ref, HALF), 0)
    acc = acc_ref[...]
    rows = 2 * HEADS * SUB
    acc = acc[:rows] + acc[rows:]
    sub_row = lax.broadcasted_iota(jnp.int32, acc.shape, 0) % SUB
    sub_col = lax.broadcasted_iota(jnp.int32, acc.shape, 1) % SUB
    acc = jnp.where(sub_row == sub_col, acc, 0.0)
    acc = acc.reshape(2 * HEADS, SUB, HIDDEN * SUB).sum(axis=1)
    unit = lax.broadcasted_iota(jnp.int32, (HIDDEN * SUB, D), 0) // SUB
    lane = lax.broadcasted_iota(jnp.int32, (HIDDEN * SUB, D), 1) % HIDDEN
    gather = jnp.where(unit == lane, 1.0, 0.0)
    sums = lax.dot_general(
        acc, gather, (((1,), (0,)), ((), ())),
        precision=lax.Precision.HIGHEST, preferred_element_type=jnp.float32,
    )
    weights = coef_ref[0] * sums[:HEADS] + coef_ref[1] * sums[HEADS:]
    place_levels(ctx_ref[0], 6, coarse_ref, away_ref, None, weights)


def place_levels(ctx, level, coarse_ref, out_ref, base, weights):
    quarter = (ctx >> level) & 3
    near = coarse_ref[level * COARSE : (level + 1) * COARSE, :]
    far = coarse_ref[(level + 1) * COARSE : (level + 2) * COARSE, :]
    far = jnp.broadcast_to(far[:, None, :], (COARSE, 2, 2 * WIDTH)).reshape(2 * COARSE, 2 * WIDTH)
    for q in range(4):
        rows = jnp.where(quarter == q ^ 1, near, 0.0)
        rows = jnp.where(quarter >> 1 != q >> 1, far[(q & 1) * COARSE : (q & 1) * COARSE + COARSE], rows)
        if base is not None:
            rows = rows + base[q * COARSE : (q + 1) * COARSE]
        for n in range(4):
            out_ref[q * 4 + n, :, : 2 * WIDTH] = rows[n * CHUNK : (n + 1) * CHUNK]
            out_ref[q * 4 + n, :, 2 * WIDTH :] = weights


def summed(ref):
    return sum(ref[n] + ref[n + SIDE // 2] for n in range(SIDE // 2))


def repeated(rows, by):
    return jnp.broadcast_to(rows[:, None, :], (rows.shape[0], by, rows.shape[1])).reshape(-1, rows.shape[1])


def return_kernel(ctx_ref, away_ref, keep_ref, came_ref, coarse_ref, near_ref):
    away = summed(away_ref)
    group = keep_ref[...] + came_ref[...] + repeated(away[:, : 2 * WIDTH], SIDE // 4)
    place_levels(ctx_ref[0], 2, coarse_ref, near_ref, repeated(group, SIDE // 4), away[:, 2 * WIDTH :])


def final_kernel(len_ref, near_ref, keep_ref, came_ref, own_ref, gk_ref, gv_ref):
    near = summed(near_ref)
    back = keep_ref[...] + came_ref[...] + repeated(near[:, : 2 * WIDTH], SIDE // 4)
    live = lax.broadcasted_iota(jnp.int32, (T, 1), 0) < len_ref[0]
    grad = (own_ref[...] + repeated(back, T // COARSE)) * live.astype(jnp.float32)
    gk_ref[...] = grad[:, :WIDTH].astype(jnp.bfloat16)
    gv_ref[...] = grad[:, WIDTH:].astype(jnp.bfloat16)


def merge(own, got, upper):
    first = jnp.where(upper, got, own)
    second = jnp.where(upper, own, got)
    return jnp.concatenate([first, second], 0).reshape(COARSE, 2, -1).sum(1)


def halves(back, upper):
    low, high = jnp.repeat(back[: COARSE // 2], 2, axis=0), jnp.repeat(back[COARSE // 2 :], 2, axis=0)
    return jnp.where(upper, high, low), jnp.where(upper, low, high)


def swap_groups(value, groups):
    return lax.all_to_all(value, "ctx", 0, 0, axis_index_groups=groups)


def shards(queries, keys, values, lengths, fire_w1, fire_b1, fire_w2, grad_out):
    f32, bf16 = jnp.float32, jnp.bfloat16
    shape = jax.ShapeDtypeStruct
    ctx = lax.axis_index("ctx")
    mp = lax.axis_index("mp")
    ctx_1 = ctx.reshape(1)
    bit = [(ctx >> k) & 1 == 1 for k in range(LEVELS)]
    blocks = range(SIDE)
    low_groups = [[high * SIDE + low for low in blocks] for high in blocks]
    high_groups = [[high * SIDE + (low ^ (8 * (high % 2))) for high in blocks] for low in blocks]

    w2 = lax.dynamic_slice_in_dim(fire_w2, mp * HEADS, HEADS, 1)
    w2_t = w2.T
    same = jnp.eye(SUB, dtype=f32)
    w2_wide = (w2_t[:, None, :, None] * same[None, :, None, :]).reshape(HEADS * SUB, HIDDEN * SUB)
    zero = jnp.zeros((HEADS, HIDDEN), f32)
    own_w2 = lambda row, core: jnp.broadcast_to(jnp.where(mp == core, row, 0.0)[None], (HEADS, HIDDEN))
    coef = jnp.stack([
        jnp.concatenate([own_w2(fire_b1, 0), own_w2(fire_b1, 1), zero, w2_t], axis=1),
        jnp.concatenate([own_w2(fire_w1, 0), own_w2(fire_w1, 1), w2_t, zero], axis=1),
    ])

    payload = shape((SIDE, CHUNK, 2 * WIDTH + D), f32)
    sums = shape((COARSE, 2 * WIDTH + D), f32)
    fine, wide = pl.pallas_call(
        leaf_kernel,
        out_shape=(sums, payload),
        in_specs=[SMEM, VMEM, VMEM],
        out_specs=(VMEM, VMEM),
        name="leaf",
    )(lengths, keys, values)

    def bias_half(first, after):
        return pl.pallas_call(
            functools.partial(bias_kernel, first),
            out_shape=(shape((HEADS, HALF, KEYS), f32), shape((HALF, KEYS), f32)),
            in_specs=[SMEM] * 3 + [VMEM, pl.BlockSpec(memory_space=pl.ANY)],
            out_specs=(VMEM, VMEM),
            cost_estimate=pl.CostEstimate(flops=300_000_000, bytes_accessed=1_000_000, transcendentals=25_000),
            name="bias",
        )(ctx_1, fire_w1, fire_b1, w2_wide, after)

    low = swap_groups(wide, low_groups).reshape(SIDE * CHUNK, -1)
    bias_a, phase_a = bias_half(0, fine)
    own4, wide4 = pl.pallas_call(
        middle_kernel,
        out_shape=(sums, payload),
        in_specs=[VMEM, pl.BlockSpec(memory_space=pl.ANY)],
        out_specs=(VMEM, VMEM),
        name="middle",
    )(low, phase_a)
    high = swap_groups(wide4, high_groups).reshape(SIDE * CHUNK, -1)
    bias_b, phase_b = bias_half(HALF, own4)
    got0 = exchange(fine, 0)
    got1 = exchange(merge(fine, got0, bit[0]), 1)
    got4 = exchange(own4, 4)
    got5 = exchange(merge(own4, got4, bit[4]), 5)

    attended, grad_q, own_grad, coarse, dscores = pl.pallas_call(
        main_kernel,
        out_shape=(
            shape((T, HEADS * D), bf16),
            shape((T, HEADS * D), bf16),
            shape((T, 2 * WIDTH), f32),
            shape((LEVELS * COARSE, 2 * WIDTH), f32),
            shape((HEADS, T, KEYS), f32),
        ),
        in_specs=[SMEM, SMEM] + [VMEM] * 12,
        out_specs=(VMEM,) * 5,
        scratch_shapes=[pltpu.VMEM((LEVELS * COARSE, 2 * WIDTH + D), f32)],
        compiler_params=pltpu.CompilerParams(vmem_limit_bytes=32 * 2**20),
        name="attention",
    )(ctx_1, lengths, queries, keys, values, grad_out, got0, got1, low, got4, got5, high, bias_a, bias_b)
    part = [coarse[k * COARSE : (k + 1) * COARSE] for k in range(LEVELS)]
    keep4, send4 = halves(exchange(part[5], 5), bit[4])
    keep0, send0 = halves(exchange(part[1], 1), bit[0])
    away = pl.pallas_call(
        weight_kernel,
        out_shape=payload,
        in_specs=[SMEM] * 3 + [VMEM] * 5,
        out_specs=VMEM,
        scratch_shapes=[pltpu.VMEM((4 * HEADS * SUB, HIDDEN * SUB), f32)],
        cost_estimate=pl.CostEstimate(flops=900_000_000, bytes_accessed=2_000_000, transcendentals=0),
        name="weights",
    )(ctx_1, fire_w1, fire_b1, coef, dscores, phase_a, phase_b, coarse)
    away = swap_groups(away, high_groups)
    came4 = exchange(part[4] + send4, 4)
    came0 = exchange(part[0] + send0, 0)
    near = pl.pallas_call(
        return_kernel,
        out_shape=payload,
        in_specs=[SMEM] + [VMEM] * 4,
        out_specs=VMEM,
        name="return",
    )(ctx_1, away, keep4, came4, coarse)
    near = swap_groups(near, low_groups)
    grad_k, grad_v = pl.pallas_call(
        final_kernel,
        out_shape=(shape((T, WIDTH), bf16), shape((T, WIDTH), bf16)),
        in_specs=[SMEM] + [VMEM] * 4,
        out_specs=(VMEM, VMEM),
        name="final",
    )(lengths, near, keep0, came0, own_grad)
    w_all = near[:, :, 2 * WIDTH :]
    w_all = (w_all[: SIDE // 2] + w_all[SIDE // 2 :]).sum(0)
    w_all = w_all + lax.ppermute(w_all, "mp", [(0, 1), (1, 0)])
    grad_w2 = jnp.concatenate([w_all[:, :HIDDEN], w_all[:, HIDDEN : 2 * HIDDEN]], 0).T
    grad_w1 = w_all[:, 2 * HIDDEN : 3 * HIDDEN].sum(0)
    grad_b1 = w_all[:, 3 * HIDDEN :].sum(0)
    return (attended, grad_q, grad_k, grad_v, grad_w1, grad_b1, grad_w2)


def solution(mesh):
    split = P("ctx", "mp")
    return jax.shard_map(
        shards,
        mesh=mesh,
        in_specs=(split, split, split, P("ctx"), P(), P(), P(), split),
        out_specs=(split, split, split, split, P(), P(), P()),
        check_vma=False,
    )
```

```python
import functools

import jax
import jax.numpy as jnp
from jax import lax
from jax.experimental import pallas as pl
from jax.experimental.pallas import tpu as pltpu
from jax.sharding import PartitionSpec as P

D = 128
COARSE = 32
T = 128
LEVELS = 8
KEYS = T + LEVELS * COARSE
HIDDEN = 32
HEADS = 8
KV = 2
GROUP = HEADS // KV
SUB = 8
BATCH = 4
UNROLL = 2
CHUNK = 8
SIDE = 16
WIDTH = KV * D
LEVEL_TOKENS = float(T * 2**LEVELS)
SCALE = D ** (-0.5)
MASKS = (1, 2, 6, 8, 24, 32, 64, 192)
NT = (((1,), (1,)), ((), ()))
TN = (((0,), (0,)), ((), ()))
VMEM = pl.BlockSpec(memory_space=pltpu.VMEM)
SMEM = pl.BlockSpec(memory_space=pltpu.SMEM)
HBM = pl.BlockSpec(memory_space=pltpu.HBM)
ANY = pl.BlockSpec(memory_space=pl.ANY)
SMALL = pltpu.CompilerParams(vmem_limit_bytes=12 * 2**20)


def dot(a, b, dims=(((1,), (0,)), ((), ()))):
    return lax.dot_general(a, b, dims, preferred_element_type=jnp.float32)


def shifted(value, mask):
    return lax.ppermute(value, "ctx", [(i, i ^ mask) for i in range(lax.axis_size("ctx"))])


def exchange(value, level):
    return shifted(value, MASKS[level])


def fetch(pairs, sems):
    copies = [pltpu.make_async_copy(src, dst, sems.at[n]) for n, (src, dst) in enumerate(pairs)]
    for copy in copies:
        copy.start()
    return copies


def leaf_kernel(len_ref, k_hbm, v_hbm, fine_ref, wide_ref, k_ref, v_ref, sems):
    copies = fetch([(k_hbm, k_ref), (v_hbm, v_ref)], sems)
    row = lax.broadcasted_iota(jnp.int32, (COARSE + CHUNK, T), 0)
    tok = lax.broadcasted_iota(jnp.int32, (COARSE + CHUNK, T), 1)
    run = jnp.where(row < COARSE, tok // (T // COARSE), tok // (T // CHUNK) + COARSE)
    member = jnp.where((run == row) & (tok < len_ref[0]), 1.0, 0.0)
    member_b = member.astype(jnp.bfloat16)
    count = jnp.broadcast_to(jnp.sum(member, axis=1, keepdims=True), (COARSE + CHUNK, D))
    for copy in copies:
        copy.wait()
    rows = jnp.concatenate([dot(member_b, k_ref[...]), dot(member_b, v_ref[...]), count], axis=1)
    fine_ref[...] = rows[:COARSE, : 2 * WIDTH]
    for n in range(SIDE):
        wide_ref[n] = rows[COARSE:]


def exact_dot(a, b, dims=(((1,), (0,)), ((), ()))):
    return lax.dot_general(a, b, dims, precision=lax.Precision.HIGHEST, preferred_element_type=jnp.float32)


def unit_weights(core, w2_ref, rows, columns, by_row, by_column):
    shape = (rows, 2 * HEADS)
    head = lax.broadcasted_iota(jnp.int32, shape, 0) // by_row + core * HEADS
    pick = jnp.where(lax.broadcasted_iota(jnp.int32, shape, 1) == head, 1.0, 0.0)
    return exact_dot(exact_dot(pick, w2_ref[...]), unit_columns(columns, by_column))


def unit_columns(columns, by):
    unit = lax.broadcasted_iota(jnp.int32, (HIDDEN, columns), 0)
    column = lax.broadcasted_iota(jnp.int32, (HIDDEN, columns), 1)
    return jnp.where(column // by % HIDDEN == unit, 1.0, 0.0)


def bias_kernel(
    place_ref, w1_hbm, b1_hbm, w2_hbm, after_ref, bias_ref, phase_ref, line_ref, slot_ref, w1_ref, b1_ref, w2_ref, sems
):
    copies = fetch([(w1_hbm, w1_ref), (b1_hbm, b1_ref), (w2_hbm, w2_ref)], sems)
    ctx, core = place_ref[0], place_ref[1]
    col = lax.broadcasted_iota(jnp.int32, (1, KEYS), 1)
    level = (col - T) // COARSE
    pos = col.astype(jnp.float32)
    for k in range(LEVELS):
        run = 2**k * T // COARSE
        start = ((ctx >> k) ^ 1) * 2**k * T - ctx * T
        inside = (col - T - k * COARSE) * run
        here = (start + inside).astype(jnp.float32) + (run - 1) / 2.0
        pos = jnp.where((col >= T) & (level == k), here, pos)
    top = jnp.log1p(jnp.full((1, KEYS), LEVEL_TOKENS, jnp.float32))
    row = lax.broadcasted_iota(jnp.int32, (T, KEYS), 0).astype(jnp.float32)
    phase_ref[...] = jnp.log1p(jnp.abs(row - pos)) / top
    for copy in copies:
        copy.wait()
    lane = lax.broadcasted_iota(jnp.int32, (HEADS, D), 1) // HIDDEN
    w2 = unit_weights(core, w2_ref, HEADS, D, 1, 1)
    spread = unit_columns(HIDDEN * SUB, SUB)
    for n, ref in enumerate((w1_ref, b1_ref)):
        line = jnp.broadcast_to(ref[...], (D, HIDDEN))
        line_ref[n] = exact_dot(spread, line, (((0,), (1,)), ((), ())))
        slot_ref[n] = jnp.where(lane == core, exact_dot(ref[...], unit_columns(D, 1)), jnp.where(lane == 2 + n, w2, 0.0))
    weight = unit_weights(core, w2_ref, HEADS * SUB, HIDDEN * SUB, SUB, SUB)
    row = lax.broadcasted_iota(jnp.int32, weight.shape, 0)
    column = lax.broadcasted_iota(jnp.int32, weight.shape, 1)
    weight = jnp.where(row % SUB == column % SUB, weight, 0.0)
    weight_high = weight.astype(jnp.bfloat16)
    weight_low = (weight - weight_high.astype(jnp.float32)).astype(jnp.bfloat16)
    weight_both = jnp.concatenate([weight_high, weight_low], axis=0)

    def body(i, carry):
        rows = pl.ds(pl.multiple_of(i * SUB, SUB), SUB)
        hidden = jnp.maximum(by_units(line_ref, phase_ref[rows, :]), 0.0)
        high = hidden.astype(jnp.bfloat16)
        low = (hidden - high.astype(jnp.float32)).astype(jnp.bfloat16)
        with_high = dot(weight_both, high)
        bias = with_high[: HEADS * SUB] + with_high[HEADS * SUB :] + dot(weight_high, low)
        for h in range(HEADS):
            bias_ref[h, rows, :] = bias[h * SUB : (h + 1) * SUB]
        return carry

    lax.fori_loop(0, T // SUB, body, 0, unroll=UNROLL)


def by_units(line_ref, phase):
    slope = line_ref[0].reshape(HIDDEN, SUB, D)
    offset = line_ref[1].reshape(HIDDEN, SUB, D)
    tiles = [phase[None, :, n * D : (n + 1) * D] * slope + offset for n in range(KEYS // D)]
    return jnp.concatenate(tiles, axis=2).reshape(HIDDEN * SUB, KEYS)


def pooled(rows, by):
    shape = (rows.shape[0] // by, rows.shape[0])
    row = lax.broadcasted_iota(jnp.int32, shape, 0)
    col = lax.broadcasted_iota(jnp.int32, shape, 1)
    return picked(jnp.where(col // by == row, 1.0, 0.0).astype(jnp.bfloat16), rows)


def middle_kernel(low_ref, after_bias_ref, after_merge_ref, own_ref, wide_ref):
    row = lax.broadcasted_iota(jnp.int32, (COARSE + CHUNK, SIDE * CHUNK), 0)
    col = lax.broadcasted_iota(jnp.int32, (COARSE + CHUNK, SIDE * CHUNK), 1)
    run = jnp.where(row < COARSE, col >> 2, (col >> 4) + COARSE)
    rows = picked(jnp.where(run == row, 1.0, 0.0).astype(jnp.bfloat16), low_ref[...])
    own_ref[...] = rows[:COARSE]
    for n in range(SIDE):
        wide_ref[n] = rows[COARSE:]


def main_kernel(
    place_ref, len_ref, q_hbm, k_hbm, v_hbm, g_hbm, got0_ref, got1_ref, low_ref, got4_ref, got5_ref, high_ref, bias_ref,
    out_ref, gq_ref, own_ref, coarse_ref, ds_ref, q_ref, k_ref, v_ref, g_ref, sib_ref, sems,
):
    copies = fetch([(k_hbm, k_ref), (q_hbm, q_ref), (v_hbm, v_ref), (g_hbm, g_ref)], sems)
    length = len_ref[0]
    ctx = place_ref[0]
    for level, ref in ((0, got0_ref), (1, got1_ref), (4, got4_ref), (5, got5_ref)):
        sib_ref[level * COARSE : (level + 1) * COARSE, : ref.shape[1]] = ref[...]
    for level, ref in ((2, low_ref), (6, high_ref)):
        start = pl.multiple_of((((ctx >> level) & 3) ^ 1) * COARSE, COARSE)
        sib_ref[level * COARSE : (level + 1) * COARSE, :] = ref[pl.ds(start, COARSE), :]
        start = pl.multiple_of((((ctx >> level + 1) & 1) ^ 1) * 2 * COARSE, 2 * COARSE)
        sib_ref[(level + 1) * COARSE : (level + 2) * COARSE, :] = pooled(ref[pl.ds(start, 2 * COARSE), :], 2)
    group = (((ctx >> 1) & 7) ^ 1) * 2
    blocks = ((0, COARSE, (ctx & 15) ^ 1), (COARSE, COARSE // 2, group), (COARSE * 3 // 2, COARSE // 2, group + 1))
    for first, rows, block in blocks:
        block = low_ref[pl.ds(pl.multiple_of(block * CHUNK, CHUNK), CHUNK), 2 * WIDTH :]
        run = T // rows
        before = lax.broadcasted_iota(jnp.int32, (rows, D), 0) * run
        here = jnp.sum(block, axis=0, keepdims=True) - before.astype(jnp.float32)
        sib_ref[first : first + rows, 2 * WIDTH :] = jnp.clip(here, 0.0, float(run))
    count = sib_ref[:, 2 * WIDTH :]
    inverse = 1.0 / jnp.maximum(count, 1.0)
    count_t = jnp.concatenate([count[:T].T[:1], count[T:].T[:1]], axis=1)
    token_live = lax.broadcasted_iota(jnp.int32, (1, T), 1) < length
    live = jnp.concatenate([token_live.astype(jnp.float32), count_t], axis=1) > 0.0
    row_live = lax.broadcasted_iota(jnp.int32, (T, 1), 0) < length
    for copy in copies:
        copy.wait()
    for j in range(KV):
        cols = slice(j * D, (j + 1) * D)
        vcols = slice((KV + j) * D, (KV + j + 1) * D)
        keys = jnp.concatenate([k_ref[:, cols], (sib_ref[:, cols] * inverse).astype(jnp.bfloat16)], axis=0)
        values = jnp.concatenate([v_ref[:, cols], (sib_ref[:, vcols] * inverse).astype(jnp.bfloat16)], axis=0)
        heads = range(j * GROUP, (j + 1) * GROUP)
        key_grads = jnp.zeros((KEYS, D), jnp.float32)
        value_grads = jnp.zeros((KEYS, D), jnp.float32)
        for first in range(j * GROUP, (j + 1) * GROUP, BATCH):
            heads = range(first, first + BATCH)
            query = jnp.concatenate([q_ref[:, h * D : (h + 1) * D] for h in heads], axis=0)
            grad = [g_ref[:, h * D : (h + 1) * D] for h in heads]
            grad = jnp.concatenate([jnp.where(row_live, part, jnp.zeros_like(part)) for part in grad], axis=0)
            scores = dot(query, keys, NT) * SCALE + bias_ref[first : first + BATCH].reshape(BATCH * T, KEYS)
            scores = jnp.where(live, scores, -jnp.inf)
            weights = jnp.exp(scores - jnp.max(scores, axis=1, keepdims=True))
            probs = weights * (1.0 / jnp.sum(weights, axis=1, keepdims=True))
            probs_b = probs.astype(jnp.bfloat16)
            attended = dot(probs_b, values)
            dprobs = dot(grad, values, NT)
            dscores = probs * (dprobs - jnp.sum(probs * dprobs, axis=1, keepdims=True))
            ds_ref[first : first + BATCH] = dscores.reshape(BATCH, T, KEYS)
            dscores_b = dscores.astype(jnp.bfloat16)
            grad_query = dot(dscores_b, keys) * SCALE
            for n, h in enumerate(heads):
                rows = slice(n * T, (n + 1) * T)
                out_ref[:, h * D : (h + 1) * D] = jnp.where(row_live, attended[rows], 0.0).astype(jnp.bfloat16)
                gq_ref[:, h * D : (h + 1) * D] = grad_query[rows].astype(jnp.bfloat16)
            key_grads = key_grads + dot(dscores_b, query, TN)
            value_grads = value_grads + dot(probs_b, grad, TN)
        key_grads = key_grads * SCALE
        own_ref[:, cols] = key_grads[:T]
        own_ref[:, vcols] = value_grads[:T]
        coarse_ref[:, cols] = key_grads[T:] * inverse
        coarse_ref[:, vcols] = value_grads[T:] * inverse


def weight_kernel(
    line_ref, slot_ref, ds_ref, phase_ref, out_ref, gq_ref, w_ref, out_hbm, gq_hbm, acc_ref, sems
):
    copies = fetch([(out_ref, out_hbm), (gq_ref, gq_hbm)], sems)
    acc_ref[...] = jnp.zeros_like(acc_ref)

    def body(i, carry):
        rows = pl.ds(pl.multiple_of(i * SUB, SUB), SUB)
        phase = phase_ref[rows, :]
        parts = [ds_ref[h, rows, :] for h in range(HEADS)]
        parts = jnp.concatenate(parts + [p * phase for p in parts], axis=0)
        high = parts.astype(jnp.bfloat16)
        low = (parts - high.astype(jnp.float32)).astype(jnp.bfloat16)
        both = jnp.concatenate([high, low], axis=0)
        active = jnp.where(by_units(line_ref, phase) > 0.0, 1.0, 0.0).astype(jnp.bfloat16)
        acc_ref[...] += dot(both, active, NT)
        return carry

    lax.fori_loop(0, T // SUB, body, 0, unroll=UNROLL)
    acc = acc_ref[...]
    rows = 2 * HEADS * SUB
    acc = acc[:rows] + acc[rows:]
    sub_row = lax.broadcasted_iota(jnp.int32, acc.shape, 0) % SUB
    sub_col = lax.broadcasted_iota(jnp.int32, acc.shape, 1) % SUB
    acc = jnp.where(sub_row == sub_col, acc, 0.0)
    acc = acc.reshape(2 * HEADS, SUB, HIDDEN * SUB).sum(axis=1)
    unit = lax.broadcasted_iota(jnp.int32, (HIDDEN * SUB, D), 0) // SUB
    lane = lax.broadcasted_iota(jnp.int32, (HIDDEN * SUB, D), 1) % HIDDEN
    sums = exact_dot(acc, jnp.where(unit == lane, 1.0, 0.0))
    w_ref[...] = slot_ref[1] * sums[:HEADS] + slot_ref[0] * sums[HEADS:]
    for copy in copies:
        copy.wait()


def chosen(rows, parts):
    sizes = [value.shape[0] for value, _ in parts]
    depth = -(-sum(sizes) // 16) * 16
    row = lax.broadcasted_iota(jnp.int32, (rows, 1), 0)
    col = lax.broadcasted_iota(jnp.int32, (rows, depth), 1)
    pick, first = col < 0, 0
    for size, (_, name) in zip(sizes, parts):
        pick = pick | (col == name(row, first))
        first += size
    pick = jnp.where(pick, 1.0, 0.0).astype(jnp.bfloat16)
    value = [value for value, _ in parts]
    if first < depth:
        value.append(jnp.zeros((depth - first, value[0].shape[1]), jnp.float32))
    return picked(pick, jnp.concatenate(value, axis=0))


def picked(pick, value):
    total = 0.0
    for _ in range(3):
        part = value.astype(jnp.bfloat16)
        total = total + dot(pick, part)
        value = value - part.astype(jnp.float32)
    return total


def level_parts(ctx, level, coarse_ref):
    quarter = (ctx >> level) & 3

    def near(i, first):
        return jnp.where(i >> 5 == quarter ^ 1, (i & 31) + first, -1)

    def far(i, first):
        return jnp.where(i >> 6 != quarter >> 1, ((i & 63) >> 1) + first, -1)

    return [
        (coarse_ref[level * COARSE : (level + 1) * COARSE, :], near),
        (coarse_ref[(level + 1) * COARSE : (level + 2) * COARSE, :], far),
    ]


def half_of(ctx, level, shift):
    return lambda i, first: first + ((ctx >> level) & 1) * (COARSE // 2) + (i >> shift)


def every(shift):
    return lambda i, first: first + (i >> shift)


def sibling_rows(ctx, level, coarse_ref, came_ref):
    return chosen(
        COARSE,
        [
            (coarse_ref[level * COARSE : (level + 1) * COARSE, :], every(0)),
            (came_ref[...], half_of(ctx ^ (1 << level), level, 1)),
        ],
    )


def fill(payload_ref, rows, weights):
    for n in range(SIDE):
        payload_ref[n, :, : 2 * WIDTH] = rows[n * CHUNK : (n + 1) * CHUNK]
        payload_ref[n, :, 2 * WIDTH :] = weights


def away_kernel(place_ref, w_ref, coarse_ref, came5_ref, away_ref, send_ref):
    ctx = place_ref[0]
    fill(away_ref, chosen(SIDE * CHUNK, level_parts(ctx, 6, coarse_ref)), w_ref[...])
    send_ref[...] = sibling_rows(ctx, 4, coarse_ref, came5_ref)


def summed(ref):
    return sum(ref[n] + ref[n + SIDE // 2] for n in range(SIDE // 2))


def return_kernel(place_ref, away_ref, came5_ref, came4_ref, came1_ref, coarse_ref, near_ref, send_ref):
    ctx = place_ref[0]
    away = summed(away_ref)
    parts = level_parts(ctx, 2, coarse_ref)
    parts += [(came5_ref[...], half_of(ctx, 4, 3)), (came4_ref[...], every(2))]
    parts += [(away[:, : 2 * WIDTH], every(4))]
    fill(near_ref, chosen(SIDE * CHUNK, parts), away[:, 2 * WIDTH :])
    send_ref[...] = sibling_rows(ctx, 0, coarse_ref, came1_ref)


def final_kernel(place_ref, len_ref, near_ref, came1_ref, came0_ref, own_ref, gk_ref, gv_ref):
    ctx = place_ref[0]
    near = sum(near_ref[n, :, : 2 * WIDTH] for n in range(SIDE))
    parts = [(came1_ref[...], half_of(ctx, 0, 3)), (came0_ref[...], every(2)), (near, every(4))]
    live = lax.broadcasted_iota(jnp.int32, (T, 1), 0) < len_ref[0]
    grad = jnp.where(live, own_ref[...] + chosen(T, parts), 0.0)
    gk_ref[...] = grad[:, :WIDTH].astype(jnp.bfloat16)
    gv_ref[...] = grad[:, WIDTH:].astype(jnp.bfloat16)


def outputs_kernel(mine_ref, got_ref, w1_ref, b1_ref, w2_ref):
    total = mine_ref[...] + got_ref[...]
    for core in range(2):
        w2_ref[core * HEADS : (core + 1) * HEADS, :] = total[:, core * HIDDEN : (core + 1) * HIDDEN]
    sums = jnp.sum(total, axis=0, keepdims=True)
    w1_ref[...] = sums[:, 2 * HIDDEN : 3 * HIDDEN]
    b1_ref[...] = sums[:, 3 * HIDDEN :]


def merge_kernel(place_ref, own_ref, got_ref, out_ref):
    shape = (COARSE, 2 * COARSE)
    row = lax.broadcasted_iota(jnp.int32, shape, 0)
    col = lax.broadcasted_iota(jnp.int32, shape, 1)
    upper = (place_ref[0] >> 4) & 1
    pick = jnp.where((row & 15 == (col & 31) >> 1) & (row >> 4 == (col >> 5) ^ upper), 1.0, 0.0)
    out_ref[...] = picked(pick.astype(jnp.bfloat16), jnp.concatenate([own_ref[...], got_ref[...]], axis=0))


def merge(own, got, upper):
    first = jnp.where(upper, got, own)
    second = jnp.where(upper, own, got)
    return jnp.concatenate([first, second], 0).reshape(COARSE, 2, -1).sum(1)


def in_hbm(value):
    return pltpu.with_memory_space_constraint(value, pltpu.HBM)


def swap_groups(value, groups):
    return lax.all_to_all(value, "ctx", 0, 0, axis_index_groups=groups)


def shards(queries, keys, values, lengths, fire_w1, fire_b1, fire_w2, grad_out):
    f32, bf16 = jnp.float32, jnp.bfloat16
    shape = jax.ShapeDtypeStruct
    ctx = lax.axis_index("ctx")
    mp = lax.axis_index("mp")
    place = jnp.stack([ctx, mp])
    bit = [(ctx >> k) & 1 == 1 for k in range(LEVELS)]
    blocks = range(SIDE)
    low_groups = [[high * SIDE + low for low in blocks] for high in blocks]
    high_groups = [[high * SIDE + (low ^ (8 * (high % 2))) for high in blocks] for low in blocks]

    payload = shape((SIDE, CHUNK, 2 * WIDTH + D), f32)
    sums = shape((COARSE, 2 * WIDTH + D), f32)
    rows = shape((COARSE, 2 * WIDTH), f32)
    dma = pltpu.SemaphoreType.DMA
    fine, wide = pl.pallas_call(
        leaf_kernel,
        out_shape=(rows, payload),
        in_specs=[SMEM, HBM, HBM],
        out_specs=(VMEM, VMEM),
        scratch_shapes=[pltpu.VMEM((T, WIDTH), bf16)] * 2 + [dma((2,))],
        compiler_params=SMALL,
        name="leaf",
    )(lengths, in_hbm(keys), in_hbm(values))
    low = swap_groups(wide, low_groups).reshape(SIDE * CHUNK, -1)
    got0 = exchange(fine, 0)
    own1 = merge(fine, got0, bit[0])
    wide_tokens, tokens = shape((T, HEADS * D), bf16), shape((T, WIDTH), bf16)
    bias, phase, line, slot = pl.pallas_call(
        bias_kernel,
        out_shape=(
            shape((HEADS, T, KEYS), f32),
            shape((T, KEYS), f32),
            shape((2, HIDDEN * SUB, D), f32),
            shape((2, HEADS, D), f32),
        ),
        in_specs=[SMEM] + [HBM] * 3 + [ANY],
        out_specs=(VMEM,) * 4,
        scratch_shapes=[
            pltpu.VMEM((1, HIDDEN), f32),
            pltpu.VMEM((1, HIDDEN), f32),
            pltpu.VMEM((2 * HEADS, HIDDEN), f32),
            dma((3,)),
        ],
        compiler_params=SMALL,
        cost_estimate=pl.CostEstimate(flops=600_000_000, bytes_accessed=2_000_000, transcendentals=50_000),
        name="bias",
    )(place, *map(in_hbm, (fire_w1.reshape(1, -1), fire_b1.reshape(1, -1), fire_w2.T)), fine)
    own4, wide4 = pl.pallas_call(
        middle_kernel,
        out_shape=(sums, payload),
        in_specs=[VMEM, ANY, ANY],
        out_specs=(VMEM, VMEM),
        compiler_params=SMALL,
        name="middle",
    )(low, slot, own1)
    high = swap_groups(wide4, high_groups).reshape(SIDE * CHUNK, -1)
    got4 = exchange(own4, 4)
    got1 = exchange(jnp.pad(own1, ((0, 0), (0, D))), 1)
    own5 = pl.pallas_call(
        merge_kernel,
        out_shape=sums,
        in_specs=[SMEM, VMEM, VMEM],
        out_specs=VMEM,
        compiler_params=SMALL,
        name="merge",
    )(place, own4, got4)
    got5 = exchange(own5, 5)

    attended, grad_q, own_grad, coarse, dscores = pl.pallas_call(
        main_kernel,
        out_shape=(
            wide_tokens,
            wide_tokens,
            shape((T, 2 * WIDTH), f32),
            shape((LEVELS * COARSE, 2 * WIDTH), f32),
            shape((HEADS, T, KEYS), f32),
        ),
        in_specs=[SMEM, SMEM] + [HBM] * 4 + [VMEM] * 7,
        out_specs=(VMEM,) * 5,
        scratch_shapes=[pltpu.VMEM((T, n), bf16) for n in (HEADS * D, WIDTH, WIDTH, HEADS * D)]
        + [pltpu.VMEM((LEVELS * COARSE, 2 * WIDTH + D), f32), dma((4,))],
        compiler_params=SMALL,
        name="attention",
    )(place, lengths, *map(in_hbm, (queries, keys, values, grad_out)), got0, got1, low, got4, got5, high, bias)

    came5 = exchange(coarse[5 * COARSE : 6 * COARSE], 5)
    w_part, attended, grad_q = pl.pallas_call(
        weight_kernel,
        out_shape=(shape((HEADS, D), f32), wide_tokens, wide_tokens),
        in_specs=[VMEM] * 6,
        out_specs=(VMEM, HBM, HBM),
        scratch_shapes=[pltpu.VMEM((4 * HEADS * SUB, HIDDEN * SUB), f32), dma((2,))],
        compiler_params=SMALL,
        cost_estimate=pl.CostEstimate(flops=900_000_000, bytes_accessed=2_000_000, transcendentals=0),
        name="weights",
    )(line, slot, dscores, phase, attended, grad_q)
    away, send4 = pl.pallas_call(
        away_kernel,
        out_shape=(payload, rows),
        in_specs=[SMEM] + [VMEM] * 3,
        out_specs=(VMEM, VMEM),
        compiler_params=SMALL,
        name="away",
    )(place, w_part, coarse, came5)
    away = swap_groups(away, high_groups)
    came4 = exchange(send4, 4)
    came1 = exchange(coarse[COARSE : 2 * COARSE], 1)
    near, send0 = pl.pallas_call(
        return_kernel,
        out_shape=(payload, rows),
        in_specs=[SMEM] + [VMEM] * 5,
        out_specs=(VMEM, VMEM),
        compiler_params=SMALL,
        name="return",
    )(place, away, came5, came4, came1, coarse)
    near = swap_groups(near, low_groups)
    came0 = exchange(send0, 0)
    w_all = near[:, :, 2 * WIDTH :]
    w_all = (w_all[: SIDE // 2] + w_all[SIDE // 2 :]).sum(0)
    w_other = lax.ppermute(w_all, "mp", [(0, 1), (1, 0)])
    grad_k, grad_v = pl.pallas_call(
        final_kernel,
        out_shape=(tokens, tokens),
        in_specs=[SMEM, SMEM] + [VMEM] * 4,
        out_specs=(VMEM, VMEM),
        compiler_params=SMALL,
        name="final",
    )(place, lengths, near, came1, came0, own_grad)
    grad_w1, grad_b1, grad_w2 = pl.pallas_call(
        outputs_kernel,
        out_shape=(shape((1, HIDDEN), f32), shape((1, HIDDEN), f32), shape((2 * HEADS, HIDDEN), f32)),
        in_specs=[VMEM] * 2,
        out_specs=(VMEM,) * 3,
        compiler_params=SMALL,
        name="outputs",
    )(w_all, w_other)
    grad_w1, grad_b1, grad_w2 = grad_w1.reshape(-1), grad_b1.reshape(-1), grad_w2.T
    return (attended, grad_q, grad_k, grad_v, grad_w1, grad_b1, grad_w2)


def solution(mesh):
    split = P("ctx", "mp")
    return jax.shard_map(
        shards,
        mesh=mesh,
        in_specs=(split, split, split, P("ctx"), P(), P(), P(), split),
        out_specs=(split, split, split, split, P(), P(), P()),
        check_vma=False,
    )
```

```python
import functools

import jax
import jax.numpy as jnp
from jax import lax
from jax.experimental import pallas as pl
from jax.experimental.pallas import tpu as pltpu
from jax.sharding import PartitionSpec as P

D = 128
COARSE = 32
T = 128
LEVELS = 8
KEYS = T + LEVELS * COARSE
HIDDEN = 32
HEADS = 8
KV = 2
GROUP = HEADS // KV
SUB = 8
BATCH = 4
UNROLL = 2
CHUNK = 8
SIDE = 16
FIRST = {"low": 12, "high": 12, "away": 3, "near": 2}
WIDTH = KV * D
LEVEL_TOKENS = float(T * 2**LEVELS)
SCALE = D ** (-0.5)
MASKS = (1, 2, 6, 8, 24, 32, 64, 192)
NT = (((1,), (1,)), ((), ()))
TN = (((0,), (0,)), ((), ()))
VMEM = pl.BlockSpec(memory_space=pltpu.VMEM)
SMEM = pl.BlockSpec(memory_space=pltpu.SMEM)
HBM = pl.BlockSpec(memory_space=pltpu.HBM)
ANY = pl.BlockSpec(memory_space=pl.ANY)
SMALL = pltpu.CompilerParams(vmem_limit_bytes=12 * 2**20)


def dot(a, b, dims=(((1,), (0,)), ((), ()))):
    return lax.dot_general(a, b, dims, preferred_element_type=jnp.float32)


def shifted(value, mask):
    return lax.ppermute(value, "ctx", [(i, i ^ mask) for i in range(lax.axis_size("ctx"))])


def exchange(value, level):
    return shifted(value, MASKS[level])


def fetch(pairs, sems):
    copies = [pltpu.make_async_copy(src, dst, sems.at[n]) for n, (src, dst) in enumerate(pairs)]
    for copy in copies:
        copy.start()
    return copies


def leaf_kernel(len_ref, k_hbm, v_hbm, fine_ref, wide_ref, k_ref, v_ref, sems):
    copies = fetch([(k_hbm, k_ref), (v_hbm, v_ref)], sems)
    row = lax.broadcasted_iota(jnp.int32, (COARSE + CHUNK, T), 0)
    tok = lax.broadcasted_iota(jnp.int32, (COARSE + CHUNK, T), 1)
    run = jnp.where(row < COARSE, tok // (T // COARSE), tok // (T // CHUNK) + COARSE)
    member = jnp.where((run == row) & (tok < len_ref[0]), 1.0, 0.0)
    member_b = member.astype(jnp.bfloat16)
    count = jnp.broadcast_to(jnp.sum(member, axis=1, keepdims=True), (COARSE + CHUNK, D))
    for copy in copies:
        copy.wait()
    rows = jnp.concatenate([dot(member_b, k_ref[...]), dot(member_b, v_ref[...]), count], axis=1)
    fine_ref[...] = rows[:COARSE, : 2 * WIDTH]
    for n in range(SIDE):
        wide_ref[n] = rows[COARSE:]


def exact_dot(a, b, dims=(((1,), (0,)), ((), ()))):
    return lax.dot_general(a, b, dims, precision=lax.Precision.HIGHEST, preferred_element_type=jnp.float32)


def unit_weights(core, w2_ref, rows, columns, by_row, by_column):
    shape = (rows, 2 * HEADS)
    head = lax.broadcasted_iota(jnp.int32, shape, 0) // by_row + core * HEADS
    pick = jnp.where(lax.broadcasted_iota(jnp.int32, shape, 1) == head, 1.0, 0.0)
    return exact_dot(exact_dot(pick, w2_ref[...]), unit_columns(columns, by_column))


def unit_columns(columns, by):
    unit = lax.broadcasted_iota(jnp.int32, (HIDDEN, columns), 0)
    column = lax.broadcasted_iota(jnp.int32, (HIDDEN, columns), 1)
    return jnp.where(column // by % HIDDEN == unit, 1.0, 0.0)


def bias_kernel(
    place_ref, w1_hbm, b1_hbm, w2_hbm, after_ref, bias_ref, phase_ref, line_ref, slot_ref, w1_ref, b1_ref, w2_ref, sems
):
    copies = fetch([(w1_hbm, w1_ref), (b1_hbm, b1_ref), (w2_hbm, w2_ref)], sems)
    ctx, core = place_ref[0], place_ref[1]
    col = lax.broadcasted_iota(jnp.int32, (1, KEYS), 1)
    level = (col - T) // COARSE
    pos = col.astype(jnp.float32)
    for k in range(LEVELS):
        run = 2**k * T // COARSE
        start = ((ctx >> k) ^ 1) * 2**k * T - ctx * T
        inside = (col - T - k * COARSE) * run
        here = (start + inside).astype(jnp.float32) + (run - 1) / 2.0
        pos = jnp.where((col >= T) & (level == k), here, pos)
    top = jnp.log1p(jnp.full((1, KEYS), LEVEL_TOKENS, jnp.float32))
    row = lax.broadcasted_iota(jnp.int32, (T, KEYS), 0).astype(jnp.float32)
    phase_ref[...] = jnp.log1p(jnp.abs(row - pos)) / top
    for copy in copies:
        copy.wait()
    lane = lax.broadcasted_iota(jnp.int32, (HEADS, D), 1) // HIDDEN
    w2 = unit_weights(core, w2_ref, HEADS, D, 1, 1)
    spread = unit_columns(HIDDEN * SUB, SUB)
    for n, ref in enumerate((w1_ref, b1_ref)):
        line = jnp.broadcast_to(ref[...], (D, HIDDEN))
        line_ref[n] = exact_dot(spread, line, (((0,), (1,)), ((), ())))
        slot_ref[n] = jnp.where(lane == core, exact_dot(ref[...], unit_columns(D, 1)), jnp.where(lane == 2 + n, w2, 0.0))
    weight = unit_weights(core, w2_ref, HEADS * SUB, HIDDEN * SUB, SUB, SUB)
    row = lax.broadcasted_iota(jnp.int32, weight.shape, 0)
    column = lax.broadcasted_iota(jnp.int32, weight.shape, 1)
    weight = jnp.where(row % SUB == column % SUB, weight, 0.0)
    weight_high = weight.astype(jnp.bfloat16)
    weight_low = (weight - weight_high.astype(jnp.float32)).astype(jnp.bfloat16)
    weight_both = jnp.concatenate([weight_high, weight_low], axis=0)

    def body(i, carry):
        rows = pl.ds(pl.multiple_of(i * SUB, SUB), SUB)
        hidden = jnp.maximum(by_units(line_ref, phase_ref[rows, :]), 0.0)
        high = hidden.astype(jnp.bfloat16)
        low = (hidden - high.astype(jnp.float32)).astype(jnp.bfloat16)
        with_high = dot(weight_both, high)
        bias = with_high[: HEADS * SUB] + with_high[HEADS * SUB :] + dot(weight_high, low)
        for h in range(HEADS):
            bias_ref[h, rows, :] = bias[h * SUB : (h + 1) * SUB]
        return carry

    lax.fori_loop(0, T // SUB, body, 0, unroll=UNROLL)


def by_units(line_ref, phase):
    slope = line_ref[0].reshape(HIDDEN, SUB, D)
    offset = line_ref[1].reshape(HIDDEN, SUB, D)
    tiles = [phase[None, :, n * D : (n + 1) * D] * slope + offset for n in range(KEYS // D)]
    return jnp.concatenate(tiles, axis=2).reshape(HIDDEN * SUB, KEYS)


def pooled(rows, by):
    shape = (rows.shape[0] // by, rows.shape[0])
    row = lax.broadcasted_iota(jnp.int32, shape, 0)
    col = lax.broadcasted_iota(jnp.int32, shape, 1)
    return picked(jnp.where(col // by == row, 1.0, 0.0).astype(jnp.bfloat16), rows)


def middle_kernel(low_ref, after_bias_ref, after_merge_ref, own_ref, wide_ref):
    row = lax.broadcasted_iota(jnp.int32, (COARSE + CHUNK, SIDE * CHUNK), 0)
    col = lax.broadcasted_iota(jnp.int32, (COARSE + CHUNK, SIDE * CHUNK), 1)
    member = (col >> 3) ^ FIRST["low"]
    run = jnp.where(row < COARSE, (member << 1) + ((col & 7) >> 2), (member >> 1) + COARSE)
    rows = picked(jnp.where(run == row, 1.0, 0.0).astype(jnp.bfloat16), low_ref[...])
    own_ref[...] = rows[:COARSE]
    for n in range(SIDE):
        wide_ref[n] = rows[COARSE:]


def main_kernel(
    place_ref, len_ref, q_hbm, k_hbm, v_hbm, g_hbm, got0_ref, got1_ref, low_ref, got4_ref, got5_ref, high_ref, bias_ref,
    out_ref, gq_ref, own_ref, coarse_ref, ds_ref, q_ref, k_ref, v_ref, g_ref, sib_ref, sems,
):
    copies = fetch([(k_hbm, k_ref), (q_hbm, q_ref), (v_hbm, v_ref), (g_hbm, g_ref)], sems)
    length = len_ref[0]
    ctx = place_ref[0]
    for level, ref in ((0, got0_ref), (1, got1_ref), (4, got4_ref), (5, got5_ref)):
        sib_ref[level * COARSE : (level + 1) * COARSE, : ref.shape[1]] = ref[...]
    for level, ref, first in ((2, low_ref, FIRST["low"] >> 2), (6, high_ref, FIRST["high"] >> 2)):
        quarter = ((ctx >> level) & 3) ^ 1
        start = pl.multiple_of((quarter ^ first) * COARSE, COARSE)
        sib_ref[level * COARSE : (level + 1) * COARSE, :] = ref[pl.ds(start, COARSE), :]
        for n in range(2):
            quarter = (((ctx >> level + 1) & 1) ^ 1) * 2 + n
            start = pl.multiple_of((quarter ^ first) * COARSE, COARSE)
            place = (level + 1) * COARSE + n * COARSE // 2
            sib_ref[place : place + COARSE // 2, :] = pooled(ref[pl.ds(start, COARSE), :], 2)
    group = (((ctx >> 1) & 7) ^ 1) * 2
    blocks = ((0, COARSE, (ctx & 15) ^ 1), (COARSE, COARSE // 2, group), (COARSE * 3 // 2, COARSE // 2, group + 1))
    for first, rows, block in blocks:
        block = low_ref[pl.ds(pl.multiple_of((block ^ FIRST["low"]) * CHUNK, CHUNK), CHUNK), 2 * WIDTH :]
        run = T // rows
        before = lax.broadcasted_iota(jnp.int32, (rows, D), 0) * run
        here = jnp.sum(block, axis=0, keepdims=True) - before.astype(jnp.float32)
        sib_ref[first : first + rows, 2 * WIDTH :] = jnp.clip(here, 0.0, float(run))
    count = sib_ref[:, 2 * WIDTH :]
    inverse = 1.0 / jnp.maximum(count, 1.0)
    count_t = jnp.concatenate([count[:T].T[:1], count[T:].T[:1]], axis=1)
    token_live = lax.broadcasted_iota(jnp.int32, (1, T), 1) < length
    live = jnp.concatenate([token_live.astype(jnp.float32), count_t], axis=1) > 0.0
    row_live = lax.broadcasted_iota(jnp.int32, (T, 1), 0) < length
    for copy in copies:
        copy.wait()
    for j in range(KV):
        cols = slice(j * D, (j + 1) * D)
        vcols = slice((KV + j) * D, (KV + j + 1) * D)
        keys = jnp.concatenate([k_ref[:, cols], (sib_ref[:, cols] * inverse).astype(jnp.bfloat16)], axis=0)
        values = jnp.concatenate([v_ref[:, cols], (sib_ref[:, vcols] * inverse).astype(jnp.bfloat16)], axis=0)
        heads = range(j * GROUP, (j + 1) * GROUP)
        key_grads = jnp.zeros((KEYS, D), jnp.float32)
        value_grads = jnp.zeros((KEYS, D), jnp.float32)
        for first in range(j * GROUP, (j + 1) * GROUP, BATCH):
            heads = range(first, first + BATCH)
            query = jnp.concatenate([q_ref[:, h * D : (h + 1) * D] for h in heads], axis=0)
            grad = [g_ref[:, h * D : (h + 1) * D] for h in heads]
            grad = jnp.concatenate([jnp.where(row_live, part, jnp.zeros_like(part)) for part in grad], axis=0)
            scores = dot(query, keys, NT) * SCALE + bias_ref[first : first + BATCH].reshape(BATCH * T, KEYS)
            scores = jnp.where(live, scores, -jnp.inf)
            weights = jnp.exp(scores - jnp.max(scores, axis=1, keepdims=True))
            probs = weights * (1.0 / jnp.sum(weights, axis=1, keepdims=True))
            probs_b = probs.astype(jnp.bfloat16)
            attended = dot(probs_b, values)
            dprobs = dot(grad, values, NT)
            dscores = probs * (dprobs - jnp.sum(probs * dprobs, axis=1, keepdims=True))
            ds_ref[first : first + BATCH] = dscores.reshape(BATCH, T, KEYS)
            dscores_b = dscores.astype(jnp.bfloat16)
            grad_query = dot(dscores_b, keys) * SCALE
            for n, h in enumerate(heads):
                rows = slice(n * T, (n + 1) * T)
                out_ref[:, h * D : (h + 1) * D] = jnp.where(row_live, attended[rows], 0.0).astype(jnp.bfloat16)
                gq_ref[:, h * D : (h + 1) * D] = grad_query[rows].astype(jnp.bfloat16)
            key_grads = key_grads + dot(dscores_b, query, TN)
            value_grads = value_grads + dot(probs_b, grad, TN)
        key_grads = key_grads * SCALE
        own_ref[:, cols] = key_grads[:T]
        own_ref[:, vcols] = value_grads[:T]
        coarse_ref[:, cols] = key_grads[T:] * inverse
        coarse_ref[:, vcols] = value_grads[T:] * inverse


def weight_kernel(
    line_ref, slot_ref, ds_ref, phase_ref, out_ref, gq_ref, w_ref, out_hbm, gq_hbm, acc_ref, sems
):
    copies = fetch([(out_ref, out_hbm), (gq_ref, gq_hbm)], sems)
    acc_ref[...] = jnp.zeros_like(acc_ref)

    def body(i, carry):
        rows = pl.ds(pl.multiple_of(i * SUB, SUB), SUB)
        phase = phase_ref[rows, :]
        parts = [ds_ref[h, rows, :] for h in range(HEADS)]
        parts = jnp.concatenate(parts + [p * phase for p in parts], axis=0)
        high = parts.astype(jnp.bfloat16)
        low = (parts - high.astype(jnp.float32)).astype(jnp.bfloat16)
        both = jnp.concatenate([high, low], axis=0)
        active = jnp.where(by_units(line_ref, phase) > 0.0, 1.0, 0.0).astype(jnp.bfloat16)
        acc_ref[...] += dot(both, active, NT)
        return carry

    lax.fori_loop(0, T // SUB, body, 0, unroll=UNROLL)
    acc = acc_ref[...]
    rows = 2 * HEADS * SUB
    acc = acc[:rows] + acc[rows:]
    sub_row = lax.broadcasted_iota(jnp.int32, acc.shape, 0) % SUB
    sub_col = lax.broadcasted_iota(jnp.int32, acc.shape, 1) % SUB
    acc = jnp.where(sub_row == sub_col, acc, 0.0)
    acc = acc.reshape(2 * HEADS, SUB, HIDDEN * SUB).sum(axis=1)
    unit = lax.broadcasted_iota(jnp.int32, (HIDDEN * SUB, D), 0) // SUB
    lane = lax.broadcasted_iota(jnp.int32, (HIDDEN * SUB, D), 1) % HIDDEN
    sums = exact_dot(acc, jnp.where(unit == lane, 1.0, 0.0))
    w_ref[...] = slot_ref[1] * sums[:HEADS] + slot_ref[0] * sums[HEADS:]
    for copy in copies:
        copy.wait()


def chosen(rows, parts):
    sizes = [value.shape[0] for value, _ in parts]
    depth = -(-sum(sizes) // 16) * 16
    row = lax.broadcasted_iota(jnp.int32, (rows, 1), 0)
    col = lax.broadcasted_iota(jnp.int32, (rows, depth), 1)
    pick, first = col < 0, 0
    for size, (_, name) in zip(sizes, parts):
        pick = pick | (col == name(row, first))
        first += size
    pick = jnp.where(pick, 1.0, 0.0).astype(jnp.bfloat16)
    value = [value for value, _ in parts]
    if first < depth:
        value.append(jnp.zeros((depth - first, value[0].shape[1]), jnp.float32))
    return picked(pick, jnp.concatenate(value, axis=0))


def picked(pick, value):
    total = 0.0
    for _ in range(3):
        part = value.astype(jnp.bfloat16)
        total = total + dot(pick, part)
        value = value - part.astype(jnp.float32)
    return total


def level_parts(ctx, level, coarse_ref):
    quarter = (ctx >> level) & 3

    def near(i, first):
        return jnp.where(i >> 5 == quarter ^ 1, (i & 31) + first, -1)

    def far(i, first):
        return jnp.where(i >> 6 != quarter >> 1, ((i & 63) >> 1) + first, -1)

    return [
        (coarse_ref[level * COARSE : (level + 1) * COARSE, :], near),
        (coarse_ref[(level + 1) * COARSE : (level + 2) * COARSE, :], far),
    ]


def half_of(ctx, level, shift):
    return lambda i, first: first + ((ctx >> level) & 1) * (COARSE // 2) + (i >> shift)


def every(shift):
    return lambda i, first: first + (i >> shift)


def sibling_rows(ctx, level, coarse_ref, came_ref):
    return chosen(
        COARSE,
        [
            (coarse_ref[level * COARSE : (level + 1) * COARSE, :], every(0)),
            (came_ref[...], half_of(ctx ^ (1 << level), level, 1)),
        ],
    )


def fill(payload_ref, first, rows, weights):
    for n in range(SIDE):
        payload_ref[n ^ first, :, : 2 * WIDTH] = rows[n * CHUNK : (n + 1) * CHUNK]
        payload_ref[n ^ first, :, 2 * WIDTH :] = weights


def away_kernel(place_ref, w_ref, coarse_ref, came5_ref, away_ref, send_ref):
    ctx = place_ref[0]
    fill(away_ref, FIRST["away"], chosen(SIDE * CHUNK, level_parts(ctx, 6, coarse_ref)), w_ref[...])
    send_ref[...] = sibling_rows(ctx, 4, coarse_ref, came5_ref)


def summed(ref):
    return sum(ref[n] + ref[n + SIDE // 2] for n in range(SIDE // 2))


def return_kernel(place_ref, away_ref, came5_ref, came4_ref, came1_ref, coarse_ref, near_ref, send_ref):
    ctx = place_ref[0]
    away = summed(away_ref)
    parts = level_parts(ctx, 2, coarse_ref)
    parts += [(came5_ref[...], half_of(ctx, 4, 3)), (came4_ref[...], every(2))]
    parts += [(away[:, : 2 * WIDTH], every(4))]
    fill(near_ref, FIRST["near"] ^ (((ctx >> 4) & 1) * 8), chosen(SIDE * CHUNK, parts), away[:, 2 * WIDTH :])
    send_ref[...] = sibling_rows(ctx, 0, coarse_ref, came1_ref)


def final_kernel(place_ref, len_ref, near_ref, came1_ref, came0_ref, own_ref, gk_ref, gv_ref):
    ctx = place_ref[0]
    near = sum(near_ref[n, :, : 2 * WIDTH] for n in range(SIDE))
    parts = [(came1_ref[...], half_of(ctx, 0, 3)), (came0_ref[...], every(2)), (near, every(4))]
    live = lax.broadcasted_iota(jnp.int32, (T, 1), 0) < len_ref[0]
    grad = jnp.where(live, own_ref[...] + chosen(T, parts), 0.0)
    gk_ref[...] = grad[:, :WIDTH].astype(jnp.bfloat16)
    gv_ref[...] = grad[:, WIDTH:].astype(jnp.bfloat16)


def outputs_kernel(mine_ref, got_ref, w1_ref, b1_ref, w2_ref):
    total = mine_ref[...] + got_ref[...]
    for core in range(2):
        w2_ref[core * HEADS : (core + 1) * HEADS, :] = total[:, core * HIDDEN : (core + 1) * HIDDEN]
    sums = jnp.sum(total, axis=0, keepdims=True)
    w1_ref[...] = sums[:, 2 * HIDDEN : 3 * HIDDEN]
    b1_ref[...] = sums[:, 3 * HIDDEN :]


def merge_kernel(place_ref, own_ref, got_ref, out_ref):
    shape = (COARSE, 2 * COARSE)
    row = lax.broadcasted_iota(jnp.int32, shape, 0)
    col = lax.broadcasted_iota(jnp.int32, shape, 1)
    upper = (place_ref[0] >> 4) & 1
    pick = jnp.where((row & 15 == (col & 31) >> 1) & (row >> 4 == (col >> 5) ^ upper), 1.0, 0.0)
    out_ref[...] = picked(pick.astype(jnp.bfloat16), jnp.concatenate([own_ref[...], got_ref[...]], axis=0))


def merge(own, got, upper):
    first = jnp.where(upper, got, own)
    second = jnp.where(upper, own, got)
    return jnp.concatenate([first, second], 0).reshape(COARSE, 2, -1).sum(1)


def in_hbm(value):
    return pltpu.with_memory_space_constraint(value, pltpu.HBM)


def swap_groups(value, groups):
    return lax.all_to_all(value, "ctx", 0, 0, axis_index_groups=groups)


def shards(queries, keys, values, lengths, fire_w1, fire_b1, fire_w2, grad_out):
    f32, bf16 = jnp.float32, jnp.bfloat16
    shape = jax.ShapeDtypeStruct
    ctx = lax.axis_index("ctx")
    mp = lax.axis_index("mp")
    place = jnp.stack([ctx, mp])
    bit = [(ctx >> k) & 1 == 1 for k in range(LEVELS)]
    blocks = range(SIDE)
    def low_groups(first, odd=0):
        return [[high * SIDE + (low ^ first ^ (odd * (high % 2))) for low in blocks] for high in blocks]

    def high_groups(first):
        order = [high ^ first for high in blocks]
        return [[high * SIDE + (low ^ (8 * (high % 2))) for high in order] for low in blocks]

    payload = shape((SIDE, CHUNK, 2 * WIDTH + D), f32)
    sums = shape((COARSE, 2 * WIDTH + D), f32)
    rows = shape((COARSE, 2 * WIDTH), f32)
    dma = pltpu.SemaphoreType.DMA
    fine, wide = pl.pallas_call(
        leaf_kernel,
        out_shape=(rows, payload),
        in_specs=[SMEM, HBM, HBM],
        out_specs=(VMEM, VMEM),
        scratch_shapes=[pltpu.VMEM((T, WIDTH), bf16)] * 2 + [dma((2,))],
        compiler_params=SMALL,
        name="leaf",
    )(lengths, in_hbm(keys), in_hbm(values))
    low = swap_groups(wide, low_groups(FIRST["low"])).reshape(SIDE * CHUNK, -1)
    got0 = exchange(fine, 0)
    own1 = merge(fine, got0, bit[0])
    wide_tokens, tokens = shape((T, HEADS * D), bf16), shape((T, WIDTH), bf16)
    bias, phase, line, slot = pl.pallas_call(
        bias_kernel,
        out_shape=(
            shape((HEADS, T, KEYS), f32),
            shape((T, KEYS), f32),
            shape((2, HIDDEN * SUB, D), f32),
            shape((2, HEADS, D), f32),
        ),
        in_specs=[SMEM] + [HBM] * 3 + [ANY],
        out_specs=(VMEM,) * 4,
        scratch_shapes=[
            pltpu.VMEM((1, HIDDEN), f32),
            pltpu.VMEM((1, HIDDEN), f32),
            pltpu.VMEM((2 * HEADS, HIDDEN), f32),
            dma((3,)),
        ],
        compiler_params=SMALL,
        cost_estimate=pl.CostEstimate(flops=600_000_000, bytes_accessed=2_000_000, transcendentals=50_000),
        name="bias",
    )(place, *map(in_hbm, (fire_w1.reshape(1, -1), fire_b1.reshape(1, -1), fire_w2.T)), fine)
    own4, wide4 = pl.pallas_call(
        middle_kernel,
        out_shape=(sums, payload),
        in_specs=[VMEM, ANY, ANY],
        out_specs=(VMEM, VMEM),
        compiler_params=SMALL,
        name="middle",
    )(low, slot, own1)
    high = swap_groups(wide4, high_groups(FIRST["high"])).reshape(SIDE * CHUNK, -1)
    got4 = exchange(own4, 4)
    got1 = exchange(jnp.pad(own1, ((0, 0), (0, D))), 1)
    own5 = pl.pallas_call(
        merge_kernel,
        out_shape=sums,
        in_specs=[SMEM, VMEM, VMEM],
        out_specs=VMEM,
        compiler_params=SMALL,
        name="merge",
    )(place, own4, got4)
    got5 = exchange(own5, 5)

    attended, grad_q, own_grad, coarse, dscores = pl.pallas_call(
        main_kernel,
        out_shape=(
            wide_tokens,
            wide_tokens,
            shape((T, 2 * WIDTH), f32),
            shape((LEVELS * COARSE, 2 * WIDTH), f32),
            shape((HEADS, T, KEYS), f32),
        ),
        in_specs=[SMEM, SMEM] + [HBM] * 4 + [VMEM] * 7,
        out_specs=(VMEM,) * 5,
        scratch_shapes=[pltpu.VMEM((T, n), bf16) for n in (HEADS * D, WIDTH, WIDTH, HEADS * D)]
        + [pltpu.VMEM((LEVELS * COARSE, 2 * WIDTH + D), f32), dma((4,))],
        compiler_params=SMALL,
        name="attention",
    )(place, lengths, *map(in_hbm, (queries, keys, values, grad_out)), got0, got1, low, got4, got5, high, bias)

    came5 = exchange(coarse[5 * COARSE : 6 * COARSE], 5)
    w_part, attended, grad_q = pl.pallas_call(
        weight_kernel,
        out_shape=(shape((HEADS, D), f32), wide_tokens, wide_tokens),
        in_specs=[VMEM] * 6,
        out_specs=(VMEM, HBM, HBM),
        scratch_shapes=[pltpu.VMEM((4 * HEADS * SUB, HIDDEN * SUB), f32), dma((2,))],
        compiler_params=SMALL,
        cost_estimate=pl.CostEstimate(flops=900_000_000, bytes_accessed=2_000_000, transcendentals=0),
        name="weights",
    )(line, slot, dscores, phase, attended, grad_q)
    away, send4 = pl.pallas_call(
        away_kernel,
        out_shape=(payload, rows),
        in_specs=[SMEM] + [VMEM] * 3,
        out_specs=(VMEM, VMEM),
        compiler_params=SMALL,
        name="away",
    )(place, w_part, coarse, came5)
    away = swap_groups(away, high_groups(FIRST["away"]))
    came4 = exchange(send4, 4)
    came1 = exchange(coarse[COARSE : 2 * COARSE], 1)
    near, send0 = pl.pallas_call(
        return_kernel,
        out_shape=(payload, rows),
        in_specs=[SMEM] + [VMEM] * 5,
        out_specs=(VMEM, VMEM),
        compiler_params=SMALL,
        name="return",
    )(place, away, came5, came4, came1, coarse)
    near = swap_groups(near, low_groups(FIRST["near"], 8))
    came0 = exchange(send0, 0)
    w_all = near[:, :, 2 * WIDTH :]
    w_all = (w_all[: SIDE // 2] + w_all[SIDE // 2 :]).sum(0)
    w_other = lax.ppermute(w_all, "mp", [(0, 1), (1, 0)])
    grad_k, grad_v = pl.pallas_call(
        final_kernel,
        out_shape=(tokens, tokens),
        in_specs=[SMEM, SMEM] + [VMEM] * 4,
        out_specs=(VMEM, VMEM),
        compiler_params=SMALL,
        name="final",
    )(place, lengths, near, came1, came0, own_grad)
    grad_w1, grad_b1, grad_w2 = pl.pallas_call(
        outputs_kernel,
        out_shape=(shape((1, HIDDEN), f32), shape((1, HIDDEN), f32), shape((2 * HEADS, HIDDEN), f32)),
        in_specs=[VMEM] * 2,
        out_specs=(VMEM,) * 3,
        compiler_params=SMALL,
        name="outputs",
    )(w_all, w_other)
    grad_w1, grad_b1, grad_w2 = grad_w1.reshape(-1), grad_b1.reshape(-1), grad_w2.T
    return (attended, grad_q, grad_k, grad_v, grad_w1, grad_b1, grad_w2)


def solution(mesh):
    split = P("ctx", "mp")
    return jax.shard_map(
        shards,
        mesh=mesh,
        in_specs=(split, split, split, P("ctx"), P(), P(), P(), split),
        out_specs=(split, split, split, split, P(), P(), P()),
        check_vma=False,
    )
```

```python
import functools

import jax
import jax.numpy as jnp
from jax import lax
from jax.experimental import pallas as pl
from jax.experimental.pallas import tpu as pltpu
from jax.sharding import PartitionSpec as P

D = 128
COARSE = 32
T = 128
LEVELS = 8
KEYS = T + LEVELS * COARSE
HIDDEN = 32
HEADS = 8
KV = 2
GROUP = HEADS // KV
SUB = 8
BATCH = 4
UNROLL = 2
CHUNK = 8
SIDE = 16
FIRST = {"low": 12, "high": 14, "away": 3, "near": 2}
WIDTH = KV * D
LEVEL_TOKENS = float(T * 2**LEVELS)
SCALE = D ** (-0.5)
MASKS = (1, 2, 6, 8, 24, 32, 64, 192)
NT = (((1,), (1,)), ((), ()))
TN = (((0,), (0,)), ((), ()))
VMEM = pl.BlockSpec(memory_space=pltpu.VMEM)
SMEM = pl.BlockSpec(memory_space=pltpu.SMEM)
HBM = pl.BlockSpec(memory_space=pltpu.HBM)
ANY = pl.BlockSpec(memory_space=pl.ANY)
SMALL = pltpu.CompilerParams(vmem_limit_bytes=12 * 2**20)


def dot(a, b, dims=(((1,), (0,)), ((), ()))):
    return lax.dot_general(a, b, dims, preferred_element_type=jnp.float32)


def shifted(value, mask):
    return lax.ppermute(value, "ctx", [(i, i ^ mask) for i in range(lax.axis_size("ctx"))])


def exchange(value, level):
    return shifted(value, MASKS[level])


def fetch(pairs, sems):
    copies = [pltpu.make_async_copy(src, dst, sems.at[n]) for n, (src, dst) in enumerate(pairs)]
    for copy in copies:
        copy.start()
    return copies


def leaf_kernel(len_ref, k_hbm, v_hbm, fine_ref, wide_ref, k_ref, v_ref, sems):
    copies = fetch([(k_hbm, k_ref), (v_hbm, v_ref)], sems)
    row = lax.broadcasted_iota(jnp.int32, (COARSE + CHUNK, T), 0)
    tok = lax.broadcasted_iota(jnp.int32, (COARSE + CHUNK, T), 1)
    run = jnp.where(row < COARSE, tok // (T // COARSE), tok // (T // CHUNK) + COARSE)
    member = jnp.where((run == row) & (tok < len_ref[0]), 1.0, 0.0)
    member_b = member.astype(jnp.bfloat16)
    count = jnp.broadcast_to(jnp.sum(member, axis=1, keepdims=True), (COARSE + CHUNK, D))
    for copy in copies:
        copy.wait()
    rows = jnp.concatenate([dot(member_b, k_ref[...]), dot(member_b, v_ref[...]), count], axis=1)
    fine_ref[...] = rows[:COARSE, : 2 * WIDTH]
    for n in range(SIDE):
        wide_ref[n] = rows[COARSE:]


def exact_dot(a, b, dims=(((1,), (0,)), ((), ()))):
    return lax.dot_general(a, b, dims, precision=lax.Precision.HIGHEST, preferred_element_type=jnp.float32)


def unit_weights(core, w2_ref, rows, columns, by_row, by_column):
    shape = (rows, 2 * HEADS)
    head = lax.broadcasted_iota(jnp.int32, shape, 0) // by_row + core * HEADS
    pick = jnp.where(lax.broadcasted_iota(jnp.int32, shape, 1) == head, 1.0, 0.0)
    return exact_dot(exact_dot(pick, w2_ref[...]), unit_columns(columns, by_column))


def unit_columns(columns, by):
    unit = lax.broadcasted_iota(jnp.int32, (HIDDEN, columns), 0)
    column = lax.broadcasted_iota(jnp.int32, (HIDDEN, columns), 1)
    return jnp.where(column // by % HIDDEN == unit, 1.0, 0.0)


def bias_kernel(
    place_ref, w1_hbm, b1_hbm, w2_hbm, after_ref, bias_ref, phase_ref, line_ref, slot_ref, w1_ref, b1_ref, w2_ref, sems
):
    copies = fetch([(w1_hbm, w1_ref), (b1_hbm, b1_ref), (w2_hbm, w2_ref)], sems)
    ctx, core = place_ref[0], place_ref[1]
    col = lax.broadcasted_iota(jnp.int32, (1, KEYS), 1)
    level = (col - T) // COARSE
    pos = col.astype(jnp.float32)
    for k in range(LEVELS):
        run = 2**k * T // COARSE
        start = ((ctx >> k) ^ 1) * 2**k * T - ctx * T
        inside = (col - T - k * COARSE) * run
        here = (start + inside).astype(jnp.float32) + (run - 1) / 2.0
        pos = jnp.where((col >= T) & (level == k), here, pos)
    top = jnp.log1p(jnp.full((1, KEYS), LEVEL_TOKENS, jnp.float32))
    row = lax.broadcasted_iota(jnp.int32, (T, KEYS), 0).astype(jnp.float32)
    phase_ref[...] = jnp.log1p(jnp.abs(row - pos)) / top
    for copy in copies:
        copy.wait()
    lane = lax.broadcasted_iota(jnp.int32, (HEADS, D), 1) // HIDDEN
    w2 = unit_weights(core, w2_ref, HEADS, D, 1, 1)
    spread = unit_columns(HIDDEN * SUB, SUB)
    for n, ref in enumerate((w1_ref, b1_ref)):
        line = jnp.broadcast_to(ref[...], (D, HIDDEN))
        line_ref[n] = exact_dot(spread, line, (((0,), (1,)), ((), ())))
        slot_ref[n] = jnp.where(lane == core, exact_dot(ref[...], unit_columns(D, 1)), jnp.where(lane == 2 + n, w2, 0.0))
    weight = unit_weights(core, w2_ref, HEADS * SUB, HIDDEN * SUB, SUB, SUB)
    row = lax.broadcasted_iota(jnp.int32, weight.shape, 0)
    column = lax.broadcasted_iota(jnp.int32, weight.shape, 1)
    weight = jnp.where(row % SUB == column % SUB, weight, 0.0)
    weight_high = weight.astype(jnp.bfloat16)
    weight_low = (weight - weight_high.astype(jnp.float32)).astype(jnp.bfloat16)
    weight_both = jnp.concatenate([weight_high, weight_low], axis=0)

    def body(i, carry):
        rows = pl.ds(pl.multiple_of(i * SUB, SUB), SUB)
        hidden = jnp.maximum(by_units(line_ref, phase_ref[rows, :]), 0.0)
        high = hidden.astype(jnp.bfloat16)
        low = (hidden - high.astype(jnp.float32)).astype(jnp.bfloat16)
        with_high = dot(weight_both, high)
        bias = with_high[: HEADS * SUB] + with_high[HEADS * SUB :] + dot(weight_high, low)
        for h in range(HEADS):
            bias_ref[h, rows, :] = bias[h * SUB : (h + 1) * SUB]
        return carry

    lax.fori_loop(0, T // SUB, body, 0, unroll=UNROLL)


def by_units(line_ref, phase):
    slope = line_ref[0].reshape(HIDDEN, SUB, D)
    offset = line_ref[1].reshape(HIDDEN, SUB, D)
    tiles = [phase[None, :, n * D : (n + 1) * D] * slope + offset for n in range(KEYS // D)]
    return jnp.concatenate(tiles, axis=2).reshape(HIDDEN * SUB, KEYS)


def pooled(rows, by):
    row = lax.broadcasted_iota(jnp.int32, (rows.shape[0] // by, 1), 0)
    return picked(twice(rows.shape[0] // by, rows.shape[0]) // by == row, rows)


def middle_kernel(low_ref, after_bias_ref, after_merge_ref, own_ref, wide_ref):
    row = lax.broadcasted_iota(jnp.int32, (COARSE + CHUNK, 1), 0)
    col = twice(COARSE + CHUNK, SIDE * CHUNK)
    member = (col >> 3) ^ FIRST["low"]
    run = jnp.where(row < COARSE, (member << 1) + ((col & 7) >> 2), (member >> 1) + COARSE)
    rows = picked(run == row, low_ref[...])
    own_ref[...] = rows[:COARSE]
    for n in range(SIDE):
        wide_ref[n] = rows[COARSE:]


def gather_kernel(
    place_ref, len_ref, q_hbm, k_hbm, v_hbm, g_hbm, got0_ref, got1_ref, low_ref, got4_ref, high_ref, after_ref,
    q_ref, g_ref, keys_ref, values_ref, count_ref, k_ref, v_ref, sib_ref, sems,
):
    copies = fetch([(k_hbm, k_ref), (q_hbm, q_ref), (v_hbm, v_ref), (g_hbm, g_ref)], sems)
    ctx = place_ref[0]
    for level, ref in ((0, got0_ref), (1, got1_ref), (4, got4_ref), (5, got4_ref)):
        sib_ref[level * COARSE : (level + 1) * COARSE, : ref.shape[1]] = ref[...]
    row = lax.broadcasted_iota(jnp.int32, (2 * COARSE, 1), 0)
    col = twice(2 * COARSE, SIDE * CHUNK)
    for level, ref, first in ((2, low_ref, FIRST["low"]), (6, high_ref, FIRST["high"])):
        quarter = ((ctx >> level) & 3) ^ 1
        half = ((ctx >> level + 1) & 1) ^ 1
        place = (((col >> 3) ^ first) << 3) + (col & 7)
        want = jnp.where(row < COARSE, quarter * COARSE + row, (half - 1) * COARSE + row)
        rows = picked(jnp.where(row < COARSE, place, place >> 1) == want, ref[...])
        sib_ref[level * COARSE : (level + 2) * COARSE, :] = rows
    group = (((ctx >> 1) & 7) ^ 1) * 2
    blocks = ((0, COARSE, (ctx & 15) ^ 1), (COARSE, COARSE // 2, group), (COARSE * 3 // 2, COARSE // 2, group + 1))
    for first, rows, block in blocks:
        block = low_ref[pl.ds(pl.multiple_of((block ^ FIRST["low"]) * CHUNK, CHUNK), CHUNK), 2 * WIDTH :]
        run = T // rows
        before = lax.broadcasted_iota(jnp.int32, (rows, D), 0) * run
        here = jnp.sum(block, axis=0, keepdims=True) - before.astype(jnp.float32)
        sib_ref[first : first + rows, 2 * WIDTH :] = jnp.clip(here, 0.0, float(run))
    count = sib_ref[:, 2 * WIDTH :]
    count_ref[...] = count
    inverse = 1.0 / jnp.maximum(count, 1.0)
    for n in range(2 * KV):
        cols = slice(n * D, (n + 1) * D)
        ref = keys_ref if n < KV else values_ref
        ref[T:, n % KV * D : (n % KV + 1) * D] = (sib_ref[:, cols] * inverse).astype(jnp.bfloat16)
    for copy in copies:
        copy.wait()
    keys_ref[:T, :] = k_ref[...]
    values_ref[:T, :] = v_ref[...]
    row_live = lax.broadcasted_iota(jnp.int32, (T, 1), 0) < len_ref[0]
    g_ref[...] = jnp.where(row_live, g_ref[...], jnp.zeros_like(g_ref))


def with_level_5(rows, level, first):
    return jnp.concatenate([rows[: first + 5 * COARSE], level, rows[first + 6 * COARSE :]], axis=0)


def main_kernel(
    len_ref, q_ref, g_ref, keys_ref, values_ref, count_ref, got5_ref, bias_ref,
    out_ref, gq_ref, own_ref, coarse_ref, ds_ref,
):
    length = len_ref[0]
    count = with_level_5(count_ref[...], got5_ref[:, 2 * WIDTH :], 0)
    inverse = 1.0 / jnp.maximum(count, 1.0)
    count_t = jnp.concatenate([count[:T].T[:1], count[T:].T[:1]], axis=1)
    token_live = lax.broadcasted_iota(jnp.int32, (1, T), 1) < length
    live = jnp.concatenate([token_live.astype(jnp.float32), count_t], axis=1) > 0.0
    row_live = lax.broadcasted_iota(jnp.int32, (T, 1), 0) < length
    inverse_5 = inverse[5 * COARSE : 6 * COARSE]
    for j in range(KV):
        cols = slice(j * D, (j + 1) * D)
        vcols = slice((KV + j) * D, (KV + j + 1) * D)
        keys = with_level_5(keys_ref[:, cols], (got5_ref[:, cols] * inverse_5).astype(jnp.bfloat16), T)
        values = with_level_5(values_ref[:, cols], (got5_ref[:, vcols] * inverse_5).astype(jnp.bfloat16), T)
        key_grads = jnp.zeros((KEYS, D), jnp.float32)
        value_grads = jnp.zeros((KEYS, D), jnp.float32)
        for first in range(j * GROUP, (j + 1) * GROUP, BATCH):
            heads = range(first, first + BATCH)
            query = jnp.concatenate([q_ref[:, h * D : (h + 1) * D] for h in heads], axis=0)
            grad = jnp.concatenate([g_ref[:, h * D : (h + 1) * D] for h in heads], axis=0)
            scores = dot(query, keys, NT) * SCALE + bias_ref[first : first + BATCH].reshape(BATCH * T, KEYS)
            scores = jnp.where(live, scores, -jnp.inf)
            weights = jnp.exp(scores - jnp.max(scores, axis=1, keepdims=True))
            probs = weights * (1.0 / jnp.sum(weights, axis=1, keepdims=True))
            probs_b = probs.astype(jnp.bfloat16)
            attended = dot(probs_b, values)
            dprobs = dot(grad, values, NT)
            dscores = probs * (dprobs - jnp.sum(probs * dprobs, axis=1, keepdims=True))
            ds_ref[first : first + BATCH] = dscores.reshape(BATCH, T, KEYS)
            dscores_b = dscores.astype(jnp.bfloat16)
            grad_query = dot(dscores_b, keys) * SCALE
            for n, h in enumerate(heads):
                rows = slice(n * T, (n + 1) * T)
                out_ref[:, h * D : (h + 1) * D] = jnp.where(row_live, attended[rows], 0.0).astype(jnp.bfloat16)
                gq_ref[:, h * D : (h + 1) * D] = grad_query[rows].astype(jnp.bfloat16)
            key_grads = key_grads + dot(dscores_b, query, TN)
            value_grads = value_grads + dot(probs_b, grad, TN)
        key_grads = key_grads * SCALE
        own_ref[:, cols] = key_grads[:T]
        own_ref[:, vcols] = value_grads[:T]
        coarse_ref[:, cols] = key_grads[T:] * inverse
        coarse_ref[:, vcols] = value_grads[T:] * inverse


def weight_kernel(
    line_ref, slot_ref, ds_ref, phase_ref, out_ref, gq_ref, w_ref, out_hbm, gq_hbm, acc_ref, sems
):
    copies = fetch([(out_ref, out_hbm), (gq_ref, gq_hbm)], sems)
    acc_ref[...] = jnp.zeros_like(acc_ref)

    def operands(rows):
        phase = phase_ref[rows, :]
        parts = [ds_ref[h, rows, :] for h in range(HEADS)]
        parts = jnp.concatenate(parts + [p * phase for p in parts], axis=0)
        high = parts.astype(jnp.bfloat16)
        low = (parts - high.astype(jnp.float32)).astype(jnp.bfloat16)
        active = jnp.where(by_units(line_ref, phase) > 0.0, 1.0, 0.0).astype(jnp.bfloat16)
        return jnp.concatenate([high, low], axis=0), active

    def body(i, carry):
        first = pl.multiple_of(i * 2 * SUB, 2 * SUB)
        groups = [operands(pl.ds(first + n * SUB, SUB)) for n in range(2)]
        both, active = (jnp.concatenate(side, axis=1) for side in zip(*groups))
        acc_ref[...] += dot(both, active, NT)
        return carry

    lax.fori_loop(0, T // SUB // 2, body, 0, unroll=UNROLL)
    acc = acc_ref[...]
    rows = 2 * HEADS * SUB
    acc = acc[:rows] + acc[rows:]
    sub_row = lax.broadcasted_iota(jnp.int32, acc.shape, 0) % SUB
    sub_col = lax.broadcasted_iota(jnp.int32, acc.shape, 1) % SUB
    acc = jnp.where(sub_row == sub_col, acc, 0.0)
    acc = acc.reshape(2 * HEADS, SUB, HIDDEN * SUB).sum(axis=1)
    unit = lax.broadcasted_iota(jnp.int32, (HIDDEN * SUB, D), 0) // SUB
    lane = lax.broadcasted_iota(jnp.int32, (HIDDEN * SUB, D), 1) % HIDDEN
    sums = exact_dot(acc, jnp.where(unit == lane, 1.0, 0.0))
    w_ref[...] = slot_ref[1] * sums[:HEADS] + slot_ref[0] * sums[HEADS:]
    for copy in copies:
        copy.wait()


def chosen(rows, parts):
    sizes = [value.shape[0] for value, _ in parts]
    depth = -(-sum(sizes) // 16) * 16
    row = lax.broadcasted_iota(jnp.int32, (rows, 1), 0)
    col = twice(rows, depth)
    pick, first = col < 0, 0
    for size, (_, name) in zip(sizes, parts):
        pick = pick | (col == name(row, first))
        first += size
    value = [value for value, _ in parts]
    if first < depth:
        value.append(jnp.zeros((depth - first, value[0].shape[1]), jnp.float32))
    return picked(pick, jnp.concatenate(value, axis=0))


def twice(rows, depth):
    col = lax.broadcasted_iota(jnp.int32, (rows, 2 * depth), 1)
    return jnp.where(col < depth, col, col - depth)


def picked(pick, value):
    high = value.astype(jnp.bfloat16)
    low = (value - high.astype(jnp.float32)).astype(jnp.bfloat16)
    return dot(jnp.where(pick, 1.0, 0.0).astype(jnp.bfloat16), jnp.concatenate([high, low], axis=0))


def level_parts(ctx, level, coarse_ref):
    quarter = (ctx >> level) & 3

    def near(i, first):
        return jnp.where(i >> 5 == quarter ^ 1, (i & 31) + first, -1)

    def far(i, first):
        return jnp.where(i >> 6 != quarter >> 1, ((i & 63) >> 1) + first, -1)

    return [
        (coarse_ref[level * COARSE : (level + 1) * COARSE, :], near),
        (coarse_ref[(level + 1) * COARSE : (level + 2) * COARSE, :], far),
    ]


def half_of(ctx, level, shift):
    return lambda i, first: first + ((ctx >> level) & 1) * (COARSE // 2) + (i >> shift)


def every(shift):
    return lambda i, first: first + (i >> shift)


def sibling_rows(ctx, level, coarse_ref, came_ref):
    return chosen(
        COARSE,
        [
            (coarse_ref[level * COARSE : (level + 1) * COARSE, :], every(0)),
            (came_ref[...], half_of(ctx ^ (1 << level), level, 1)),
        ],
    )


def fill(payload_ref, first, rows, weights):
    for n in range(SIDE):
        payload_ref[n ^ first, :, : 2 * WIDTH] = rows[n * CHUNK : (n + 1) * CHUNK]
        payload_ref[n ^ first, :, 2 * WIDTH :] = weights


def away_kernel(place_ref, w_ref, coarse_ref, came5_ref, away_ref, send_ref):
    ctx = place_ref[0]
    fill(away_ref, FIRST["away"], chosen(SIDE * CHUNK, level_parts(ctx, 6, coarse_ref)), w_ref[...])
    send_ref[...] = sibling_rows(ctx, 4, coarse_ref, came5_ref)


def summed(ref):
    return sum(ref[n] + ref[n + SIDE // 2] for n in range(SIDE // 2))


def base_kernel(place_ref, came5_ref, came1_ref, coarse_ref, base_ref, send_ref):
    ctx = place_ref[0]
    parts = level_parts(ctx, 2, coarse_ref) + [(came5_ref[...], half_of(ctx, 4, 3))]
    base_ref[...] = chosen(SIDE * CHUNK, parts)
    send_ref[...] = sibling_rows(ctx, 0, coarse_ref, came1_ref)


def return_kernel(place_ref, away_ref, came4_ref, base_ref, near_ref):
    ctx = place_ref[0]
    away = summed(away_ref)
    rows = base_ref[...] + chosen(SIDE * CHUNK, [(came4_ref[...], every(2)), (away[:, : 2 * WIDTH], every(4))])
    fill(near_ref, FIRST["near"] ^ (((ctx >> 4) & 1) * 8), rows, away[:, 2 * WIDTH :])


def own_kernel(place_ref, own_ref, came1_ref, came0_ref, out_ref):
    parts = [(came1_ref[...], half_of(place_ref[0], 0, 3)), (came0_ref[...], every(2))]
    out_ref[...] = own_ref[...] + chosen(T, parts)


def final_kernel(len_ref, near_ref, own_ref, gk_ref, gv_ref):
    near = sum(near_ref[n, :, : 2 * WIDTH] for n in range(SIDE))
    live = lax.broadcasted_iota(jnp.int32, (T, 1), 0) < len_ref[0]
    grad = jnp.where(live, own_ref[...] + chosen(T, [(near, every(4))]), 0.0)
    gk_ref[...] = grad[:, :WIDTH].astype(jnp.bfloat16)
    gv_ref[...] = grad[:, WIDTH:].astype(jnp.bfloat16)


def outputs_kernel(mine_ref, got_ref, w1_ref, b1_ref, w2_ref):
    total = mine_ref[...] + got_ref[...]
    for core in range(2):
        w2_ref[core * HEADS : (core + 1) * HEADS, :] = total[:, core * HIDDEN : (core + 1) * HIDDEN]
    sums = jnp.sum(total, axis=0, keepdims=True)
    w1_ref[...] = sums[:, 2 * HIDDEN : 3 * HIDDEN]
    b1_ref[...] = sums[:, 3 * HIDDEN :]


def merge_kernel(place_ref, own_ref, got_ref, out_ref):
    row = lax.broadcasted_iota(jnp.int32, (COARSE, 1), 0)
    col = twice(COARSE, 2 * COARSE)
    upper = (place_ref[0] >> 4) & 1
    pick = (row & 15 == (col & 31) >> 1) & (row >> 4 == (col >> 5) ^ upper)
    out_ref[...] = picked(pick, jnp.concatenate([own_ref[...], got_ref[...]], axis=0))


def merge(own, got, upper):
    first = jnp.where(upper, got, own)
    second = jnp.where(upper, own, got)
    return jnp.concatenate([first, second], 0).reshape(COARSE, 2, -1).sum(1)


def in_hbm(value):
    return pltpu.with_memory_space_constraint(value, pltpu.HBM)


def swap_groups(value, groups):
    return lax.all_to_all(value, "ctx", 0, 0, axis_index_groups=groups)


def shards(queries, keys, values, lengths, fire_w1, fire_b1, fire_w2, grad_out):
    f32, bf16 = jnp.float32, jnp.bfloat16
    shape = jax.ShapeDtypeStruct
    ctx = lax.axis_index("ctx")
    mp = lax.axis_index("mp")
    place = jnp.stack([ctx, mp])
    bit = [(ctx >> k) & 1 == 1 for k in range(LEVELS)]
    blocks = range(SIDE)
    def low_groups(first, odd=0):
        return [[high * SIDE + (low ^ first ^ (odd * (high % 2))) for low in blocks] for high in blocks]

    def high_groups(first):
        order = [high ^ first for high in blocks]
        return [[high * SIDE + (low ^ (8 * (high % 2))) for high in order] for low in blocks]

    payload = shape((SIDE, CHUNK, 2 * WIDTH + D), f32)
    sums = shape((COARSE, 2 * WIDTH + D), f32)
    rows = shape((COARSE, 2 * WIDTH), f32)
    dma = pltpu.SemaphoreType.DMA
    fine, wide = pl.pallas_call(
        leaf_kernel,
        out_shape=(rows, payload),
        in_specs=[SMEM, HBM, HBM],
        out_specs=(VMEM, VMEM),
        scratch_shapes=[pltpu.VMEM((T, WIDTH), bf16)] * 2 + [dma((2,))],
        compiler_params=SMALL,
        name="leaf",
    )(lengths, in_hbm(keys), in_hbm(values))
    low = swap_groups(wide, low_groups(FIRST["low"])).reshape(SIDE * CHUNK, -1)
    got0 = exchange(fine, 0)
    own1 = merge(fine, got0, bit[0])
    wide_tokens, tokens = shape((T, HEADS * D), bf16), shape((T, WIDTH), bf16)
    bias, phase, line, slot = pl.pallas_call(
        bias_kernel,
        out_shape=(
            shape((HEADS, T, KEYS), f32),
            shape((T, KEYS), f32),
            shape((2, HIDDEN * SUB, D), f32),
            shape((2, HEADS, D), f32),
        ),
        in_specs=[SMEM] + [HBM] * 3 + [ANY],
        out_specs=(VMEM,) * 4,
        scratch_shapes=[
            pltpu.VMEM((1, HIDDEN), f32),
            pltpu.VMEM((1, HIDDEN), f32),
            pltpu.VMEM((2 * HEADS, HIDDEN), f32),
            dma((3,)),
        ],
        compiler_params=SMALL,
        cost_estimate=pl.CostEstimate(flops=600_000_000, bytes_accessed=2_000_000, transcendentals=50_000),
        name="bias",
    )(place, *map(in_hbm, (fire_w1.reshape(1, -1), fire_b1.reshape(1, -1), fire_w2.T)), fine)
    own4, wide4 = pl.pallas_call(
        middle_kernel,
        out_shape=(sums, payload),
        in_specs=[VMEM, ANY, ANY],
        out_specs=(VMEM, VMEM),
        compiler_params=SMALL,
        name="middle",
    )(low, slot, own1)
    high = swap_groups(wide4, high_groups(FIRST["high"])).reshape(SIDE * CHUNK, -1)
    got4 = exchange(own4, 4)
    got1 = exchange(jnp.pad(own1, ((0, 0), (0, D))), 1)
    own5 = pl.pallas_call(
        merge_kernel,
        out_shape=sums,
        in_specs=[SMEM, VMEM, VMEM],
        out_specs=VMEM,
        compiler_params=SMALL,
        name="merge",
    )(place, own4, got4)
    got5 = exchange(own5, 5)

    both = shape((KEYS, WIDTH), bf16)
    gathered = pl.pallas_call(
        gather_kernel,
        out_shape=(wide_tokens, wide_tokens, both, both, shape((LEVELS * COARSE, D), f32)),
        in_specs=[SMEM, SMEM] + [HBM] * 4 + [VMEM] * 5 + [ANY],
        out_specs=(VMEM,) * 5,
        scratch_shapes=[pltpu.VMEM((T, WIDTH), bf16)] * 2
        + [pltpu.VMEM((LEVELS * COARSE, 2 * WIDTH + D), f32), dma((4,))],
        compiler_params=SMALL,
        cost_estimate=pl.CostEstimate(flops=300_000_000, bytes_accessed=2_000_000, transcendentals=0),
        name="gather",
    )(place, lengths, *map(in_hbm, (queries, keys, values, grad_out)), got0, got1, low, got4, high, own5)
    attended, grad_q, own_grad, coarse, dscores = pl.pallas_call(
        main_kernel,
        out_shape=(
            wide_tokens,
            wide_tokens,
            shape((T, 2 * WIDTH), f32),
            shape((LEVELS * COARSE, 2 * WIDTH), f32),
            shape((HEADS, T, KEYS), f32),
        ),
        in_specs=[SMEM] + [VMEM] * 7,
        out_specs=(VMEM,) * 5,
        compiler_params=SMALL,
        name="attention",
    )(lengths, *gathered, got5, bias)

    came5 = exchange(coarse[5 * COARSE : 6 * COARSE], 5)
    w_part, attended, grad_q = pl.pallas_call(
        weight_kernel,
        out_shape=(shape((HEADS, D), f32), wide_tokens, wide_tokens),
        in_specs=[VMEM] * 6,
        out_specs=(VMEM, HBM, HBM),
        scratch_shapes=[pltpu.VMEM((4 * HEADS * SUB, HIDDEN * SUB), f32), dma((2,))],
        compiler_params=SMALL,
        cost_estimate=pl.CostEstimate(flops=900_000_000, bytes_accessed=2_000_000, transcendentals=0),
        name="weights",
    )(line, slot, dscores, phase, attended, grad_q)
    away, send4 = pl.pallas_call(
        away_kernel,
        out_shape=(payload, rows),
        in_specs=[SMEM] + [VMEM] * 3,
        out_specs=(VMEM, VMEM),
        compiler_params=SMALL,
        name="away",
    )(place, w_part, coarse, came5)
    away = swap_groups(away, high_groups(FIRST["away"]))
    came4 = exchange(send4, 4)
    came1 = exchange(coarse[COARSE : 2 * COARSE], 1)
    base, send0 = pl.pallas_call(
        base_kernel,
        out_shape=(shape((T, 2 * WIDTH), f32), rows),
        in_specs=[SMEM] + [VMEM] * 3,
        out_specs=(VMEM, VMEM),
        compiler_params=SMALL,
        cost_estimate=pl.CostEstimate(flops=300_000_000, bytes_accessed=1_000_000, transcendentals=0),
        name="base",
    )(place, came5, came1, coarse)
    near = pl.pallas_call(
        return_kernel,
        out_shape=payload,
        in_specs=[SMEM] + [VMEM] * 3,
        out_specs=VMEM,
        compiler_params=SMALL,
        name="return",
    )(place, away, came4, base)
    near = swap_groups(near, low_groups(FIRST["near"], 8))
    came0 = exchange(send0, 0)
    own_grad = pl.pallas_call(
        own_kernel,
        out_shape=shape((T, 2 * WIDTH), f32),
        in_specs=[SMEM] + [VMEM] * 3,
        out_specs=VMEM,
        compiler_params=SMALL,
        cost_estimate=pl.CostEstimate(flops=300_000_000, bytes_accessed=1_000_000, transcendentals=0),
        name="own",
    )(place, own_grad, came1, came0)
    near, own_grad = lax.optimization_barrier((near, own_grad))
    w_all = near[:, :, 2 * WIDTH :]
    w_all = (w_all[: SIDE // 2] + w_all[SIDE // 2 :]).sum(0)
    w_other = lax.ppermute(w_all, "mp", [(0, 1), (1, 0)])
    grad_k, grad_v = pl.pallas_call(
        final_kernel,
        out_shape=(tokens, tokens),
        in_specs=[SMEM] + [VMEM] * 2,
        out_specs=(VMEM, VMEM),
        compiler_params=SMALL,
        name="final",
    )(lengths, near, own_grad)
    grad_w1, grad_b1, grad_w2 = pl.pallas_call(
        outputs_kernel,
        out_shape=(shape((1, HIDDEN), f32), shape((1, HIDDEN), f32), shape((2 * HEADS, HIDDEN), f32)),
        in_specs=[VMEM] * 2,
        out_specs=(VMEM,) * 3,
        compiler_params=SMALL,
        name="outputs",
    )(w_all, w_other)
    grad_w1, grad_b1, grad_w2 = grad_w1.reshape(-1), grad_b1.reshape(-1), grad_w2.T
    return (attended, grad_q, grad_k, grad_v, grad_w1, grad_b1, grad_w2)


def solution(mesh):
    split = P("ctx", "mp")
    return jax.shard_map(
        shards,
        mesh=mesh,
        in_specs=(split, split, split, P("ctx"), P(), P(), P(), split),
        out_specs=(split, split, split, split, P(), P(), P()),
        check_vma=False,
    )
```

```python
import functools

import jax
import jax.numpy as jnp
from jax import lax
from jax.experimental import pallas as pl
from jax.experimental.pallas import tpu as pltpu
from jax.sharding import PartitionSpec as P

D = 128
COARSE = 32
T = 128
LEVELS = 8
KEYS = T + LEVELS * COARSE
HIDDEN = 32
HEADS = 8
KV = 2
GROUP = HEADS // KV
SUB = 8
UNROLL = 4
CHUNK = 8
SIDE = 16
FIRST = {"low": 12, "high": 14, "away": 3, "near": 2}
WIDTH = KV * D
LEVEL_TOKENS = float(T * 2**LEVELS)
SCALE = D ** (-0.5)
MASKS = (1, 2, 6, 8, 24, 32, 64, 192)
NT = (((1,), (1,)), ((), ()))
TN = (((0,), (0,)), ((), ()))
VMEM = pl.BlockSpec(memory_space=pltpu.VMEM)
SMEM = pl.BlockSpec(memory_space=pltpu.SMEM)
HBM = pl.BlockSpec(memory_space=pltpu.HBM)
ANY = pl.BlockSpec(memory_space=pl.ANY)
SMALL = pltpu.CompilerParams(vmem_limit_bytes=12 * 2**20)
LARGE = pltpu.CompilerParams(vmem_limit_bytes=24 * 2**20)


def dot(a, b, dims=(((1,), (0,)), ((), ()))):
    return lax.dot_general(a, b, dims, preferred_element_type=jnp.float32)


def shifted(value, mask):
    return lax.ppermute(value, "ctx", [(i, i ^ mask) for i in range(lax.axis_size("ctx"))])


def exchange(value, level):
    return shifted(value, MASKS[level])


def fetch(pairs, sems):
    copies = [pltpu.make_async_copy(src, dst, sems.at[n]) for n, (src, dst) in enumerate(pairs)]
    for copy in copies:
        copy.start()
    return copies


def leaf_kernel(len_ref, k_hbm, v_hbm, fine_ref, wide_ref, k_ref, v_ref, sems):
    copies = fetch([(k_hbm, k_ref), (v_hbm, v_ref)], sems)
    row = lax.broadcasted_iota(jnp.int32, (COARSE + CHUNK, T), 0)
    tok = lax.broadcasted_iota(jnp.int32, (COARSE + CHUNK, T), 1)
    run = jnp.where(row < COARSE, tok // (T // COARSE), tok // (T // CHUNK) + COARSE)
    member = jnp.where((run == row) & (tok < len_ref[0]), 1.0, 0.0)
    member_b = member.astype(jnp.bfloat16)
    count = jnp.broadcast_to(jnp.sum(member, axis=1, keepdims=True), (COARSE + CHUNK, D))
    for copy in copies:
        copy.wait()
    rows = jnp.concatenate([dot(member_b, k_ref[...]), dot(member_b, v_ref[...]), count], axis=1)
    fine_ref[...] = rows[:COARSE, : 2 * WIDTH]
    for n in range(SIDE):
        wide_ref[n] = rows[COARSE:]


def exact_dot(a, b, dims=(((1,), (0,)), ((), ()))):
    return lax.dot_general(a, b, dims, precision=lax.Precision.HIGHEST, preferred_element_type=jnp.float32)


def unit_weights(core, w2_ref, rows, columns, by_row, by_column):
    shape = (rows, 2 * HEADS)
    head = lax.broadcasted_iota(jnp.int32, shape, 0) // by_row + core * HEADS
    pick = jnp.where(lax.broadcasted_iota(jnp.int32, shape, 1) == head, 1.0, 0.0)
    return exact_dot(exact_dot(pick, w2_ref[...]), unit_columns(columns, by_column))


def unit_columns(columns, by):
    unit = lax.broadcasted_iota(jnp.int32, (HIDDEN, columns), 0)
    column = lax.broadcasted_iota(jnp.int32, (HIDDEN, columns), 1)
    return jnp.where(column // by % HIDDEN == unit, 1.0, 0.0)


def bias_kernel(
    place_ref, w1_hbm, b1_hbm, w2_hbm, after_ref, bias_ref, phase_ref, line_ref, slot_ref, w1_ref, b1_ref, w2_ref, sems
):
    copies = fetch([(w1_hbm, w1_ref), (b1_hbm, b1_ref), (w2_hbm, w2_ref)], sems)
    ctx, core = place_ref[0], place_ref[1]
    col = lax.broadcasted_iota(jnp.int32, (1, KEYS), 1)
    level = (col - T) // COARSE
    pos = col.astype(jnp.float32)
    for k in range(LEVELS):
        run = 2**k * T // COARSE
        start = ((ctx >> k) ^ 1) * 2**k * T - ctx * T
        inside = (col - T - k * COARSE) * run
        here = (start + inside).astype(jnp.float32) + (run - 1) / 2.0
        pos = jnp.where((col >= T) & (level == k), here, pos)
    top = jnp.log1p(jnp.full((1, KEYS), LEVEL_TOKENS, jnp.float32))
    row = lax.broadcasted_iota(jnp.int32, (T, KEYS), 0).astype(jnp.float32)
    phase_ref[...] = jnp.log1p(jnp.abs(row - pos)) / top
    for copy in copies:
        copy.wait()
    lane = lax.broadcasted_iota(jnp.int32, (HEADS, D), 1) // HIDDEN
    w2 = unit_weights(core, w2_ref, HEADS, D, 1, 1)
    spread = unit_columns(HIDDEN * SUB, SUB)
    for n, ref in enumerate((w1_ref, b1_ref)):
        line = jnp.broadcast_to(ref[...], (D, HIDDEN))
        line_ref[n] = exact_dot(spread, line, (((0,), (1,)), ((), ())))
        slot_ref[n] = jnp.where(lane == core, exact_dot(ref[...], unit_columns(D, 1)), jnp.where(lane == 2 + n, w2, 0.0))
    weight = unit_weights(core, w2_ref, HEADS * SUB, HIDDEN * SUB, SUB, SUB)
    row = lax.broadcasted_iota(jnp.int32, weight.shape, 0)
    column = lax.broadcasted_iota(jnp.int32, weight.shape, 1)
    weight = jnp.where(row % SUB == column % SUB, weight, 0.0)
    weight_high = weight.astype(jnp.bfloat16)
    weight_low = (weight - weight_high.astype(jnp.float32)).astype(jnp.bfloat16)
    weight_both = jnp.concatenate([weight_high, weight_low], axis=0)

    def body(i, carry):
        rows = pl.ds(pl.multiple_of(i * SUB, SUB), SUB)
        hidden = jnp.maximum(by_units(line_ref, phase_ref[rows, :]), 0.0)
        high = hidden.astype(jnp.bfloat16)
        low = (hidden - high.astype(jnp.float32)).astype(jnp.bfloat16)
        with_high = dot(weight_both, high)
        bias = with_high[: HEADS * SUB] + with_high[HEADS * SUB :] + dot(weight_high, low)
        for h in range(HEADS):
            bias_ref[h, rows, :] = bias[h * SUB : (h + 1) * SUB]
        return carry

    lax.fori_loop(0, T // SUB, body, 0, unroll=UNROLL)


def by_units(line_ref, phase):
    slope = line_ref[0].reshape(HIDDEN, SUB, D)
    offset = line_ref[1].reshape(HIDDEN, SUB, D)
    tiles = [phase[None, :, n * D : (n + 1) * D] * slope + offset for n in range(KEYS // D)]
    return jnp.concatenate(tiles, axis=2).reshape(HIDDEN * SUB, KEYS)


def pooled(rows, by):
    row = lax.broadcasted_iota(jnp.int32, (rows.shape[0] // by, 1), 0)
    return picked(twice(rows.shape[0] // by, rows.shape[0]) // by == row, rows)


def middle_kernel(low_ref, after_bias_ref, after_merge_ref, own_ref, wide_ref):
    row = lax.broadcasted_iota(jnp.int32, (COARSE + CHUNK, 1), 0)
    col = twice(COARSE + CHUNK, SIDE * CHUNK)
    member = (col >> 3) ^ FIRST["low"]
    run = jnp.where(row < COARSE, (member << 1) + ((col & 7) >> 2), (member >> 1) + COARSE)
    rows = picked(run == row, low_ref[...])
    own_ref[...] = rows[:COARSE]
    for n in range(SIDE):
        wide_ref[n] = rows[COARSE:]


def gather_kernel(
    place_ref, len_ref, q_hbm, k_hbm, v_hbm, g_hbm, got0_ref, got1_ref, low_ref, got4_ref, high_ref, after_ref,
    q_ref, g_ref, keys_ref, values_ref, count_ref, k_ref, v_ref, sib_ref, sems,
):
    copies = fetch([(k_hbm, k_ref), (q_hbm, q_ref), (v_hbm, v_ref), (g_hbm, g_ref)], sems)
    ctx = place_ref[0]
    for level, ref in ((0, got0_ref), (1, got1_ref), (4, got4_ref), (5, got4_ref)):
        sib_ref[level * COARSE : (level + 1) * COARSE, : ref.shape[1]] = ref[...]
    row = lax.broadcasted_iota(jnp.int32, (2 * COARSE, 1), 0)
    col = twice(2 * COARSE, SIDE * CHUNK)
    for level, ref, first in ((2, low_ref, FIRST["low"]), (6, high_ref, FIRST["high"])):
        quarter = ((ctx >> level) & 3) ^ 1
        half = ((ctx >> level + 1) & 1) ^ 1
        member = col >> 3 if level == 2 else side_member(col >> 3)
        place = ((member ^ first) << 3) + (col & 7)
        want = jnp.where(row < COARSE, quarter * COARSE + row, (half - 1) * COARSE + row)
        rows = picked(jnp.where(row < COARSE, place, place >> 1) == want, ref[...])
        sib_ref[level * COARSE : (level + 2) * COARSE, :] = rows
    group = (((ctx >> 1) & 7) ^ 1) * 2
    blocks = ((0, COARSE, (ctx & 15) ^ 1), (COARSE, COARSE // 2, group), (COARSE * 3 // 2, COARSE // 2, group + 1))
    for first, rows, block in blocks:
        block = low_ref[pl.ds(pl.multiple_of((block ^ FIRST["low"]) * CHUNK, CHUNK), CHUNK), 2 * WIDTH :]
        run = T // rows
        before = lax.broadcasted_iota(jnp.int32, (rows, D), 0) * run
        here = jnp.sum(block, axis=0, keepdims=True) - before.astype(jnp.float32)
        sib_ref[first : first + rows, 2 * WIDTH :] = jnp.clip(here, 0.0, float(run))
    count = sib_ref[:, 2 * WIDTH :]
    count_ref[...] = count
    inverse = 1.0 / jnp.maximum(count, 1.0)
    for n in range(2 * KV):
        cols = slice(n * D, (n + 1) * D)
        ref = keys_ref if n < KV else values_ref
        ref[T:, n % KV * D : (n % KV + 1) * D] = (sib_ref[:, cols] * inverse).astype(jnp.bfloat16)
    for copy in copies:
        copy.wait()
    keys_ref[:T, :] = k_ref[...]
    values_ref[:T, :] = v_ref[...]
    row_live = lax.broadcasted_iota(jnp.int32, (T, 1), 0) < len_ref[0]
    g_ref[...] = jnp.where(row_live, g_ref[...], jnp.zeros_like(g_ref))


def with_level_5(rows, level, first):
    return jnp.concatenate([rows[: first + 5 * COARSE], level, rows[first + 6 * COARSE :]], axis=0)


def main_kernel(
    len_ref, q_ref, g_ref, keys_ref, values_ref, count_ref, got5_ref, bias_ref,
    out_ref, gq_ref, own_ref, coarse_ref, ds_ref,
):
    length = len_ref[0]
    count = with_level_5(count_ref[...], got5_ref[:, 2 * WIDTH :], 0)
    inverse = 1.0 / jnp.maximum(count, 1.0)
    count_t = jnp.concatenate([count[:T].T[:1], count[T:].T[:1]], axis=1)
    token_live = lax.broadcasted_iota(jnp.int32, (1, T), 1) < length
    live = jnp.concatenate([token_live.astype(jnp.float32), count_t], axis=1) > 0.0
    row_live = lax.broadcasted_iota(jnp.int32, (T, 1), 0) < length
    inverse_5 = inverse[5 * COARSE : 6 * COARSE]
    def stacked(ref):
        return jnp.concatenate([ref[:, h * D : (h + 1) * D] for h in range(HEADS)], axis=0)

    def per_group(*pairs, dims=(((1,), (0,)), ((), ()))):
        return jnp.concatenate([dot(a, b, dims) for a, b in pairs], axis=0)

    span = GROUP * T
    lanes = [slice(j * D, (j + 1) * D) for j in range(KV)]
    value_lanes = [slice((KV + j) * D, (KV + j + 1) * D) for j in range(KV)]
    keys = [with_level_5(keys_ref[:, at], (got5_ref[:, at] * inverse_5).astype(jnp.bfloat16), T) for at in lanes]
    values = [
        with_level_5(values_ref[:, at], (got5_ref[:, wide] * inverse_5).astype(jnp.bfloat16), T)
        for at, wide in zip(lanes, value_lanes)
    ]
    query, grad = stacked(q_ref), stacked(g_ref)
    groups = [slice(j * span, (j + 1) * span) for j in range(KV)]
    scores = per_group(*[(query[at], k) for at, k in zip(groups, keys)], dims=NT) * SCALE
    scores = jnp.where(live, scores + bias_ref[...].reshape(HEADS * T, KEYS), -jnp.inf)
    weights = jnp.exp(scores - jnp.max(scores, axis=1, keepdims=True))
    probs = weights * (1.0 / jnp.sum(weights, axis=1, keepdims=True))
    probs_b = probs.astype(jnp.bfloat16)
    attended = per_group(*[(probs_b[at], v) for at, v in zip(groups, values)])
    dprobs = per_group(*[(grad[at], v) for at, v in zip(groups, values)], dims=NT)
    dscores = probs * (dprobs - jnp.sum(probs * dprobs, axis=1, keepdims=True))
    ds_ref[...] = dscores.reshape(HEADS, T, KEYS)
    dscores_b = dscores.astype(jnp.bfloat16)
    grad_query = per_group(*[(dscores_b[at], k) for at, k in zip(groups, keys)]) * SCALE
    for h in range(HEADS):
        rows = slice(h * T, (h + 1) * T)
        out_ref[:, h * D : (h + 1) * D] = jnp.where(row_live, attended[rows], 0.0).astype(jnp.bfloat16)
        gq_ref[:, h * D : (h + 1) * D] = grad_query[rows].astype(jnp.bfloat16)
    for at, cols, vcols in zip(groups, lanes, value_lanes):
        key_grads = dot(dscores_b[at], query[at], TN) * SCALE
        value_grads = dot(probs_b[at], grad[at], TN)
        own_ref[:, cols] = key_grads[:T]
        own_ref[:, vcols] = value_grads[:T]
        coarse_ref[:, cols] = key_grads[T:] * inverse
        coarse_ref[:, vcols] = value_grads[T:] * inverse


def weight_kernel(
    place_ref, line_ref, slot_ref, ds_ref, phase_ref, out_ref, gq_ref, coarse_ref,
    w_ref, rows_ref, out_hbm, gq_hbm, acc_ref, sems,
):
    copies = fetch([(out_ref, out_hbm), (gq_ref, gq_hbm)], sems)
    acc_ref[...] = jnp.zeros_like(acc_ref)

    def operands(rows):
        phase = phase_ref[rows, :]
        parts = [ds_ref[h, rows, :] for h in range(HEADS)]
        parts = jnp.concatenate(parts + [p * phase for p in parts], axis=0)
        high = parts.astype(jnp.bfloat16)
        low = (parts - high.astype(jnp.float32)).astype(jnp.bfloat16)
        active = jnp.where(by_units(line_ref, phase) > 0.0, 1.0, 0.0).astype(jnp.bfloat16)
        return jnp.concatenate([high, low], axis=0), active

    def body(i, carry):
        first = pl.multiple_of(i * 2 * SUB, 2 * SUB)
        groups = [operands(pl.ds(first + n * SUB, SUB)) for n in range(2)]
        both, active = (jnp.concatenate(side, axis=1) for side in zip(*groups))
        acc_ref[...] += dot(both, active, NT)
        return carry

    lax.fori_loop(0, T // SUB // 2, body, 0, unroll=UNROLL)
    acc = acc_ref[...]
    rows = 2 * HEADS * SUB
    acc = acc[:rows] + acc[rows:]
    sub_row = lax.broadcasted_iota(jnp.int32, acc.shape, 0) % SUB
    sub_col = lax.broadcasted_iota(jnp.int32, acc.shape, 1) % SUB
    acc = jnp.where(sub_row == sub_col, acc, 0.0)
    acc = acc.reshape(2 * HEADS, SUB, HIDDEN * SUB).sum(axis=1)
    unit = lax.broadcasted_iota(jnp.int32, (HIDDEN * SUB, D), 0) // SUB
    lane = lax.broadcasted_iota(jnp.int32, (HIDDEN * SUB, D), 1) % HIDDEN
    sums = exact_dot(acc, jnp.where(unit == lane, 1.0, 0.0))
    rows_ref[...] = chosen(SIDE * CHUNK, level_parts(place_ref[0], 6, coarse_ref))
    w_ref[...] = slot_ref[1] * sums[:HEADS] + slot_ref[0] * sums[HEADS:]
    for copy in copies:
        copy.wait()


def chosen(rows, parts):
    sizes = [value.shape[0] for value, _ in parts]
    depth = -(-sum(sizes) // 16) * 16
    row = lax.broadcasted_iota(jnp.int32, (rows, 1), 0)
    col = twice(rows, depth)
    pick, first = col < 0, 0
    for size, (_, name) in zip(sizes, parts):
        pick = pick | (col == name(row, first))
        first += size
    value = [value for value, _ in parts]
    if first < depth:
        value.append(jnp.zeros((depth - first, value[0].shape[1]), jnp.float32))
    return picked(pick, jnp.concatenate(value, axis=0))


def twice(rows, depth):
    col = lax.broadcasted_iota(jnp.int32, (rows, 2 * depth), 1)
    return jnp.where(col < depth, col, col - depth)


def picked(pick, value):
    high = value.astype(jnp.bfloat16)
    low = (value - high.astype(jnp.float32)).astype(jnp.bfloat16)
    return dot(jnp.where(pick, 1.0, 0.0).astype(jnp.bfloat16), jnp.concatenate([high, low], axis=0))


def level_parts(ctx, level, coarse_ref):
    quarter = (ctx >> level) & 3

    def near(i, first):
        return jnp.where(i >> 5 == quarter ^ 1, (i & 31) + first, -1)

    def far(i, first):
        return jnp.where(i >> 6 != quarter >> 1, ((i & 63) >> 1) + first, -1)

    return [
        (coarse_ref[level * COARSE : (level + 1) * COARSE, :], near),
        (coarse_ref[(level + 1) * COARSE : (level + 2) * COARSE, :], far),
    ]


def half_of(ctx, level, shift):
    return lambda i, first: first + ((ctx >> level) & 1) * (COARSE // 2) + (i >> shift)


def every(shift):
    return lambda i, first: first + (i >> shift)


def sibling_rows(ctx, level, coarse_ref, came_ref):
    return chosen(
        COARSE,
        [
            (coarse_ref[level * COARSE : (level + 1) * COARSE, :], every(0)),
            (came_ref[...], half_of(ctx ^ (1 << level), level, 1)),
        ],
    )


def side_place(member):
    return (member >> 1) | ((member & 1) << 3)


def side_member(place):
    return ((place & 7) << 1) | (place >> 3)


def fill(payload_ref, place_of, rows, weights):
    for n in range(SIDE):
        payload_ref[place_of(n), :, : 2 * WIDTH] = rows[n * CHUNK : (n + 1) * CHUNK]
        payload_ref[place_of(n), :, 2 * WIDTH :] = weights


def away_kernel(place_ref, w_ref, rows_ref, coarse_ref, came5_ref, away_ref, send_ref):
    ctx = place_ref[0]
    fill(away_ref, lambda n: side_place(n ^ FIRST["away"]), rows_ref[...], w_ref[...])
    send_ref[...] = sibling_rows(ctx, 4, coarse_ref, came5_ref)


def summed(ref):
    return sum(ref[n] + ref[n + SIDE // 2] for n in range(SIDE // 2))


def base_kernel(place_ref, came5_ref, came1_ref, coarse_ref, base_ref, send_ref):
    ctx = place_ref[0]
    parts = level_parts(ctx, 2, coarse_ref) + [(came5_ref[...], half_of(ctx, 4, 3))]
    base_ref[...] = chosen(SIDE * CHUNK, parts)
    send_ref[...] = sibling_rows(ctx, 0, coarse_ref, came1_ref)


def return_kernel(place_ref, away_ref, came4_ref, base_ref, near_ref):
    ctx = place_ref[0]
    away = summed(away_ref)
    rows = base_ref[...] + chosen(SIDE * CHUNK, [(came4_ref[...], every(2)), (away[:, : 2 * WIDTH], every(4))])
    fill(near_ref, lambda n: n ^ FIRST["near"] ^ (((ctx >> 4) & 1) * 8), rows, away[:, 2 * WIDTH :])


def own_kernel(place_ref, own_ref, came1_ref, came0_ref, out_ref):
    parts = [(came1_ref[...], half_of(place_ref[0], 0, 3)), (came0_ref[...], every(2))]
    out_ref[...] = own_ref[...] + chosen(T, parts)


def final_kernel(len_ref, near_ref, own_ref, gk_ref, gv_ref):
    near = sum(near_ref[n, :, : 2 * WIDTH] for n in range(SIDE))
    live = lax.broadcasted_iota(jnp.int32, (T, 1), 0) < len_ref[0]
    grad = jnp.where(live, own_ref[...] + chosen(T, [(near, every(4))]), 0.0)
    gk_ref[...] = grad[:, :WIDTH].astype(jnp.bfloat16)
    gv_ref[...] = grad[:, WIDTH:].astype(jnp.bfloat16)


def outputs_kernel(mine_ref, got_ref, w1_ref, b1_ref, w2_ref):
    total = mine_ref[...] + got_ref[...]
    for core in range(2):
        w2_ref[core * HEADS : (core + 1) * HEADS, :] = total[:, core * HIDDEN : (core + 1) * HIDDEN]
    sums = jnp.sum(total, axis=0, keepdims=True)
    w1_ref[...] = sums[:, 2 * HIDDEN : 3 * HIDDEN]
    b1_ref[...] = sums[:, 3 * HIDDEN :]


def merge_kernel(place_ref, own_ref, got_ref, out_ref):
    row = lax.broadcasted_iota(jnp.int32, (COARSE, 1), 0)
    col = twice(COARSE, 2 * COARSE)
    upper = (place_ref[0] >> 4) & 1
    pick = (row & 15 == (col & 31) >> 1) & (row >> 4 == (col >> 5) ^ upper)
    out_ref[...] = picked(pick, jnp.concatenate([own_ref[...], got_ref[...]], axis=0))


def merge(own, got, upper):
    first = jnp.where(upper, got, own)
    second = jnp.where(upper, own, got)
    return jnp.concatenate([first, second], 0).reshape(COARSE, 2, -1).sum(1)


def in_hbm(value):
    return pltpu.with_memory_space_constraint(value, pltpu.HBM)


def swap_groups(value, groups):
    return lax.all_to_all(value, "ctx", 0, 0, axis_index_groups=groups)


def shards(queries, keys, values, lengths, fire_w1, fire_b1, fire_w2, grad_out):
    f32, bf16 = jnp.float32, jnp.bfloat16
    shape = jax.ShapeDtypeStruct
    ctx = lax.axis_index("ctx")
    mp = lax.axis_index("mp")
    place = jnp.stack([ctx, mp])
    bit = [(ctx >> k) & 1 == 1 for k in range(LEVELS)]
    blocks = range(SIDE)
    def low_groups(first, odd=0):
        return [[high * SIDE + (low ^ first ^ (odd * (high % 2))) for low in blocks] for high in blocks]

    def high_groups(first):
        order = [side_member(place) ^ first for place in blocks]
        return [[high * SIDE + (low ^ (8 * (high % 2))) for high in order] for low in blocks]

    payload = shape((SIDE, CHUNK, 2 * WIDTH + D), f32)
    sums = shape((COARSE, 2 * WIDTH + D), f32)
    rows = shape((COARSE, 2 * WIDTH), f32)
    dma = pltpu.SemaphoreType.DMA
    fine, wide = pl.pallas_call(
        leaf_kernel,
        out_shape=(rows, payload),
        in_specs=[SMEM, HBM, HBM],
        out_specs=(VMEM, VMEM),
        scratch_shapes=[pltpu.VMEM((T, WIDTH), bf16)] * 2 + [dma((2,))],
        compiler_params=SMALL,
        name="leaf",
    )(lengths, in_hbm(keys), in_hbm(values))
    low = swap_groups(wide, low_groups(FIRST["low"])).reshape(SIDE * CHUNK, -1)
    got0 = exchange(fine, 0)
    own1 = merge(fine, got0, bit[0])
    wide_tokens, tokens = shape((T, HEADS * D), bf16), shape((T, WIDTH), bf16)
    bias, phase, line, slot = pl.pallas_call(
        bias_kernel,
        out_shape=(
            shape((HEADS, T, KEYS), f32),
            shape((T, KEYS), f32),
            shape((2, HIDDEN * SUB, D), f32),
            shape((2, HEADS, D), f32),
        ),
        in_specs=[SMEM] + [HBM] * 3 + [ANY],
        out_specs=(VMEM,) * 4,
        scratch_shapes=[
            pltpu.VMEM((1, HIDDEN), f32),
            pltpu.VMEM((1, HIDDEN), f32),
            pltpu.VMEM((2 * HEADS, HIDDEN), f32),
            dma((3,)),
        ],
        compiler_params=SMALL,
        cost_estimate=pl.CostEstimate(flops=600_000_000, bytes_accessed=2_000_000, transcendentals=50_000),
        name="bias",
    )(place, *map(in_hbm, (fire_w1.reshape(1, -1), fire_b1.reshape(1, -1), fire_w2.T)), fine)
    own4, wide4 = pl.pallas_call(
        middle_kernel,
        out_shape=(sums, payload),
        in_specs=[VMEM, ANY, ANY],
        out_specs=(VMEM, VMEM),
        compiler_params=SMALL,
        name="middle",
    )(low, slot, own1)
    high = swap_groups(wide4, high_groups(FIRST["high"])).reshape(SIDE * CHUNK, -1)
    got4 = exchange(own4, 4)
    got1 = exchange(jnp.pad(own1, ((0, 0), (0, D))), 1)
    own5 = pl.pallas_call(
        merge_kernel,
        out_shape=sums,
        in_specs=[SMEM, VMEM, VMEM],
        out_specs=VMEM,
        compiler_params=SMALL,
        name="merge",
    )(place, own4, got4)
    got5 = exchange(own5, 5)

    both = shape((KEYS, WIDTH), bf16)
    gathered = pl.pallas_call(
        gather_kernel,
        out_shape=(wide_tokens, wide_tokens, both, both, shape((LEVELS * COARSE, D), f32)),
        in_specs=[SMEM, SMEM] + [HBM] * 4 + [VMEM] * 5 + [ANY],
        out_specs=(VMEM,) * 5,
        scratch_shapes=[pltpu.VMEM((T, WIDTH), bf16)] * 2
        + [pltpu.VMEM((LEVELS * COARSE, 2 * WIDTH + D), f32), dma((4,))],
        compiler_params=SMALL,
        cost_estimate=pl.CostEstimate(flops=300_000_000, bytes_accessed=2_000_000, transcendentals=0),
        name="gather",
    )(place, lengths, *map(in_hbm, (queries, keys, values, grad_out)), got0, got1, low, got4, high, own5)
    attended, grad_q, own_grad, coarse, dscores = pl.pallas_call(
        main_kernel,
        out_shape=(
            wide_tokens,
            wide_tokens,
            shape((T, 2 * WIDTH), f32),
            shape((LEVELS * COARSE, 2 * WIDTH), f32),
            shape((HEADS, T, KEYS), f32),
        ),
        in_specs=[SMEM] + [VMEM] * 7,
        out_specs=(VMEM,) * 5,
        compiler_params=LARGE,
        name="attention",
    )(lengths, *gathered, got5, bias)

    came5 = exchange(coarse[5 * COARSE : 6 * COARSE], 5)
    w_part, away_rows, attended, grad_q = pl.pallas_call(
        weight_kernel,
        out_shape=(shape((HEADS, D), f32), shape((T, 2 * WIDTH), f32), wide_tokens, wide_tokens),
        in_specs=[SMEM] + [VMEM] * 7,
        out_specs=(VMEM, VMEM, HBM, HBM),
        scratch_shapes=[pltpu.VMEM((4 * HEADS * SUB, HIDDEN * SUB), f32), dma((2,))],
        compiler_params=SMALL,
        cost_estimate=pl.CostEstimate(flops=900_000_000, bytes_accessed=2_000_000, transcendentals=0),
        name="weights",
    )(place, line, slot, dscores, phase, attended, grad_q, coarse)
    away, send4 = pl.pallas_call(
        away_kernel,
        out_shape=(payload, rows),
        in_specs=[SMEM] + [VMEM] * 4,
        out_specs=(VMEM, VMEM),
        compiler_params=SMALL,
        name="away",
    )(place, w_part, away_rows, coarse, came5)
    away = swap_groups(away, high_groups(FIRST["away"]))
    came4 = exchange(send4, 4)
    came1 = exchange(coarse[COARSE : 2 * COARSE], 1)
    base, send0 = pl.pallas_call(
        base_kernel,
        out_shape=(shape((T, 2 * WIDTH), f32), rows),
        in_specs=[SMEM] + [VMEM] * 3,
        out_specs=(VMEM, VMEM),
        compiler_params=SMALL,
        cost_estimate=pl.CostEstimate(flops=300_000_000, bytes_accessed=1_000_000, transcendentals=0),
        name="base",
    )(place, came5, came1, coarse)
    near = pl.pallas_call(
        return_kernel,
        out_shape=payload,
        in_specs=[SMEM] + [VMEM] * 3,
        out_specs=VMEM,
        compiler_params=SMALL,
        name="return",
    )(place, away, came4, base)
    near = swap_groups(near, low_groups(FIRST["near"], 8))
    came0 = exchange(send0, 0)
    own_grad = pl.pallas_call(
        own_kernel,
        out_shape=shape((T, 2 * WIDTH), f32),
        in_specs=[SMEM] + [VMEM] * 3,
        out_specs=VMEM,
        compiler_params=SMALL,
        cost_estimate=pl.CostEstimate(flops=300_000_000, bytes_accessed=1_000_000, transcendentals=0),
        name="own",
    )(place, own_grad, came1, came0)
    near, own_grad = lax.optimization_barrier((near, own_grad))
    w_all = near[:, :, 2 * WIDTH :]
    w_all = (w_all[: SIDE // 2] + w_all[SIDE // 2 :]).sum(0)
    w_other = lax.ppermute(w_all, "mp", [(0, 1), (1, 0)])
    grad_k, grad_v = pl.pallas_call(
        final_kernel,
        out_shape=(tokens, tokens),
        in_specs=[SMEM] + [VMEM] * 2,
        out_specs=(VMEM, VMEM),
        compiler_params=SMALL,
        name="final",
    )(lengths, near, own_grad)
    grad_w1, grad_b1, grad_w2 = pl.pallas_call(
        outputs_kernel,
        out_shape=(shape((1, HIDDEN), f32), shape((1, HIDDEN), f32), shape((2 * HEADS, HIDDEN), f32)),
        in_specs=[VMEM] * 2,
        out_specs=(VMEM,) * 3,
        compiler_params=SMALL,
        name="outputs",
    )(w_all, w_other)
    grad_w1, grad_b1, grad_w2 = grad_w1.reshape(-1), grad_b1.reshape(-1), grad_w2.T
    return (attended, grad_q, grad_k, grad_v, grad_w1, grad_b1, grad_w2)


def solution(mesh):
    split = P("ctx", "mp")
    return jax.shard_map(
        shards,
        mesh=mesh,
        in_specs=(split, split, split, P("ctx"), P(), P(), P(), split),
        out_specs=(split, split, split, split, P(), P(), P()),
        check_vma=False,
    )
```

```python
import functools

import jax
import jax.numpy as jnp
from jax import lax
from jax.experimental import pallas as pl
from jax.experimental.pallas import tpu as pltpu
from jax.sharding import PartitionSpec as P

D = 128
COARSE = 32
T = 128
LEVELS = 8
KEYS = T + LEVELS * COARSE
HIDDEN = 32
HEADS = 8
KV = 2
GROUP = HEADS // KV
SUB = 8
UNROLL = 4
CHUNK = 8
SIDE = 16
FIRST = {"low": 12, "high": 14, "away": 3, "near": 3}
WIDTH = KV * D
LEVEL_TOKENS = float(T * 2**LEVELS)
SCALE = D ** (-0.5)
MASKS = (1, 2, 6, 8, 24, 32, 64, 192)
NT = (((1,), (1,)), ((), ()))
TN = (((0,), (0,)), ((), ()))
VMEM = pl.BlockSpec(memory_space=pltpu.VMEM)
SMEM = pl.BlockSpec(memory_space=pltpu.SMEM)
HBM = pl.BlockSpec(memory_space=pltpu.HBM)
ANY = pl.BlockSpec(memory_space=pl.ANY)
SMALL = pltpu.CompilerParams(vmem_limit_bytes=12 * 2**20)
LARGE = pltpu.CompilerParams(vmem_limit_bytes=24 * 2**20)


def dot(a, b, dims=(((1,), (0,)), ((), ()))):
    return lax.dot_general(a, b, dims, preferred_element_type=jnp.float32)


def shifted(value, mask):
    return lax.ppermute(value, "ctx", [(i, i ^ mask) for i in range(lax.axis_size("ctx"))])


def exchange(value, level):
    return shifted(value, MASKS[level])


def fetch(pairs, sems):
    copies = [pltpu.make_async_copy(src, dst, sems.at[n]) for n, (src, dst) in enumerate(pairs)]
    for copy in copies:
        copy.start()
    return copies


def leaf_kernel(len_ref, k_hbm, v_hbm, fine_ref, wide_ref, k_ref, v_ref, sems):
    copies = fetch([(k_hbm, k_ref), (v_hbm, v_ref)], sems)
    row = lax.broadcasted_iota(jnp.int32, (COARSE + CHUNK, T), 0)
    tok = lax.broadcasted_iota(jnp.int32, (COARSE + CHUNK, T), 1)
    run = jnp.where(row < COARSE, tok // (T // COARSE), tok // (T // CHUNK) + COARSE)
    member = jnp.where((run == row) & (tok < len_ref[0]), 1.0, 0.0)
    member_b = member.astype(jnp.bfloat16)
    count = jnp.broadcast_to(jnp.sum(member, axis=1, keepdims=True), (COARSE + CHUNK, D))
    for copy in copies:
        copy.wait()
    rows = jnp.concatenate([dot(member_b, k_ref[...]), dot(member_b, v_ref[...]), count], axis=1)
    fine_ref[...] = rows[:COARSE, : 2 * WIDTH]
    for n in range(SIDE):
        wide_ref[n] = rows[COARSE:]


def exact_dot(a, b, dims=(((1,), (0,)), ((), ()))):
    return lax.dot_general(a, b, dims, precision=lax.Precision.HIGHEST, preferred_element_type=jnp.float32)


def unit_weights(core, w2_ref, rows, columns, by_row, by_column):
    shape = (rows, 2 * HEADS)
    head = lax.broadcasted_iota(jnp.int32, shape, 0) // by_row + core * HEADS
    pick = jnp.where(lax.broadcasted_iota(jnp.int32, shape, 1) == head, 1.0, 0.0)
    return exact_dot(exact_dot(pick, w2_ref[...]), unit_columns(columns, by_column))


def unit_columns(columns, by):
    unit = lax.broadcasted_iota(jnp.int32, (HIDDEN, columns), 0)
    column = lax.broadcasted_iota(jnp.int32, (HIDDEN, columns), 1)
    return jnp.where(column // by % HIDDEN == unit, 1.0, 0.0)


def bias_kernel(
    place_ref, w1_hbm, b1_hbm, w2_hbm, after_ref, bias_ref, phase_ref, line_ref, slot_ref, w1_ref, b1_ref, w2_ref, sems
):
    copies = fetch([(w1_hbm, w1_ref), (b1_hbm, b1_ref), (w2_hbm, w2_ref)], sems)
    ctx, core = place_ref[0], place_ref[1]
    col = lax.broadcasted_iota(jnp.int32, (1, KEYS), 1)
    level = (col - T) // COARSE
    pos = col.astype(jnp.float32)
    for k in range(LEVELS):
        run = 2**k * T // COARSE
        start = ((ctx >> k) ^ 1) * 2**k * T - ctx * T
        inside = (col - T - k * COARSE) * run
        here = (start + inside).astype(jnp.float32) + (run - 1) / 2.0
        pos = jnp.where((col >= T) & (level == k), here, pos)
    top = jnp.log1p(jnp.full((1, KEYS), LEVEL_TOKENS, jnp.float32))
    row = lax.broadcasted_iota(jnp.int32, (T, KEYS), 0).astype(jnp.float32)
    phase_ref[...] = jnp.log1p(jnp.abs(row - pos)) / top
    for copy in copies:
        copy.wait()
    lane = lax.broadcasted_iota(jnp.int32, (HEADS, D), 1) // HIDDEN
    w2 = unit_weights(core, w2_ref, HEADS, D, 1, 1)
    spread = unit_columns(HIDDEN * SUB, SUB)
    for n, ref in enumerate((w1_ref, b1_ref)):
        line = jnp.broadcast_to(ref[...], (D, HIDDEN))
        line_ref[n] = exact_dot(spread, line, (((0,), (1,)), ((), ())))
        slot_ref[n] = jnp.where(lane == core, exact_dot(ref[...], unit_columns(D, 1)), jnp.where(lane == 2 + n, w2, 0.0))
    weight = unit_weights(core, w2_ref, HEADS * SUB, HIDDEN * SUB, SUB, SUB)
    row = lax.broadcasted_iota(jnp.int32, weight.shape, 0)
    column = lax.broadcasted_iota(jnp.int32, weight.shape, 1)
    weight = jnp.where(row % SUB == column % SUB, weight, 0.0)
    weight_high = weight.astype(jnp.bfloat16)
    weight_low = (weight - weight_high.astype(jnp.float32)).astype(jnp.bfloat16)
    weight_both = jnp.concatenate([weight_high, weight_low], axis=0)

    def body(i, carry):
        rows = pl.ds(pl.multiple_of(i * SUB, SUB), SUB)
        hidden = jnp.maximum(by_units(line_ref, phase_ref[rows, :]), 0.0)
        high = hidden.astype(jnp.bfloat16)
        low = (hidden - high.astype(jnp.float32)).astype(jnp.bfloat16)
        with_high = dot(weight_both, high)
        bias = with_high[: HEADS * SUB] + with_high[HEADS * SUB :] + dot(weight_high, low)
        for h in range(HEADS):
            bias_ref[h, rows, :] = bias[h * SUB : (h + 1) * SUB]
        return carry

    lax.fori_loop(0, T // SUB, body, 0, unroll=UNROLL)


def by_units(line_ref, phase):
    slope = line_ref[0].reshape(HIDDEN, SUB, D)
    offset = line_ref[1].reshape(HIDDEN, SUB, D)
    tiles = [phase[None, :, n * D : (n + 1) * D] * slope + offset for n in range(KEYS // D)]
    return jnp.concatenate(tiles, axis=2).reshape(HIDDEN * SUB, KEYS)


def pooled(rows, by):
    row = lax.broadcasted_iota(jnp.int32, (rows.shape[0] // by, 1), 0)
    return picked(twice(rows.shape[0] // by, rows.shape[0]) // by == row, rows)


def middle_kernel(low_ref, after_bias_ref, after_merge_ref, own_ref, wide_ref):
    row = lax.broadcasted_iota(jnp.int32, (COARSE + CHUNK, 1), 0)
    col = twice(COARSE + CHUNK, SIDE * CHUNK)
    member = (col >> 3) ^ FIRST["low"]
    run = jnp.where(row < COARSE, (member << 1) + ((col & 7) >> 2), (member >> 1) + COARSE)
    rows = picked(run == row, low_ref[...])
    own_ref[...] = rows[:COARSE]
    for n in range(SIDE):
        wide_ref[n] = rows[COARSE:]


def gather_kernel(
    place_ref, len_ref, q_hbm, k_hbm, v_hbm, g_hbm, got0_ref, got1_ref, low_ref, got4_ref, high_ref, after_ref,
    q_ref, g_ref, keys_ref, values_ref, count_ref, k_ref, v_ref, sib_ref, sems,
):
    copies = fetch([(k_hbm, k_ref), (q_hbm, q_ref), (v_hbm, v_ref), (g_hbm, g_ref)], sems)
    ctx = place_ref[0]
    for level, ref in ((0, got0_ref), (1, got1_ref), (4, got4_ref), (5, got4_ref)):
        sib_ref[level * COARSE : (level + 1) * COARSE, : ref.shape[1]] = ref[...]
    row = lax.broadcasted_iota(jnp.int32, (2 * COARSE, 1), 0)
    col = twice(2 * COARSE, SIDE * CHUNK)
    for level, ref, first in ((2, low_ref, FIRST["low"]), (6, high_ref, FIRST["high"])):
        quarter = ((ctx >> level) & 3) ^ 1
        half = ((ctx >> level + 1) & 1) ^ 1
        member = col >> 3 if level == 2 else side_member(col >> 3)
        place = ((member ^ first) << 3) + (col & 7)
        want = jnp.where(row < COARSE, quarter * COARSE + row, (half - 1) * COARSE + row)
        rows = picked(jnp.where(row < COARSE, place, place >> 1) == want, ref[...])
        sib_ref[level * COARSE : (level + 2) * COARSE, :] = rows
    group = (((ctx >> 1) & 7) ^ 1) * 2
    blocks = ((0, COARSE, (ctx & 15) ^ 1), (COARSE, COARSE // 2, group), (COARSE * 3 // 2, COARSE // 2, group + 1))
    for first, rows, block in blocks:
        block = low_ref[pl.ds(pl.multiple_of((block ^ FIRST["low"]) * CHUNK, CHUNK), CHUNK), 2 * WIDTH :]
        run = T // rows
        before = lax.broadcasted_iota(jnp.int32, (rows, D), 0) * run
        here = jnp.sum(block, axis=0, keepdims=True) - before.astype(jnp.float32)
        sib_ref[first : first + rows, 2 * WIDTH :] = jnp.clip(here, 0.0, float(run))
    count = sib_ref[:, 2 * WIDTH :]
    count_ref[...] = count
    inverse = 1.0 / jnp.maximum(count, 1.0)
    for n in range(2 * KV):
        cols = slice(n * D, (n + 1) * D)
        ref = keys_ref if n < KV else values_ref
        ref[T:, n % KV * D : (n % KV + 1) * D] = (sib_ref[:, cols] * inverse).astype(jnp.bfloat16)
    for copy in copies:
        copy.wait()
    keys_ref[:T, :] = k_ref[...]
    values_ref[:T, :] = v_ref[...]
    row_live = lax.broadcasted_iota(jnp.int32, (T, 1), 0) < len_ref[0]
    g_ref[...] = jnp.where(row_live, g_ref[...], jnp.zeros_like(g_ref))


def with_level_5(rows, level, first):
    return jnp.concatenate([rows[: first + 5 * COARSE], level, rows[first + 6 * COARSE :]], axis=0)


def main_kernel(
    len_ref, q_ref, g_ref, keys_ref, values_ref, count_ref, got5_ref, bias_ref,
    out_ref, gq_ref, own_ref, coarse_ref, ds_ref,
):
    length = len_ref[0]
    count = with_level_5(count_ref[...], got5_ref[:, 2 * WIDTH :], 0)
    inverse = 1.0 / jnp.maximum(count, 1.0)
    count_t = jnp.concatenate([count[:T].T[:1], count[T:].T[:1]], axis=1)
    token_live = lax.broadcasted_iota(jnp.int32, (1, T), 1) < length
    live = jnp.concatenate([token_live.astype(jnp.float32), count_t], axis=1) > 0.0
    row_live = lax.broadcasted_iota(jnp.int32, (T, 1), 0) < length
    inverse_5 = inverse[5 * COARSE : 6 * COARSE]
    def stacked(ref):
        return jnp.concatenate([ref[:, h * D : (h + 1) * D] for h in range(HEADS)], axis=0)

    def per_group(*pairs, dims=(((1,), (0,)), ((), ()))):
        return jnp.concatenate([dot(a, b, dims) for a, b in pairs], axis=0)

    span = GROUP * T
    lanes = [slice(j * D, (j + 1) * D) for j in range(KV)]
    value_lanes = [slice((KV + j) * D, (KV + j + 1) * D) for j in range(KV)]
    keys = [with_level_5(keys_ref[:, at], (got5_ref[:, at] * inverse_5).astype(jnp.bfloat16), T) for at in lanes]
    values = [
        with_level_5(values_ref[:, at], (got5_ref[:, wide] * inverse_5).astype(jnp.bfloat16), T)
        for at, wide in zip(lanes, value_lanes)
    ]
    query, grad = stacked(q_ref), stacked(g_ref)
    groups = [slice(j * span, (j + 1) * span) for j in range(KV)]
    scores = per_group(*[(query[at], k) for at, k in zip(groups, keys)], dims=NT) * SCALE
    scores = jnp.where(live, scores + bias_ref[...].reshape(HEADS * T, KEYS), -jnp.inf)
    weights = jnp.exp(scores - jnp.max(scores, axis=1, keepdims=True))
    probs = weights * (1.0 / jnp.sum(weights, axis=1, keepdims=True))
    probs_b = probs.astype(jnp.bfloat16)
    attended = per_group(*[(probs_b[at], v) for at, v in zip(groups, values)])
    dprobs = per_group(*[(grad[at], v) for at, v in zip(groups, values)], dims=NT)
    dscores = probs * (dprobs - jnp.sum(probs * dprobs, axis=1, keepdims=True))
    ds_ref[...] = dscores.reshape(HEADS, T, KEYS)
    dscores_b = dscores.astype(jnp.bfloat16)
    grad_query = per_group(*[(dscores_b[at], k) for at, k in zip(groups, keys)]) * SCALE
    for h in range(HEADS):
        rows = slice(h * T, (h + 1) * T)
        out_ref[:, h * D : (h + 1) * D] = jnp.where(row_live, attended[rows], 0.0).astype(jnp.bfloat16)
        gq_ref[:, h * D : (h + 1) * D] = grad_query[rows].astype(jnp.bfloat16)
    for at, cols, vcols in zip(groups, lanes, value_lanes):
        key_grads = dot(dscores_b[at], query[at], TN) * SCALE
        value_grads = dot(probs_b[at], grad[at], TN)
        own_ref[:, cols] = key_grads[:T]
        own_ref[:, vcols] = value_grads[:T]
        coarse_ref[:, cols] = key_grads[T:] * inverse
        coarse_ref[:, vcols] = value_grads[T:] * inverse


def weight_kernel(
    place_ref, line_ref, slot_ref, ds_ref, phase_ref, out_ref, gq_ref, coarse_ref,
    w_ref, rows_ref, out_hbm, gq_hbm, acc_ref, sems,
):
    copies = fetch([(out_ref, out_hbm), (gq_ref, gq_hbm)], sems)
    acc_ref[...] = jnp.zeros_like(acc_ref)

    def operands(rows):
        phase = phase_ref[rows, :]
        parts = [ds_ref[h, rows, :] for h in range(HEADS)]
        parts = jnp.concatenate(parts + [p * phase for p in parts], axis=0)
        high = parts.astype(jnp.bfloat16)
        low = (parts - high.astype(jnp.float32)).astype(jnp.bfloat16)
        active = jnp.where(by_units(line_ref, phase) > 0.0, 1.0, 0.0).astype(jnp.bfloat16)
        return jnp.concatenate([high, low], axis=0), active

    def body(i, carry):
        first = pl.multiple_of(i * 2 * SUB, 2 * SUB)
        groups = [operands(pl.ds(first + n * SUB, SUB)) for n in range(2)]
        both, active = (jnp.concatenate(side, axis=1) for side in zip(*groups))
        acc_ref[...] += dot(both, active, NT)
        return carry

    lax.fori_loop(0, T // SUB // 2, body, 0, unroll=UNROLL)
    acc = acc_ref[...]
    rows = 2 * HEADS * SUB
    acc = acc[:rows] + acc[rows:]
    sub_row = lax.broadcasted_iota(jnp.int32, acc.shape, 0) % SUB
    sub_col = lax.broadcasted_iota(jnp.int32, acc.shape, 1) % SUB
    acc = jnp.where(sub_row == sub_col, acc, 0.0)
    acc = acc.reshape(2 * HEADS, SUB, HIDDEN * SUB).sum(axis=1)
    unit = lax.broadcasted_iota(jnp.int32, (HIDDEN * SUB, D), 0) // SUB
    lane = lax.broadcasted_iota(jnp.int32, (HIDDEN * SUB, D), 1) % HIDDEN
    sums = exact_dot(acc, jnp.where(unit == lane, 1.0, 0.0))
    rows_ref[...] = chosen(SIDE * CHUNK, level_parts(place_ref[0], 6, coarse_ref))
    w_ref[...] = slot_ref[1] * sums[:HEADS] + slot_ref[0] * sums[HEADS:]
    for copy in copies:
        copy.wait()


def chosen(rows, parts):
    sizes = [value.shape[0] for value, _ in parts]
    depth = -(-sum(sizes) // 16) * 16
    row = lax.broadcasted_iota(jnp.int32, (rows, 1), 0)
    col = twice(rows, depth)
    pick, first = col < 0, 0
    for size, (_, name) in zip(sizes, parts):
        pick = pick | (col == name(row, first))
        first += size
    value = [value for value, _ in parts]
    if first < depth:
        value.append(jnp.zeros((depth - first, value[0].shape[1]), jnp.float32))
    return picked(pick, jnp.concatenate(value, axis=0))


def twice(rows, depth):
    col = lax.broadcasted_iota(jnp.int32, (rows, 2 * depth), 1)
    return jnp.where(col < depth, col, col - depth)


def picked(pick, value):
    high = value.astype(jnp.bfloat16)
    low = (value - high.astype(jnp.float32)).astype(jnp.bfloat16)
    return dot(jnp.where(pick, 1.0, 0.0).astype(jnp.bfloat16), jnp.concatenate([high, low], axis=0))


def level_parts(ctx, level, coarse_ref):
    quarter = (ctx >> level) & 3

    def near(i, first):
        return jnp.where(i >> 5 == quarter ^ 1, (i & 31) + first, -1)

    def far(i, first):
        return jnp.where(i >> 6 != quarter >> 1, ((i & 63) >> 1) + first, -1)

    return [
        (coarse_ref[level * COARSE : (level + 1) * COARSE, :], near),
        (coarse_ref[(level + 1) * COARSE : (level + 2) * COARSE, :], far),
    ]


def half_of(ctx, level, shift):
    return lambda i, first: first + ((ctx >> level) & 1) * (COARSE // 2) + (i >> shift)


def every(shift):
    return lambda i, first: first + (i >> shift)


def sibling_rows(ctx, level, coarse_ref, came_ref):
    return chosen(
        COARSE,
        [
            (coarse_ref[level * COARSE : (level + 1) * COARSE, :], every(0)),
            (came_ref[...], half_of(ctx ^ (1 << level), level, 1)),
        ],
    )


def side_place(member):
    return (member >> 1) | ((member & 1) << 3)


def side_member(place):
    return ((place & 7) << 1) | (place >> 3)


def fill(payload_ref, place_of, rows, weights):
    for n in range(SIDE):
        payload_ref[place_of(n), :, : 2 * WIDTH] = rows[n * CHUNK : (n + 1) * CHUNK]
        payload_ref[place_of(n), :, 2 * WIDTH :] = weights


def away_kernel(place_ref, w_ref, rows_ref, coarse_ref, came5_ref, away_ref, send_ref):
    ctx = place_ref[0]
    fill(away_ref, lambda n: side_place(n ^ FIRST["away"]), rows_ref[...], w_ref[...])
    send_ref[...] = sibling_rows(ctx, 4, coarse_ref, came5_ref)


def summed(ref):
    return sum(ref[n] + ref[n + SIDE // 2] for n in range(SIDE // 2))


def base_kernel(place_ref, away_ref, came5_ref, came1_ref, coarse_ref, base_ref, w_ref, send_ref):
    ctx = place_ref[0]
    away = summed(away_ref)
    parts = level_parts(ctx, 2, coarse_ref) + [(came5_ref[...], half_of(ctx, 4, 3))]
    base_ref[...] = chosen(SIDE * CHUNK, parts + [(away[:, : 2 * WIDTH], every(4))])
    w_ref[...] = away[:, 2 * WIDTH :]
    send_ref[...] = sibling_rows(ctx, 0, coarse_ref, came1_ref)


def return_kernel(place_ref, w_ref, came4_ref, base_ref, near_ref):
    ctx = place_ref[0]
    rows = base_ref[...] + chosen(SIDE * CHUNK, [(came4_ref[...], every(2))])
    fill(near_ref, lambda n: n ^ FIRST["near"] ^ (((ctx >> 4) & 1) * 8), rows, w_ref[...])


def own_kernel(place_ref, own_ref, came1_ref, came0_ref, out_ref):
    parts = [(came1_ref[...], half_of(place_ref[0], 0, 3)), (came0_ref[...], every(2))]
    out_ref[...] = own_ref[...] + chosen(T, parts)


def final_kernel(len_ref, near_ref, own_ref, gk_ref, gv_ref):
    near = sum(near_ref[n, :, : 2 * WIDTH] for n in range(SIDE))
    live = lax.broadcasted_iota(jnp.int32, (T, 1), 0) < len_ref[0]
    grad = jnp.where(live, own_ref[...] + chosen(T, [(near, every(4))]), 0.0)
    gk_ref[...] = grad[:, :WIDTH].astype(jnp.bfloat16)
    gv_ref[...] = grad[:, WIDTH:].astype(jnp.bfloat16)


def outputs_kernel(mine_ref, got_ref, w1_ref, b1_ref, w2_ref):
    total = mine_ref[...] + got_ref[...]
    for core in range(2):
        w2_ref[core * HEADS : (core + 1) * HEADS, :] = total[:, core * HIDDEN : (core + 1) * HIDDEN]
    sums = jnp.sum(total, axis=0, keepdims=True)
    w1_ref[...] = sums[:, 2 * HIDDEN : 3 * HIDDEN]
    b1_ref[...] = sums[:, 3 * HIDDEN :]


def merge_kernel(place_ref, own_ref, got_ref, out_ref):
    row = lax.broadcasted_iota(jnp.int32, (COARSE, 1), 0)
    col = twice(COARSE, 2 * COARSE)
    upper = (place_ref[0] >> 4) & 1
    pick = (row & 15 == (col & 31) >> 1) & (row >> 4 == (col >> 5) ^ upper)
    out_ref[...] = picked(pick, jnp.concatenate([own_ref[...], got_ref[...]], axis=0))


def merge(own, got, upper):
    first = jnp.where(upper, got, own)
    second = jnp.where(upper, own, got)
    return jnp.concatenate([first, second], 0).reshape(COARSE, 2, -1).sum(1)


def in_hbm(value):
    return pltpu.with_memory_space_constraint(value, pltpu.HBM)


def swap_groups(value, groups):
    return lax.all_to_all(value, "ctx", 0, 0, axis_index_groups=groups)


def shards(queries, keys, values, lengths, fire_w1, fire_b1, fire_w2, grad_out):
    f32, bf16 = jnp.float32, jnp.bfloat16
    shape = jax.ShapeDtypeStruct
    ctx = lax.axis_index("ctx")
    mp = lax.axis_index("mp")
    place = jnp.stack([ctx, mp])
    bit = [(ctx >> k) & 1 == 1 for k in range(LEVELS)]
    blocks = range(SIDE)
    def low_groups(first, odd=0):
        return [[high * SIDE + (low ^ first ^ (odd * (high % 2))) for low in blocks] for high in blocks]

    def high_groups(first):
        order = [side_member(place) ^ first for place in blocks]
        return [[high * SIDE + (low ^ (8 * (high % 2))) for high in order] for low in blocks]

    payload = shape((SIDE, CHUNK, 2 * WIDTH + D), f32)
    sums = shape((COARSE, 2 * WIDTH + D), f32)
    rows = shape((COARSE, 2 * WIDTH), f32)
    dma = pltpu.SemaphoreType.DMA
    fine, wide = pl.pallas_call(
        leaf_kernel,
        out_shape=(rows, payload),
        in_specs=[SMEM, HBM, HBM],
        out_specs=(VMEM, VMEM),
        scratch_shapes=[pltpu.VMEM((T, WIDTH), bf16)] * 2 + [dma((2,))],
        compiler_params=SMALL,
        name="leaf",
    )(lengths, in_hbm(keys), in_hbm(values))
    low = swap_groups(wide, low_groups(FIRST["low"])).reshape(SIDE * CHUNK, -1)
    got0 = exchange(fine, 0)
    own1 = merge(fine, got0, bit[0])
    wide_tokens, tokens = shape((T, HEADS * D), bf16), shape((T, WIDTH), bf16)
    bias, phase, line, slot = pl.pallas_call(
        bias_kernel,
        out_shape=(
            shape((HEADS, T, KEYS), f32),
            shape((T, KEYS), f32),
            shape((2, HIDDEN * SUB, D), f32),
            shape((2, HEADS, D), f32),
        ),
        in_specs=[SMEM] + [HBM] * 3 + [ANY],
        out_specs=(VMEM,) * 4,
        scratch_shapes=[
            pltpu.VMEM((1, HIDDEN), f32),
            pltpu.VMEM((1, HIDDEN), f32),
            pltpu.VMEM((2 * HEADS, HIDDEN), f32),
            dma((3,)),
        ],
        compiler_params=SMALL,
        cost_estimate=pl.CostEstimate(flops=600_000_000, bytes_accessed=2_000_000, transcendentals=50_000),
        name="bias",
    )(place, *map(in_hbm, (fire_w1.reshape(1, -1), fire_b1.reshape(1, -1), fire_w2.T)), fine)
    own4, wide4 = pl.pallas_call(
        middle_kernel,
        out_shape=(sums, payload),
        in_specs=[VMEM, ANY, ANY],
        out_specs=(VMEM, VMEM),
        compiler_params=SMALL,
        name="middle",
    )(low, slot, own1)
    high = swap_groups(wide4, high_groups(FIRST["high"])).reshape(SIDE * CHUNK, -1)
    got4 = exchange(own4, 4)
    got1 = exchange(jnp.pad(own1, ((0, 0), (0, D))), 1)
    own5 = pl.pallas_call(
        merge_kernel,
        out_shape=sums,
        in_specs=[SMEM, VMEM, VMEM],
        out_specs=VMEM,
        compiler_params=SMALL,
        name="merge",
    )(place, own4, got4)
    got5 = exchange(own5, 5)

    both = shape((KEYS, WIDTH), bf16)
    gathered = pl.pallas_call(
        gather_kernel,
        out_shape=(wide_tokens, wide_tokens, both, both, shape((LEVELS * COARSE, D), f32)),
        in_specs=[SMEM, SMEM] + [HBM] * 4 + [VMEM] * 5 + [ANY],
        out_specs=(VMEM,) * 5,
        scratch_shapes=[pltpu.VMEM((T, WIDTH), bf16)] * 2
        + [pltpu.VMEM((LEVELS * COARSE, 2 * WIDTH + D), f32), dma((4,))],
        compiler_params=SMALL,
        cost_estimate=pl.CostEstimate(flops=300_000_000, bytes_accessed=2_000_000, transcendentals=0),
        name="gather",
    )(place, lengths, *map(in_hbm, (queries, keys, values, grad_out)), got0, got1, low, got4, high, own5)
    attended, grad_q, own_grad, coarse, dscores = pl.pallas_call(
        main_kernel,
        out_shape=(
            wide_tokens,
            wide_tokens,
            shape((T, 2 * WIDTH), f32),
            shape((LEVELS * COARSE, 2 * WIDTH), f32),
            shape((HEADS, T, KEYS), f32),
        ),
        in_specs=[SMEM] + [VMEM] * 7,
        out_specs=(VMEM,) * 5,
        compiler_params=LARGE,
        name="attention",
    )(lengths, *gathered, got5, bias)

    came5 = exchange(coarse[5 * COARSE : 6 * COARSE], 5)
    w_part, away_rows, attended, grad_q = pl.pallas_call(
        weight_kernel,
        out_shape=(shape((HEADS, D), f32), shape((T, 2 * WIDTH), f32), wide_tokens, wide_tokens),
        in_specs=[SMEM] + [VMEM] * 7,
        out_specs=(VMEM, VMEM, HBM, HBM),
        scratch_shapes=[pltpu.VMEM((4 * HEADS * SUB, HIDDEN * SUB), f32), dma((2,))],
        compiler_params=SMALL,
        cost_estimate=pl.CostEstimate(flops=900_000_000, bytes_accessed=2_000_000, transcendentals=0),
        name="weights",
    )(place, line, slot, dscores, phase, attended, grad_q, coarse)
    away, send4 = pl.pallas_call(
        away_kernel,
        out_shape=(payload, rows),
        in_specs=[SMEM] + [VMEM] * 4,
        out_specs=(VMEM, VMEM),
        compiler_params=SMALL,
        name="away",
    )(place, w_part, away_rows, coarse, came5)
    away = swap_groups(away, high_groups(FIRST["away"]))
    came4 = exchange(send4, 4)
    came1 = exchange(coarse[COARSE : 2 * COARSE], 1)
    base, w_away, send0 = pl.pallas_call(
        base_kernel,
        out_shape=(shape((T, 2 * WIDTH), f32), shape((HEADS, D), f32), rows),
        in_specs=[SMEM] + [VMEM] * 4,
        out_specs=(VMEM,) * 3,
        compiler_params=SMALL,
        cost_estimate=pl.CostEstimate(flops=300_000_000, bytes_accessed=1_000_000, transcendentals=0),
        name="base",
    )(place, away, came5, came1, coarse)
    near = pl.pallas_call(
        return_kernel,
        out_shape=payload,
        in_specs=[SMEM] + [VMEM] * 3,
        out_specs=VMEM,
        compiler_params=SMALL,
        name="return",
    )(place, w_away, came4, base)
    near = swap_groups(near, low_groups(FIRST["near"], 8))
    came0 = exchange(send0, 0)
    own_grad = pl.pallas_call(
        own_kernel,
        out_shape=shape((T, 2 * WIDTH), f32),
        in_specs=[SMEM] + [VMEM] * 3,
        out_specs=VMEM,
        compiler_params=SMALL,
        cost_estimate=pl.CostEstimate(flops=300_000_000, bytes_accessed=1_000_000, transcendentals=0),
        name="own",
    )(place, own_grad, came1, came0)
    near, own_grad = lax.optimization_barrier((near, own_grad))
    w_all = near[:, :, 2 * WIDTH :]
    w_all = (w_all[: SIDE // 2] + w_all[SIDE // 2 :]).sum(0)
    w_other = lax.ppermute(w_all, "mp", [(0, 1), (1, 0)])
    grad_k, grad_v = pl.pallas_call(
        final_kernel,
        out_shape=(tokens, tokens),
        in_specs=[SMEM] + [VMEM] * 2,
        out_specs=(VMEM, VMEM),
        compiler_params=SMALL,
        name="final",
    )(lengths, near, own_grad)
    grad_w1, grad_b1, grad_w2 = pl.pallas_call(
        outputs_kernel,
        out_shape=(shape((1, HIDDEN), f32), shape((1, HIDDEN), f32), shape((2 * HEADS, HIDDEN), f32)),
        in_specs=[VMEM] * 2,
        out_specs=(VMEM,) * 3,
        compiler_params=SMALL,
        name="outputs",
    )(w_all, w_other)
    grad_w1, grad_b1, grad_w2 = grad_w1.reshape(-1), grad_b1.reshape(-1), grad_w2.T
    return (attended, grad_q, grad_k, grad_v, grad_w1, grad_b1, grad_w2)


def solution(mesh):
    split = P("ctx", "mp")
    return jax.shard_map(
        shards,
        mesh=mesh,
        in_specs=(split, split, split, P("ctx"), P(), P(), P(), split),
        out_specs=(split, split, split, split, P(), P(), P()),
        check_vma=False,
    )
```
